32 devices in a mesh: ctx: 8 (over z, y), fsdp: 4 (over x, core).
Axes of the slice: x: 2, y: 2, z: 4, core: 2. Of those that a mesh axis runs over, the one named last changes fastest.
Arguments:
- tokens: bfloat16 [4, 4096, 2048], P('fsdp', 'ctx'), may hold values from -6 to 6
- cotangent: bfloat16 [4, 4096, 2048], P('fsdp', 'ctx'), may hold values from -6 to 6
- cont_lengths: int32 [4, 3], P('fsdp'), may hold values from 1 to 1024, 2048 in all within a row
- routes: int32 [4, 4096, 8], P('fsdp', 'ctx'), may hold values from 0 to 15, all different within a row; in each aligned block of 512 rows (0 to 511, 512 to 1023, ..., all dimensions but the last counted through in order) at most 320 rows name the same one
- gates: float32 [4, 4096, 8], P('fsdp', 'ctx'), may hold values from 0.12 to 0.5
- attn_gain: bfloat16 [2048], P(('ctx', 'fsdp')), may hold values from 0.5 to 1.5
- query_gain: bfloat16 [2048], P(('ctx', 'fsdp')), may hold values from 0.5 to 1.5
- key_gain: bfloat16 [2048], P(('ctx', 'fsdp')), may hold values from 0.5 to 1.5
- ffn_gain: bfloat16 [2048], P(('ctx', 'fsdp')), may hold values from 0.5 to 1.5
- w_query: bfloat16 [2048, 2048], P(('ctx', 'fsdp')), may hold values from -0.125 to 0.125
- w_key: bfloat16 [2048, 2048], P(('ctx', 'fsdp')), may hold values from -0.125 to 0.125
- w_value: bfloat16 [2048, 2048], P(('ctx', 'fsdp')), may hold values from -0.125 to 0.125
- w_out: bfloat16 [2048, 2048], P(('ctx', 'fsdp')), may hold values from -1 to 1
- w_gate: bfloat16 [16, 2048, 1024], P('ctx', 'fsdp'), may hold values from -0.125 to 0.125
- w_up: bfloat16 [16, 2048, 1024], P('ctx', 'fsdp'), may hold values from -0.125 to 0.125
- w_down: bfloat16 [16, 1024, 2048], P('ctx', 'fsdp'), may hold values from -0.5 to 0.5
Outputs:
- output: float32 [4, 4096, 2048], P('fsdp', 'ctx')
- input_grad: float32 [4, 4096, 2048], P('fsdp', 'ctx')
- attn_gain_grad: float32 [2048], P(('ctx', 'fsdp'))
- query_gain_grad: float32 [2048], P(('ctx', 'fsdp'))
- key_gain_grad: float32 [2048], P(('ctx', 'fsdp'))
- ffn_gain_grad: float32 [2048], P(('ctx', 'fsdp'))
- w_query_grad: float32 [2048, 2048], P(('ctx', 'fsdp'))
- w_key_grad: float32 [2048, 2048], P(('ctx', 'fsdp'))
- w_value_grad: float32 [2048, 2048], P(('ctx', 'fsdp'))
- w_out_grad: float32 [2048, 2048], P(('ctx', 'fsdp'))
- w_gate_grad: float32 [16, 2048, 1024], P('ctx', 'fsdp')
- w_up_grad: float32 [16, 2048, 1024], P('ctx', 'fsdp')
- w_down_grad: float32 [16, 1024, 2048], P('ctx', 'fsdp')
The draws below stay inside these ranges and needn't reach their ends.
Inputs may be any that keep to these rules, and one draw needn't show every extreme that they name: In each aligned block of 512 rows (the rows of one device) no expert is named by more than 320 routes, a bound that some block reaches; a token names 8 different experts. `cont_lengths`: the lengths of a group sum to 2048 and the largest is exactly 1024.
All inputs are finite; a program needn't handle non-finite values.
Results may differ from the reference program's by a relative error of at most 0.03.
Values may be sent and summed in bfloat16 or wider, within the bound.
No kernel may reach another device: no remote copies, remote signals or barrier semaphores. Data moves between devices by JAX's collectives and lax.ppermute only.
A program may use at most 512 MiB of HBM per device.

```python
import math
import jax
import jax.numpy as jnp
import numpy as np
from jax import lax

D = 2048
HEADS = 16
HEAD = 128
FF = 1024
TOP = 8
NCONT = 3
EXPERTS = 16
GROUP_TOK = 4096
TOK_DEV = 512
BATCH = 4
PROMPT = 2048
CONT_TOK = 2048
LONGEST = 1024
CAP = 320
N_CTX = 8


def levels(rng, extent, shards, least, top_value):
    def one(dim, shards_of):
        heights = jax.random.uniform(jax.random.fold_in(jax.random.fold_in(rng, 6), dim), (shards_of,), jnp.float32, least / len(shards), top_value / len(shards))
        return jnp.repeat(jnp.exp(heights), extent[dim] // shards_of).reshape((-1,) + (1,) * (len(extent) - dim - 1))

    factor_of = one(*shards[0])
    for cut in shards[1:]:
        factor_of = factor_of * one(*cut)
    return factor_of


def split_up(number_of, total, bound, lean):
    loads = [(1 << 20) // math.isqrt(standing ** lean) + 1 for standing in range(2, number_of + 1)]
    spare, counts = total - bound - (number_of - 1), [1] * (number_of - 1)
    while spare > 0:
        movable = [i for i in range(number_of - 1) if counts[i] < bound]
        pool, left = sum([loads[i] for i in movable]), spare
        for i in movable:
            addition = min(bound - counts[i], max(1, left * loads[i] // pool), spare)
            counts[i] = counts[i] + addition
            spare = spare - addition
    return np.array([bound] + counts)


def ragged_sizes(rng, number_of, total, bound, slope):
    if number_of == 2:
        one = jax.random.randint(rng, (), max(1, total - bound), min(bound, total - 1) + 1)
        return jnp.stack([one, total - one])
    tallies = jnp.asarray(split_up(number_of, total, bound, slope), jnp.int32)
    twos = (number_of - 1) // 2
    giver, receiver = tallies[1:1 + 2 * twos:2], tallies[2:2 + 2 * twos:2]
    slack = jnp.minimum(giver - 1, bound - receiver)
    shifted = jax.random.randint(jax.random.fold_in(rng, 1), (twos,), 0, 1 << 20) % (slack + 1)
    tallies = tallies.at[1:1 + 2 * twos:2].set(giver - shifted).at[2:2 + 2 * twos:2].set(receiver + shifted)
    return tallies[jax.random.permutation(jax.random.fold_in(rng, 2), number_of)]


def assign_block(key, own, number, rows, count, top, limit, skew):
    sequence = jax.random.permutation(key, count)
    crowded, usual = portions_of(count, rows * top, limit, skew, True), portions_of(count, rows * top, limit, skew, False)
    places = jnp.arange(count)

    def named(tallies, offset_by):
        used = int((tallies > 0).sum())
        fixed = max(1, used // 4)
        moved = fixed + (places - fixed + offset_by * (used - fixed)) % max(1, count - fixed)
        return jnp.zeros((count,), jnp.int32).at[sequence[jnp.where(places < fixed, places, moved)]].set(jnp.asarray(tallies, jnp.int32))

    tallies = jnp.where(number % 4 == 0, named(crowded, number // 4), named(usual, number - number // 4 - 1))
    mixed = jax.random.permutation(jax.random.fold_in(own, 3), count)
    giver, receiver = mixed[0:count // 2 * 2:2], mixed[1:count // 2 * 2:2]
    margin = jnp.minimum(tallies[giver] - 1, limit - tallies[receiver]) // 2
    margin = jnp.where((giver == sequence[0]) | (receiver == sequence[0]) | (tallies[receiver] == 0), 0, jnp.maximum(margin, 0))
    moved = jax.random.randint(jax.random.fold_in(own, 4), (count // 2,), 0, 1 << 20) % (margin + 1)
    tallies = tallies.at[giver].add(-moved).at[receiver].add(moved)
    members = jnp.searchsorted(jnp.cumsum(tallies), jnp.arange(rows * top), side="right").astype(jnp.int32)
    listing = members.reshape(top, rows).T
    listing = listing[jax.random.permutation(jax.random.fold_in(own, 1), rows)]
    offset_by = jax.random.randint(jax.random.fold_in(own, 2), (rows, 1), 0, top)
    return jnp.take_along_axis(listing, (jnp.arange(top)[None, :] + offset_by) % top, axis=1)


def portions_of(count, total, most, lean, full):
    portions = [(1 << 20) // math.isqrt(rank ** lean) + 1 for rank in range(1, count + 1)]
    largest = most if full else min(most, max(-(-total // count), total * portions[0] // sum(portions)))
    least = 1 if total - largest >= count - 1 else 0
    given, spare = [largest] + [least] * (count - 1), total - largest - least * (count - 1)
    while spare > 0:
        free = [i for i in range(1, count) if given[i] < largest] or [i for i in range(1, count) if given[i] < most]
        mass, left = sum([portions[i] for i in free]), spare
        for i in free:
            addition = min(most - given[i], max(1, left * portions[i] // mass), spare)
            given[i] = given[i] + addition
            spare = spare - addition
    return np.array(given)


def scatter_about(rng, shape, deviation, limit, cuts=(), kind=jnp.bfloat16):
    values = deviation * jax.random.normal(rng, shape, jnp.float32)
    if cuts:
        values = values * levels(rng, shape, cuts, -0.22, 0.18)
    return jnp.clip(values, -limit, limit).astype(kind)


def setup_inputs(seed: int = 0) -> dict:
    arg_keys = jax.random.split(jax.random.key(seed), 17)
    tokens = scatter_about(arg_keys[0], (BATCH, GROUP_TOK, D), 1.0, 6.0, ((0, 4), (1, 8)))
    cotangent = scatter_about(arg_keys[1], (BATCH, GROUP_TOK, D), 1.0, 6.0, ((0, 4), (1, 8)))
    cont_lengths = jax.vmap(lambda own: ragged_sizes(own, NCONT, CONT_TOK, LONGEST, 2))(jax.random.split(arg_keys[2], BATCH)).reshape((BATCH, NCONT)).astype(jnp.int32)
    routes_keys = jax.random.split(jax.random.fold_in(arg_keys[3], 1), BATCH * GROUP_TOK // TOK_DEV)
    routes_turns = jax.random.permutation(jax.random.fold_in(arg_keys[3], 3), BATCH * GROUP_TOK // TOK_DEV)
    routes = jax.vmap(lambda own, number: assign_block(jax.random.fold_in(arg_keys[3], 2), own, number, TOK_DEV, EXPERTS, TOP, CAP, 1))(routes_keys, routes_turns).reshape((BATCH, GROUP_TOK, TOP))
    gates = jnp.clip(jnp.exp(math.log(0.5) - 1.4271164 * jax.random.uniform(arg_keys[4], (BATCH, GROUP_TOK, TOP), jnp.float32) ** levels(arg_keys[4], (BATCH, GROUP_TOK, TOP), ((0, 4), (1, 8)), -0.2, 0.2)), 0.12, 0.5)
    attn_gain = jnp.clip(1.0 + 0.1 * jax.random.normal(arg_keys[5], (D,), jnp.float32), 0.5, 1.5).astype(jnp.bfloat16)
    query_gain = jnp.clip(1.0 + 0.1 * jax.random.normal(arg_keys[6], (D,), jnp.float32), 0.5, 1.5).astype(jnp.bfloat16)
    key_gain = jnp.clip(1.0 + 0.1 * jax.random.normal(arg_keys[7], (D,), jnp.float32), 0.5, 1.5).astype(jnp.bfloat16)
    ffn_gain = jnp.clip(1.0 + 0.1 * jax.random.normal(arg_keys[8], (D,), jnp.float32), 0.5, 1.5).astype(jnp.bfloat16)
    w_query = scatter_about(arg_keys[9], (D, D), D ** -0.5, 0.125, ((0, 32),))
    w_key = scatter_about(arg_keys[10], (D, D), D ** -0.5, 0.125, ((0, 32),))
    w_value = scatter_about(arg_keys[11], (D, D), D ** -0.5, 0.125, ((0, 32),))
    w_out = scatter_about(arg_keys[12], (D, D), (D // 64) ** -0.5, 1.0, ((0, 32),))
    w_gate = scatter_about(arg_keys[13], (EXPERTS, D, FF), D ** -0.5, 0.125, ((0, 8), (1, 4)))
    w_up = scatter_about(arg_keys[14], (EXPERTS, D, FF), D ** -0.5, 0.125, ((0, 8), (1, 4)))
    w_down = scatter_about(arg_keys[15], (EXPERTS, FF, D), (FF // 8) ** -0.5, 0.5, ((0, 8), (1, 4)))
    return dict(tokens=tokens, cotangent=cotangent, cont_lengths=cont_lengths, routes=routes, gates=gates, attn_gain=attn_gain, query_gain=query_gain, key_gain=key_gain, ffn_gain=ffn_gain, w_query=w_query, w_key=w_key, w_value=w_value, w_out=w_out, w_gate=w_gate, w_up=w_up, w_down=w_down)


@jax.custom_vjp
def low(v):
    return lax.optimization_barrier(v.astype(jnp.bfloat16)).astype(jnp.float32)

@jax.custom_vjp
def low_back(v):
    return v

def low_keep(v):
    return (low(v), None)

def low_pass(kept, grad):
    return (grad,)

def back_keep(v):
    return (v, None)

def back_low(kept, grad):
    return (low(grad),)
low.defvjp(low_keep, low_pass)
low_back.defvjp(back_keep, back_low)
EPSILON = 1e-05
ROPE_BASE = 10000.0
MASKED = -1e+30
PRECISE = lax.Precision.HIGHEST

def norm_rows(values_in, gain_in):
    return values_in * lax.rsqrt(lax.optimization_barrier(jnp.mean(values_in * values_in, axis=-1, keepdims=True)) + EPSILON) * gain_in

def places(token_index, lengths_in, prompt_rows):
    ends = prompt_rows + jnp.cumsum(lengths_in).astype(jnp.int32)
    passed = (token_index[:, None] >= ends[None, :]).astype(jnp.int32)
    before = lax.optimization_barrier(jnp.sum(passed * lengths_in[None, :], axis=1)).astype(jnp.int32)
    inside = token_index >= prompt_rows
    segment = jnp.where(inside, 1 + lax.optimization_barrier(jnp.sum(passed, axis=1)).astype(jnp.int32), 0).astype(jnp.int32)
    position = jnp.where(inside, token_index - before, token_index).astype(jnp.int32)
    return (segment, position)

def rotate(values_in, positions):
    full_shape = values_in.shape
    per_head = values_in.reshape(full_shape[:-1] + (full_shape[-1] // HEAD, HEAD))
    half_dim = HEAD // 2
    frequency = ROPE_BASE ** (-jnp.arange(half_dim).astype(values_in.dtype) / half_dim)
    angles = positions.astype(values_in.dtype)[..., None] * frequency
    cosine = jnp.cos(angles)[..., None, :]
    sine = jnp.sin(angles)[..., None, :]
    former = per_head[..., :half_dim]
    latter = per_head[..., half_dim:]
    turned = jnp.concatenate([former * cosine - latter * sine, latter * cosine + former * sine], axis=-1)
    return turned.reshape(full_shape)

def attend_group(group_args):
    query, keys_in, values_in, segment = group_args
    token_index = jnp.arange(GROUP_TOK, dtype=jnp.int32)
    query_block = min(1024, GROUP_TOK)
    key_heads = keys_in.reshape(GROUP_TOK, HEADS, HEAD)
    value_heads = values_in.reshape(GROUP_TOK, HEADS, HEAD)
    score_scale = HEAD ** (-0.5)

    def one_block(block_args):
        query_rows, query_index, query_seg = block_args
        query_heads = query_rows.reshape(query_block, HEADS, HEAD)
        scores = jnp.einsum('qhd,khd->hqk', query_heads, key_heads, precision=PRECISE) * score_scale
        scores = low_back(scores)
        allowed = (token_index[None, :] <= query_index[:, None]) & ((segment[None, :] == 0) | (segment[None, :] == query_seg[:, None]))
        masked = jnp.where(allowed[None], scores, MASKED)
        highest = lax.optimization_barrier(jnp.max(masked, axis=-1, keepdims=True))
        unnormed = jnp.where(allowed[None], jnp.exp(masked - highest), 0.0)
        denominator = lax.optimization_barrier(jnp.sum(unnormed, axis=-1, keepdims=True))
        outcome = jnp.einsum('hqk,khd->hqd', low(unnormed), value_heads, precision=PRECISE) / denominator
        return jnp.transpose(outcome, (1, 0, 2)).reshape(query_block, HEADS * HEAD)
    pieces = lax.map(jax.checkpoint(one_block), (query.reshape(-1, query_block, D), token_index.reshape(-1, query_block), segment.reshape(-1, query_block)))
    return pieces.reshape(GROUP_TOK, D)

def expert_table(routes):
    block_total = BATCH * N_CTX
    blocks = routes.reshape(block_total, TOK_DEV * TOP)
    onehot = (blocks[:, :, None] == jnp.arange(EXPERTS, dtype=jnp.int32)[None, None, :]).astype(jnp.int32)
    slot_rank = lax.optimization_barrier(jnp.sum((jnp.cumsum(onehot, axis=1).astype(jnp.int32) - 1) * onehot, axis=2)).astype(jnp.int32)
    block_ids = jnp.arange(block_total, dtype=jnp.int32)[:, None]
    slot_place = (block_ids * CAP + slot_rank).reshape(-1)
    route_ids = jnp.arange(BATCH * GROUP_TOK * TOP, dtype=jnp.int32)
    table = jnp.full((EXPERTS, block_total * CAP), -1, jnp.int32)
    return table.at[blocks.reshape(-1), slot_place].set(route_ids)

def reference(tokens, cotangent, cont_lengths, routes, gates, attn_gain, query_gain, key_gain, ffn_gain, w_query, w_key, w_value, w_out, w_gate, w_up, w_down):
    token_index = jnp.arange(GROUP_TOK, dtype=jnp.int32)
    segment, position = jax.vmap(lambda lengths_row: places(token_index, lengths_row, PROMPT))(cont_lengths)
    table = expert_table(routes)
    gate_flat = gates.reshape(-1).astype(jnp.float32)

    def layer(params):
        inputs, gain_attn, gain_query, gain_key, gain_ffn, query_w, key_w, value_w, out_w, gate_w, up_w, down_w = params
        hidden = low(norm_rows(inputs, gain_attn))
        query_pre = low_back(jnp.einsum('btd,de->bte', hidden, query_w, precision=PRECISE))
        key_pre = low_back(jnp.einsum('btd,de->bte', hidden, key_w, precision=PRECISE))
        value_low = low_back(low(jnp.einsum('btd,de->bte', hidden, value_w, precision=PRECISE)))
        query_low = low(rotate(norm_rows(query_pre, gain_query), position))
        key_low = low(rotate(norm_rows(key_pre, gain_key), position))
        attended = lax.map(attend_group, (query_low, key_low, value_low, segment))
        attended = low_back(low(attended))
        mixed = inputs + low_back(jnp.einsum('btd,de->bte', attended, out_w, precision=PRECISE))
        second = low(norm_rows(mixed, gain_ffn))
        flat_second = second.reshape(-1, D)

        def one_expert(summed, expert_args):
            gate_m, up_m, down_m, route_ids = expert_args
            is_valid = route_ids >= 0
            safe_ids = jnp.where(is_valid, route_ids, 0)
            token_ids = safe_ids // TOP
            arriving = low_back(flat_second[token_ids])
            gate_pre = low_back(jnp.dot(arriving, gate_m, precision=PRECISE))
            up_pre = low_back(jnp.dot(arriving, up_m, precision=PRECISE))
            active = low(jax.nn.silu(gate_pre) * up_pre)
            produced = low_back(low(jnp.dot(active, down_m, precision=PRECISE)))
            weight_col = jnp.where(is_valid, gate_flat[safe_ids], 0.0)
            return (summed.at[token_ids].add(weight_col[:, None] * produced), None)
        routed, _ = lax.scan(jax.checkpoint(one_expert), jnp.zeros(flat_second.shape, jnp.float32), (gate_w, up_w, down_w, table))
        return mixed + routed.reshape(mixed.shape)
    primals = tuple((item.astype(jnp.float32) for item in (tokens, attn_gain, query_gain, key_gain, ffn_gain, w_query, w_key, w_value, w_out, w_gate, w_up, w_down)))
    result, pullback = jax.vjp(layer, primals)
    grads = pullback(cotangent.astype(jnp.float32))[0]
    return (result, grads[0], grads[1], grads[2], grads[3], grads[4], grads[5], grads[6], grads[7], grads[8], grads[9], grads[10], grads[11])
```

```python
from functools import partial

import jax
import jax.numpy as jnp
from jax import lax
from jax.experimental import pallas as pl
from jax.experimental.pallas import tpu as pltpu
from jax.sharding import PartitionSpec as P

HEAD = 128


EPSILON = 1e-05
ROPE_BASE = 10000.0
MASKED = -1e30


def norm_rows(values_in, gain_in):
    return (
        values_in
        * lax.rsqrt(jnp.mean(values_in * values_in, axis=-1, keepdims=True) + EPSILON)
        * gain_in
    )


def places(token_index, lengths_in, prompt_rows):
    ends = prompt_rows + jnp.cumsum(lengths_in)
    passed = (token_index[:, None] >= ends[None, :]).astype(jnp.int32)
    before = jnp.sum(passed * lengths_in[None, :], axis=1)
    inside = token_index >= prompt_rows
    segment = jnp.where(inside, 1 + jnp.sum(passed, axis=1), 0)
    position = jnp.where(inside, token_index - before, token_index)
    return (segment, position)


def rotate(values_in, positions):
    full_shape = values_in.shape
    per_head = values_in.reshape(full_shape[:-1] + (full_shape[-1] // HEAD, HEAD))
    half_dim = HEAD // 2
    frequency = ROPE_BASE ** (-jnp.arange(half_dim).astype(values_in.dtype) / half_dim)
    angles = positions.astype(values_in.dtype)[..., None] * frequency
    cosine = jnp.cos(angles)[..., None, :]
    sine = jnp.sin(angles)[..., None, :]
    former = per_head[..., :half_dim]
    latter = per_head[..., half_dim:]
    turned = jnp.concatenate(
        [former * cosine - latter * sine, latter * cosine + former * sine], axis=-1
    )
    return turned.reshape(full_shape)


def allowed_pairs(query_index, query_seg, key_index, key_seg):
    return (key_index[None, :] <= query_index[:, None]) & (
        (key_seg[None, :] == 0) | (key_seg[None, :] == query_seg[:, None])
    )


def attend_fold(
    state_in,
    shard_piece,
    first_row,
    query_heads,
    own_index,
    own_seg,
    lengths_in,
    prompt_rows,
    score_scale,
):
    highest, denominator, weighted = state_in
    key_rows, value_rows = shard_piece
    piece_count = key_rows.shape[0]
    key_index = jnp.arange(piece_count, dtype=jnp.int32)
    key_seg, _ = places(key_index, lengths_in, prompt_rows)
    key_heads = key_rows.reshape(piece_count, -1, HEAD)
    value_heads = value_rows.reshape(piece_count, -1, HEAD)
    scores = (
        jnp.einsum("qhd,khd->hqk", query_heads, key_heads, preferred_element_type=jnp.float32)
        * score_scale
    )
    allowed = allowed_pairs(own_index, own_seg, key_index, key_seg)
    masked = jnp.where(allowed[None], scores, MASKED)
    new_high = jnp.maximum(highest, jnp.max(masked, axis=-1))
    shrink = jnp.exp(highest - new_high)
    unnormed = jnp.where(allowed[None], jnp.exp(masked - new_high[..., None]), 0.0)
    denominator = jnp.sum(unnormed, axis=-1)
    weighted = jnp.einsum(
        "hqk,khd->hqd",
        unnormed.astype(jnp.bfloat16),
        value_heads,
        preferred_element_type=jnp.float32,
    )
    return (new_high, denominator, weighted)


def pair_terms(
    query_heads,
    grad_heads,
    log_rows,
    dot_rows,
    query_index,
    query_seg,
    key_heads,
    value_heads,
    key_index,
    key_seg,
    score_scale,
):
    scores = (
        jnp.einsum("qhd,khd->hqk", query_heads, key_heads, preferred_element_type=jnp.float32)
        * score_scale
    )
    allowed = allowed_pairs(query_index, query_seg, key_index, key_seg)
    prob = jnp.where(
        allowed[None], jnp.exp(jnp.where(allowed[None], scores, MASKED) - log_rows[..., None]), 0.0
    )
    prob_grad = jnp.einsum(
        "qhd,khd->hqk", grad_heads, value_heads, preferred_element_type=jnp.float32
    )
    score_grad = (prob * (prob_grad - dot_rows[..., None])).astype(jnp.bfloat16)
    return (prob, score_grad)


def slot_targets(route_list, expert_total, capacity):
    onehot = (route_list[:, None] == jnp.arange(expert_total, dtype=jnp.int32)[None, :]).astype(
        jnp.int32
    )
    slot_rank = jnp.sum((jnp.cumsum(onehot, axis=0) - 1) * onehot, axis=1)
    return route_list * capacity + slot_rank


def shards_wide(
    tokens,
    cotangent,
    cont_lengths,
    routes,
    gates,
    attn_gain,
    query_gain,
    key_gain,
    ffn_gain,
    w_query,
    w_key,
    w_value,
    w_out,
    w_gate,
    w_up,
    w_down,
):
    row_count = tokens.shape[1]
    model_width = tokens.shape[2]
    route_count = routes.shape[2]
    context_size = lax.axis_size("ctx")
    all_rows = row_count * context_size
    prompt_rows = all_rows // 2
    local_experts = w_gate.shape[0]
    expert_total = local_experts * context_size
    capacity = max(2, row_count * route_count * 5 // (4 * expert_total))
    head_count = model_width // HEAD
    score_scale = HEAD ** (-0.5)
    lengths_in = cont_lengths[0]
    own_index = lax.axis_index("ctx") * row_count + jnp.arange(row_count, dtype=jnp.int32)
    own_seg, own_pos = places(own_index, lengths_in, prompt_rows)
    attention_set = (
        lax.all_gather(w_query, ("ctx", "fsdp"), axis=0, tiled=True),
        lax.all_gather(w_key, ("ctx", "fsdp"), axis=0, tiled=True),
        lax.all_gather(w_value, ("ctx", "fsdp"), axis=0, tiled=True),
        lax.all_gather(w_out, ("ctx", "fsdp"), axis=0, tiled=True),
        lax.all_gather(attn_gain, ("ctx", "fsdp"), axis=0, tiled=True),
        lax.all_gather(query_gain, ("ctx", "fsdp"), axis=0, tiled=True),
        lax.all_gather(key_gain, ("ctx", "fsdp"), axis=0, tiled=True),
        lax.all_gather(ffn_gain, ("ctx", "fsdp"), axis=0, tiled=True),
    )
    query_all, key_all, value_all, out_all = (
        attention_set[0],
        attention_set[1],
        attention_set[2],
        attention_set[3],
    )
    gain_attn = attention_set[4].astype(jnp.float32)
    gain_query = attention_set[5].astype(jnp.float32)
    gain_key = attention_set[6].astype(jnp.float32)
    gain_ffn = attention_set[7].astype(jnp.float32)
    expert_set = (
        lax.all_gather(w_gate, "fsdp", axis=1, tiled=True),
        lax.all_gather(w_up, "fsdp", axis=1, tiled=True),
        lax.all_gather(w_down, "fsdp", axis=1, tiled=True),
    )
    gate_all, up_all, down_all = expert_set
    inputs = tokens[0].astype(jnp.float32)
    normed, attn_pull = jax.vjp(norm_rows, inputs, gain_attn)
    hidden = normed.astype(jnp.bfloat16)
    query_pre = jnp.dot(hidden, query_all, preferred_element_type=jnp.float32)
    key_pre = jnp.dot(hidden, key_all, preferred_element_type=jnp.float32)
    values = jnp.dot(hidden, value_all, preferred_element_type=jnp.float32).astype(jnp.bfloat16)
    query_rot, query_pull = jax.vjp(
        lambda pre_in, gain_in: rotate(norm_rows(pre_in, gain_in), own_pos), query_pre, gain_query
    )
    key_rot, key_pull = jax.vjp(
        lambda pre_in, gain_in: rotate(norm_rows(pre_in, gain_in), own_pos), key_pre, gain_key
    )
    query_low = query_rot.astype(jnp.bfloat16)
    key_low = key_rot.astype(jnp.bfloat16)
    query_heads = query_low.reshape(row_count, head_count, HEAD)
    folder = partial(
        attend_fold,
        query_heads=query_heads,
        own_index=own_index,
        own_seg=own_seg,
        lengths_in=lengths_in,
        prompt_rows=prompt_rows,
        score_scale=score_scale,
    )
    start_state = (
        jnp.full((head_count, row_count), MASKED, jnp.float32),
        jnp.zeros((head_count, row_count), jnp.float32),
        jnp.zeros((head_count, row_count, HEAD), jnp.float32),
    )
    final_state = folder(
        start_state,
        (
            lax.all_gather(key_low, "ctx", axis=0, tiled=True),
            lax.all_gather(values, "ctx", axis=0, tiled=True),
        ),
        jnp.int32(0),
    )
    highest, denominator, weighted = final_state
    log_total = highest + jnp.log(denominator)
    attn_heads = jnp.transpose(weighted / denominator[..., None], (1, 0, 2))
    attended = attn_heads.reshape(row_count, model_width).astype(jnp.bfloat16)
    mixed = inputs + jnp.dot(attended, out_all, preferred_element_type=jnp.float32)
    normed_second, ffn_pull = jax.vjp(norm_rows, mixed, gain_ffn)
    second = normed_second.astype(jnp.bfloat16)
    route_list = routes[0].reshape(-1)
    targets = slot_targets(route_list, expert_total, capacity)

    def dispatch_rows(route_rows):
        buffer = (
            jnp.zeros((expert_total * capacity, model_width), jnp.bfloat16)
            .at[targets]
            .set(route_rows)
        )
        return buffer.reshape(context_size, local_experts * capacity, model_width)

    sent_rows = dispatch_rows(jnp.repeat(second, route_count, axis=0))
    arrived = lax.all_to_all(sent_rows, "ctx", split_axis=0, concat_axis=0, tiled=True).reshape(
        context_size, local_experts, capacity, model_width
    )
    gate_pre = jnp.einsum("sekd,edf->sekf", arrived, gate_all, preferred_element_type=jnp.float32)
    up_pre = jnp.einsum("sekd,edf->sekf", arrived, up_all, preferred_element_type=jnp.float32)
    active = (jax.nn.silu(gate_pre) * up_pre).astype(jnp.bfloat16)
    expert_out = jnp.einsum(
        "sekf,efd->sekd", active, down_all, preferred_element_type=jnp.float32
    ).astype(jnp.bfloat16)
    returned = lax.all_to_all(
        expert_out.reshape(context_size, local_experts * capacity, model_width),
        "ctx",
        split_axis=0,
        concat_axis=0,
        tiled=True,
    )
    per_route = (
        returned.reshape(expert_total * capacity, model_width)[targets]
        .astype(jnp.float32)
        .reshape(row_count, route_count, model_width)
    )
    gate_values = gates[0]
    result = mixed + jnp.sum(gate_values[..., None] * per_route, axis=1)
    output = result[None]
    upstream = cotangent[0].astype(jnp.float32)
    route_grad = (
        (gate_values[..., None] * upstream[:, None, :])
        .astype(jnp.bfloat16)
        .reshape(row_count * route_count, model_width)
    )
    grad_arrived = lax.all_to_all(
        dispatch_rows(route_grad), "ctx", split_axis=0, concat_axis=0, tiled=True
    ).reshape(context_size, local_experts, capacity, model_width)
    active_grad = jnp.einsum(
        "sekd,efd->sekf", grad_arrived, down_all, preferred_element_type=jnp.float32
    )
    down_w_grad = jnp.einsum(
        "sekf,sekd->efd", active, grad_arrived, preferred_element_type=jnp.float32
    )
    sigmoid_gate = jax.nn.sigmoid(gate_pre)
    gate_grad = (
        active_grad * up_pre * sigmoid_gate * (1.0 + gate_pre * (1.0 - sigmoid_gate))
    ).astype(jnp.bfloat16)
    up_grad = (active_grad * gate_pre * sigmoid_gate).astype(jnp.bfloat16)
    gate_w_grad = jnp.einsum(
        "sekd,sekf->edf", arrived, gate_grad, preferred_element_type=jnp.float32
    )
    up_w_grad = jnp.einsum("sekd,sekf->edf", arrived, up_grad, preferred_element_type=jnp.float32)
    arrived_grad = jnp.einsum(
        "sekf,edf->sekd", gate_grad, gate_all, preferred_element_type=jnp.float32
    )
    arrived_grad = (
        arrived_grad
        + jnp.einsum("sekf,edf->sekd", up_grad, up_all, preferred_element_type=jnp.float32)
    ).astype(jnp.bfloat16)
    grad_back = lax.all_to_all(
        arrived_grad.reshape(context_size, local_experts * capacity, model_width),
        "ctx",
        split_axis=0,
        concat_axis=0,
        tiled=True,
    )
    second_grad = jnp.sum(
        grad_back.reshape(expert_total * capacity, model_width)[targets]
        .astype(jnp.float32)
        .reshape(row_count, route_count, model_width),
        axis=1,
    )
    expert_grads = (
        lax.psum_scatter(
            gate_w_grad.astype(jnp.bfloat16), "fsdp", scatter_dimension=1, tiled=True
        ).astype(jnp.float32),
        lax.psum_scatter(
            up_w_grad.astype(jnp.bfloat16), "fsdp", scatter_dimension=1, tiled=True
        ).astype(jnp.float32),
        lax.psum_scatter(
            down_w_grad.astype(jnp.bfloat16), "fsdp", scatter_dimension=1, tiled=True
        ).astype(jnp.float32),
    )
    mixed_norm_grad, ffn_gain_grad = ffn_pull(second_grad)
    mixed_grad = upstream + mixed_norm_grad
    branch_grad = mixed_grad.astype(jnp.bfloat16)
    out_w_grad = jnp.dot(attended.T, branch_grad, preferred_element_type=jnp.float32)
    attended_grad = jnp.dot(branch_grad, out_all.T, preferred_element_type=jnp.float32).astype(
        jnp.bfloat16
    )
    grad_heads = attended_grad.reshape(row_count, head_count, HEAD)
    row_dot = jnp.transpose(jnp.sum(grad_heads.astype(jnp.float32) * attn_heads, axis=-1))
    keys_whole, values_whole = (
        lax.all_gather(key_low, "ctx", axis=0, tiled=True),
        lax.all_gather(values, "ctx", axis=0, tiled=True),
    )
    block_rows = min(1024, all_rows)
    block_count = all_rows // block_rows
    block_index = jnp.arange(all_rows, dtype=jnp.int32).reshape(block_count, block_rows)
    key_blocks = keys_whole.reshape(block_count, block_rows, model_width)
    value_blocks = values_whole.reshape(block_count, block_rows, model_width)

    def query_side(key_rows, value_rows, key_index):
        key_seg, _ = places(key_index, lengths_in, prompt_rows)
        key_heads = key_rows.reshape(block_rows, head_count, HEAD)
        value_heads = value_rows.reshape(block_rows, head_count, HEAD)
        prob, score_grad = pair_terms(
            query_heads,
            grad_heads,
            log_total,
            row_dot,
            own_index,
            own_seg,
            key_heads,
            value_heads,
            key_index,
            key_seg,
            score_scale,
        )
        query_term = (
            jnp.einsum("hqk,khd->qhd", score_grad, key_heads, preferred_element_type=jnp.float32)
            * score_scale
        )
        return (prob, score_grad, query_term)

    def back_block(query_grad, block_args):
        key_rows, value_rows, key_index = block_args
        prob, score_grad, query_term = query_side(key_rows, value_rows, key_index)
        key_term = (
            jnp.einsum("hqk,qhd->khd", score_grad, query_heads, preferred_element_type=jnp.float32)
            * score_scale
        )
        value_term = jnp.einsum(
            "hqk,qhd->khd",
            prob.astype(jnp.bfloat16),
            grad_heads,
            preferred_element_type=jnp.float32,
        )
        return (
            query_grad + query_term,
            (
                key_term.reshape(block_rows, model_width),
                value_term.reshape(block_rows, model_width),
            ),
        )

    query_grad, (key_terms, value_terms) = lax.scan(
        back_block,
        jnp.zeros((row_count, head_count, HEAD), jnp.float32),
        (key_blocks, value_blocks, block_index),
    )
    key_grad, value_grad = (
        lax.psum_scatter(
            key_terms.reshape(all_rows, model_width).astype(jnp.bfloat16),
            "ctx",
            scatter_dimension=0,
            tiled=True,
        ).astype(jnp.float32),
        lax.psum_scatter(
            value_terms.reshape(all_rows, model_width).astype(jnp.bfloat16),
            "ctx",
            scatter_dimension=0,
            tiled=True,
        ).astype(jnp.float32),
    )
    query_pre_grad, query_gain_grad = query_pull(query_grad.reshape(row_count, model_width))
    key_pre_grad, key_gain_grad = key_pull(key_grad)
    query_low_grad = query_pre_grad.astype(jnp.bfloat16)
    key_low_grad = key_pre_grad.astype(jnp.bfloat16)
    value_low_grad = value_grad.astype(jnp.bfloat16)
    query_w_grad = jnp.dot(hidden.T, query_low_grad, preferred_element_type=jnp.float32)
    key_w_grad = jnp.dot(hidden.T, key_low_grad, preferred_element_type=jnp.float32)
    value_w_grad = jnp.dot(hidden.T, value_low_grad, preferred_element_type=jnp.float32)
    hidden_grad = jnp.dot(query_low_grad, query_all.T, preferred_element_type=jnp.float32)
    hidden_grad = hidden_grad + jnp.dot(key_low_grad, key_all.T, preferred_element_type=jnp.float32)
    hidden_grad = hidden_grad + jnp.dot(
        value_low_grad, value_all.T, preferred_element_type=jnp.float32
    )
    input_norm_grad, attn_gain_grad = attn_pull(hidden_grad)
    input_grad = (mixed_grad + input_norm_grad)[None]
    summed_grads = (
        lax.psum_scatter(query_w_grad, ("ctx", "fsdp"), scatter_dimension=0, tiled=True),
        lax.psum_scatter(key_w_grad, ("ctx", "fsdp"), scatter_dimension=0, tiled=True),
        lax.psum_scatter(value_w_grad, ("ctx", "fsdp"), scatter_dimension=0, tiled=True),
        lax.psum_scatter(out_w_grad, ("ctx", "fsdp"), scatter_dimension=0, tiled=True),
        lax.psum_scatter(attn_gain_grad, ("ctx", "fsdp"), scatter_dimension=0, tiled=True),
        lax.psum_scatter(query_gain_grad, ("ctx", "fsdp"), scatter_dimension=0, tiled=True),
        lax.psum_scatter(key_gain_grad, ("ctx", "fsdp"), scatter_dimension=0, tiled=True),
        lax.psum_scatter(ffn_gain_grad, ("ctx", "fsdp"), scatter_dimension=0, tiled=True),
    )
    return (
        output,
        input_grad,
        summed_grads[4],
        summed_grads[5],
        summed_grads[6],
        summed_grads[7],
        summed_grads[0],
        summed_grads[1],
        summed_grads[2],
        summed_grads[3],
        expert_grads[0],
        expert_grads[1],
        expert_grads[2],
    )


HEADS = 16
LOG2E = 1.4426950408889634
VMEM_BYTES = 60 * 2**20


def dot_nn(left, right):
    return lax.dot_general(
        left, right, (((1,), (0,)), ((), ())), preferred_element_type=jnp.float32
    )


def dot_nt(left, right):
    return lax.dot_general(
        left, right, (((1,), (1,)), ((), ())), preferred_element_type=jnp.float32
    )


def dot_tn(left, right):
    return lax.dot_general(
        left, right, (((0,), (0,)), ((), ())), preferred_element_type=jnp.float32
    )


def segment_start(starts, index):
    first = starts[0]
    for c in range(1, starts.shape[0]):
        first = jnp.where(index >= starts[c], starts[c], first)
    return first


def segment_end(starts, index, total):
    last = jnp.int32(total)
    for c in range(starts.shape[0] - 1, 0, -1):
        last = jnp.where(index < starts[c], starts[c], last)
    return last


def allowed_tile(starts, key_first, query_first, size, prompt_rows):
    key_index = key_first + lax.broadcasted_iota(jnp.int32, (size, size), 0)
    query_index = query_first + lax.broadcasted_iota(jnp.int32, (1, size), 1)
    own_start = jnp.full((1, size), prompt_rows, jnp.int32)
    for c in range(1, starts.shape[0]):
        own_start = jnp.where(query_index >= starts[c], starts[c], own_start)
    return (key_index <= query_index) & ((key_index < prompt_rows) | (key_index >= own_start))


def attend_forward_kernel(
    starts,
    query_pre,
    key_pre,
    value_t,
    query_inv,
    key_inv,
    query_gain,
    key_gain,
    cosine,
    sine,
    out,
    query,
    key,
    key_t,
    log_rows,
    *,
    size,
    prompt_rows,
    score_scale,
):
    i = pl.program_id(0)
    half = HEAD // 2
    total, columns = key.shape
    spans = [slice(h * HEAD, (h + 1) * HEAD) for h in range(columns // HEAD)]
    prompt_blocks = prompt_rows // size

    @pl.when(i == 0)
    def _():
        @pl.loop(0, total // size)
        def _(b):
            at = pl.ds(pl.multiple_of(b * size, size), size)
            cos, sin = cosine[:, at], sine[:, at]
            for span in spans:
                for pre, inv, gain, is_key in (
                    (query_pre, query_inv, query_gain, False),
                    (key_pre, key_inv, key_gain, True),
                ):
                    normed = pre[span, at] * inv[:, at] * gain[span, :]
                    former, latter = normed[:half], normed[half:]
                    turned = jnp.concatenate(
                        [former * cos - latter * sin, latter * cos + former * sin], axis=0
                    )
                    if is_key:
                        key_t[span, at] = turned.astype(jnp.bfloat16)
                        key[at, span] = turned.T.astype(jnp.bfloat16)
                    else:
                        turned = turned * (score_scale * LOG2E)
                        query[at, span] = turned.T.astype(jnp.bfloat16)

    query_first = i * size
    here = pl.ds(pl.multiple_of(query_first, size), size)
    chunk = size // 2
    parts = [slice(c * chunk, (c + 1) * chunk) for c in range(2)]
    work = [(span, part) for span in spans for part in parts]
    query_all = [query[here, span] for span in spans]
    query_rows = [rows[part] for rows in query_all for part in parts]

    def fold(j, states, masked):
        at = pl.ds(pl.multiple_of(j * size, size), size)
        scores = [dot_nt(key[at, span], rows) for (span, _), rows in zip(work, query_rows)]
        if masked:
            allowed = allowed_tile(starts, j * size, query_first, size, prompt_rows)
        made = []
        for (span, part), score, (highest, denominator, weighted) in zip(work, scores, states):
            if masked:
                score = jnp.where(allowed[:, part], score, MASKED)
            new_high = jnp.maximum(highest, jnp.max(score, axis=0, keepdims=True))
            shrink = jnp.exp2(highest - new_high)
            unnormed = jnp.exp2(score - new_high)
            denominator = denominator * shrink + jnp.sum(unnormed, axis=0, keepdims=True)
            weighted = weighted * shrink + dot_nn(value_t[span, at], unnormed.astype(jnp.bfloat16))
            made.append((new_high, denominator, weighted))
        return tuple(made)

    states = tuple(
        (
            jnp.full((1, chunk), MASKED, jnp.float32),
            jnp.zeros((1, chunk), jnp.float32),
            jnp.zeros((HEAD, chunk), jnp.float32),
        )
        for _ in work
    )
    in_prompt = i < prompt_blocks
    whole = jnp.where(in_prompt, i, prompt_blocks)
    states = lax.fori_loop(0, whole, lambda j, s: fold(j, s, False), states)
    own_first = jnp.where(in_prompt, i, segment_start(starts, query_first) // size)
    states = lax.fori_loop(own_first, i + 1, lambda j, s: fold(j, s, True), states)
    for k, ((span, part), (highest, denominator, weighted)) in enumerate(zip(work, states)):
        out[part, span] = (weighted / denominator).T.astype(jnp.bfloat16)
        log_rows[k // 2 : k // 2 + 1, part] = highest + jnp.log2(denominator)


def attend_forward(starts, query_pre, key_pre, value_t, query_inv, key_inv, query_gain, key_gain, cosine, sine, size, prompt_rows, score_scale):
    columns, total = query_pre.shape
    heads = columns // HEAD
    pairs = total * total // 2

    def once(shape):
        return pl.BlockSpec(shape, lambda i, s: (0, 0), pipeline_mode=pl.Buffered(1))

    wide, tall, row = (columns, total), (total, columns), (1, total)
    gain, table = (columns, 1), (HEAD // 2, total)
    return pl.pallas_call(
        partial(attend_forward_kernel, size=size, prompt_rows=prompt_rows, score_scale=score_scale),
        grid_spec=pltpu.PrefetchScalarGridSpec(
            num_scalar_prefetch=1,
            grid=(total // size,),
            in_specs=[once(k) for k in (wide, wide, wide, row, row, gain, gain, table, table)],
            out_specs=[
                pl.BlockSpec((size, columns), lambda i, s: (i, 0)),
                pl.BlockSpec(tall, lambda i, s: (0, 0)),
                pl.BlockSpec(tall, lambda i, s: (0, 0)),
                pl.BlockSpec(wide, lambda i, s: (0, 0)),
                pl.BlockSpec((heads, size), lambda i, s: (0, i)),
            ],
        ),
        out_shape=[
            jax.ShapeDtypeStruct(tall, jnp.bfloat16),
            jax.ShapeDtypeStruct(tall, jnp.bfloat16),
            jax.ShapeDtypeStruct(tall, jnp.bfloat16),
            jax.ShapeDtypeStruct(wide, jnp.bfloat16),
            jax.ShapeDtypeStruct((heads, total), jnp.float32),
        ],
        compiler_params=pltpu.CompilerParams(vmem_limit_bytes=VMEM_BYTES),
        cost_estimate=pl.CostEstimate(
            flops=12 * pairs * columns, bytes_accessed=20 * total * columns, transcendentals=pairs * heads
        ),
        name="attend_forward",
    )(starts, query_pre, key_pre, value_t, query_inv, key_inv, query_gain, key_gain, cosine, sine)


def attend_backward_kernel(
    starts,
    query,
    key,
    key_t,
    value_t,
    out_grad,
    out,
    log_rows,
    query_pre,
    key_pre,
    query_inv,
    key_inv,
    query_gain,
    key_gain,
    cosine,
    sine,
    query_scaled,
    key_scaled,
    value_grad,
    dots,
    query_gain_grad,
    key_gain_grad,
    query_sum,
    key_sum,
    row_dot,
    *,
    size,
    prompt_rows,
    score_scale,
):
    j = pl.program_id(0)
    half = HEAD // 2
    total, columns = key.shape
    spans = [slice(h * HEAD, (h + 1) * HEAD) for h in range(columns // HEAD)]
    blocks = total // size
    prompt_blocks = prompt_rows // size

    @pl.when(j == 0)
    def _():
        query_sum[...] = jnp.zeros_like(query_sum)

        @pl.loop(0, blocks)
        def _(b):
            at = pl.ds(pl.multiple_of(b * size, size), size)
            for h, span in enumerate(spans):
                product = out_grad[at, span].astype(jnp.float32) * out[at, span].astype(jnp.float32)
                row_dot[h : h + 1, at] = jnp.sum(product.T, axis=0, keepdims=True)

    chunk = size // 2
    here = pl.ds(pl.multiple_of(j * size, size), size)
    key_rows = [key[here, span] for span in spans]
    key_cols = [key_t[span, here] for span in spans]
    value_rows = [value_t[span, here].T for span in spans]

    def fold(i, states, masked):
        if masked:
            allowed = allowed_tile(starts, j * size, i * size, size, prompt_rows)
        made = list(states)
        for c in range(2):
            at = pl.ds(pl.multiple_of(i * size + c * chunk, chunk), chunk)
            query_rows = [query[at, span] for span in spans]
            grad_rows = [out_grad[at, span] for span in spans]
            scores = [dot_nt(k, q) for k, q in zip(key_rows, query_rows)]
            prob_grads = [dot_nt(v, g) for v, g in zip(value_rows, grad_rows)]
            for h, span in enumerate(spans):
                key_part, value_part = made[h]
                prob = jnp.exp2(scores[h] - log_rows[h : h + 1, at])
                if masked:
                    prob = jnp.where(allowed[:, c * chunk : (c + 1) * chunk], prob, 0.0)
                score_grad = (prob * (prob_grads[h] - row_dot[h : h + 1, at])).astype(jnp.bfloat16)
                value_part = value_part + dot_nn(prob.astype(jnp.bfloat16), grad_rows[h])
                key_part = key_part + dot_nn(score_grad, query_rows[h])
                query_sum[span, at] += dot_nn(key_cols[h], score_grad)
                made[h] = (key_part, value_part)
        return tuple(made)

    states = tuple(
        (jnp.zeros((size, HEAD), jnp.float32), jnp.zeros((size, HEAD), jnp.float32)) for _ in spans
    )
    in_prompt = j < prompt_blocks
    last_own = (segment_end(starts, (j + 1) * size - 1, total) - 1) // size + 1
    masked_end = jnp.where(in_prompt, j + 1, last_own)
    states = lax.fori_loop(j, masked_end, lambda i, s: fold(i, s, True), states)
    whole_end = jnp.where(in_prompt, blocks, masked_end)
    states = lax.fori_loop(masked_end, whole_end, lambda i, s: fold(i, s, False), states)
    for span, (key_part, value_part) in zip(spans, states):
        key_sum[span, here] = key_part.T
        value_grad[span, here] = value_part.T.astype(jnp.bfloat16)

    @pl.when(j == blocks - 1)
    def _():
        query_gain_grad[...] = jnp.zeros_like(query_gain_grad)
        key_gain_grad[...] = jnp.zeros_like(key_gain_grad)

        @pl.loop(0, blocks)
        def _(b):
            at = pl.ds(pl.multiple_of(b * size, size), size)
            cos, sin = cosine[:, at], sine[:, at]
            for place, (grad, factor, pre, inv, gain, scaled, gain_grad) in enumerate(
                (
                    (query_sum, score_scale, query_pre, query_inv, query_gain, query_scaled, query_gain_grad),
                    (key_sum, 1.0 / LOG2E, key_pre, key_inv, key_gain, key_scaled, key_gain_grad),
                )
            ):
                summed = None
                for span in spans:
                    turned = grad[span, at] * factor
                    former, latter = turned[:half], turned[half:]
                    back = jnp.concatenate(
                        [former * cos + latter * sin, latter * cos - former * sin], axis=0
                    )
                    before = pre[span, at]
                    gain_grad[span, :] += jnp.sum(
                        back * (before * inv[:, at]), axis=1, keepdims=True
                    )
                    back = back * gain[span, :]
                    scaled[span, at] = back
                    dot = jnp.sum(back * before, axis=0, keepdims=True)
                    summed = dot if summed is None else summed + dot
                dots[place : place + 1, at] = summed


def attend_backward(starts, query, key, key_t, value_t, out_grad, out, log_rows, query_pre, key_pre, query_inv, key_inv, query_gain, key_gain, cosine, sine, size, prompt_rows, score_scale):
    columns, total = query_pre.shape
    heads = columns // HEAD
    pairs = total * total // 2

    def once(shape):
        return pl.BlockSpec(shape, lambda j, s: (0, 0), pipeline_mode=pl.Buffered(1))

    wide, tall, row = (columns, total), (total, columns), (1, total)
    gain, table, per_head = (columns, 1), (HEAD // 2, total), (heads, total)
    return pl.pallas_call(
        partial(attend_backward_kernel, size=size, prompt_rows=prompt_rows, score_scale=score_scale),
        grid_spec=pltpu.PrefetchScalarGridSpec(
            num_scalar_prefetch=1,
            grid=(total // size,),
            in_specs=[
                once(k)
                for k in (tall, tall, wide, wide, tall, tall, per_head, wide, wide, row, row, gain, gain, table, table)
            ],
            out_specs=[once(k) for k in (wide, wide, wide, (2, total), gain, gain)],
            scratch_shapes=[
                pltpu.VMEM(wide, jnp.float32),
                pltpu.VMEM(wide, jnp.float32),
                pltpu.VMEM(per_head, jnp.float32),
            ],
        ),
        out_shape=[
            jax.ShapeDtypeStruct(wide, jnp.float32),
            jax.ShapeDtypeStruct(wide, jnp.float32),
            jax.ShapeDtypeStruct(wide, jnp.bfloat16),
            jax.ShapeDtypeStruct((2, total), jnp.float32),
            jax.ShapeDtypeStruct(gain, jnp.float32),
            jax.ShapeDtypeStruct(gain, jnp.float32),
        ],
        compiler_params=pltpu.CompilerParams(vmem_limit_bytes=VMEM_BYTES),
        cost_estimate=pl.CostEstimate(
            flops=24 * pairs * columns, bytes_accessed=40 * total * columns, transcendentals=pairs * heads
        ),
        name="attend_backward",
    )(starts, query, key, key_t, value_t, out_grad, out, log_rows, query_pre, key_pre, query_inv, key_inv, query_gain, key_gain, cosine, sine)


def project_kernel(places, *refs, count):
    blocks = refs[:count]
    w_t, gain = refs[count : count + 2]
    hidden, query_pre, key_pre, value_t, squares = refs[-5:]
    columns = query_pre.shape[0]
    for b, block in enumerate(blocks):

        @pl.when(pl.program_id(0) // 2 == b)
        def _(block=block):
            rows = block[...].astype(jnp.float32)
            inverse = lax.rsqrt(jnp.mean(rows * rows, axis=-1, keepdims=True) + EPSILON)
            hidden[...] = (rows * inverse * gain[...]).astype(jnp.bfloat16)

    for k, out in enumerate((query_pre, key_pre)):
        made = dot_nt(w_t[k * columns : (k + 1) * columns, :], hidden[...])
        out[...] = made
        squares[k : k + 1, :] = jnp.sum(made * made, axis=0, keepdims=True)
    value_t[...] = dot_nt(w_t[2 * columns :, :], hidden[...]).astype(jnp.bfloat16)


def project(places, blocks, rows, w_t, gain, held, total):
    count, width = len(blocks), blocks[0].shape[1]
    columns = w_t.shape[0] // 3
    tile = rows // 2
    held = () if held is None else tuple(held)

    def block_spec(b):
        return pl.BlockSpec((tile, width), lambda i, p: (jnp.clip(i - 2 * b, 0, 1), 0))

    def there(shape, along):
        if along == 0:
            return pl.BlockSpec(shape, lambda i, p: (2 * p[i // 2] + i % 2, 0))
        return pl.BlockSpec(shape, lambda i, p: (0, 2 * p[i // 2] + i % 2))

    return pl.pallas_call(
        partial(project_kernel, count=count),
        grid_spec=pltpu.PrefetchScalarGridSpec(
            num_scalar_prefetch=1,
            grid=(2 * count,),
            in_specs=[block_spec(b) for b in range(count)]
            + [
                pl.BlockSpec(w_t.shape, lambda i, p: (0, 0)),
                pl.BlockSpec((1, width), lambda i, p: (0, 0)),
            ]
            + [pl.BlockSpec(memory_space=pl.ANY)] * len(held),
            out_specs=[
                there((tile, width), 0),
                there((columns, tile), 1),
                there((columns, tile), 1),
                there((columns, tile), 1),
                there((2, tile), 1),
            ],
        ),
        out_shape=[
            jax.ShapeDtypeStruct((total, width), jnp.bfloat16),
            jax.ShapeDtypeStruct((columns, total), jnp.float32),
            jax.ShapeDtypeStruct((columns, total), jnp.float32),
            jax.ShapeDtypeStruct((columns, total), jnp.bfloat16),
            jax.ShapeDtypeStruct((2, total), jnp.float32),
        ],
        input_output_aliases={3 + count + k: k for k in range(len(held))},
        compiler_params=pltpu.CompilerParams(vmem_limit_bytes=VMEM_BYTES),
        cost_estimate=pl.CostEstimate(
            flops=6 * count * rows * width * columns,
            bytes_accessed=count * (4 * rows * width + 10 * rows * columns) + 6 * width * columns,
            transcendentals=count * rows,
        ),
        name="project",
    )(places, *blocks, w_t, gain, *held)


def place_rows_kernel(places, *refs):
    *pieces, out = refs
    for k, piece in enumerate(pieces):
        out[places[k]] = piece[...]


def place_rows(places, blocks, first, rows):
    width = blocks[0].shape[1]
    return pl.pallas_call(
        place_rows_kernel,
        grid_spec=pltpu.PrefetchScalarGridSpec(
            num_scalar_prefetch=1,
            grid=(1,),
            in_specs=[pl.BlockSpec((rows, width), lambda i, p: (first // rows, 0))] * len(blocks),
            out_specs=pl.BlockSpec((len(blocks), rows, width), lambda i, p: (0, 0, 0)),
        ),
        out_shape=jax.ShapeDtypeStruct((len(blocks), rows, width), blocks[0].dtype),
        compiler_params=pltpu.CompilerParams(vmem_limit_bytes=VMEM_BYTES),
        name="place_rows",
    )(places, *blocks)


def hidden_term_kernel(place, heads_grad, w_t, out_rows, *refs, start, halves):
    outs = refs[-2:] if halves else refs[-1:]
    rows = heads_grad.shape[1]
    term = dot_tn(heads_grad[...], w_t[...])
    below = out_rows[0]
    if halves:
        cut = outs[0].shape[0]
        outs[0][...] = term[:cut].astype(jnp.bfloat16)
        outs[1][: rows - cut, :] = term[cut:].astype(jnp.bfloat16)
        outs[1][rows - cut :, :] = below
        return
    (out,) = outs
    got = refs[0]
    stop = start + got.shape[0]
    upper = min(stop, rows)
    if start:
        out[:start, :] = term[:start].astype(jnp.bfloat16)
    if upper < rows:
        out[upper:rows, :] = term[upper:].astype(jnp.bfloat16)
    out[start:upper, :] = (
        term[start:upper] + got[: upper - start, :].astype(jnp.float32)
    ).astype(jnp.bfloat16)
    if stop > rows:
        below = below.astype(jnp.float32) + got[rows - start :, :].astype(jnp.float32)
    out[rows:, :] = below.astype(jnp.bfloat16)


def hidden_term(place, heads_grad, w_t, out_rows, rows, got=None, start=0):
    columns, width = w_t.shape
    whole = rows + out_rows.shape[1]
    tile = min(512, width)
    halves = got is None
    gots, outs = ([], [whole // 2] * 2) if halves else ([got], [whole])
    made = pl.pallas_call(
        partial(hidden_term_kernel, start=start, halves=halves),
        grid_spec=pltpu.PrefetchScalarGridSpec(
            num_scalar_prefetch=1,
            grid=(width // tile,),
            in_specs=[
                pl.BlockSpec((columns, rows), lambda i, p: (0, p[0])),
                pl.BlockSpec((columns, tile), lambda i, p: (0, i)),
                pl.BlockSpec((1, whole - rows, tile), lambda i, p: (p[0], 0, i)),
            ]
            + [pl.BlockSpec((g.shape[0], tile), lambda i, p: (0, i)) for g in gots],
            out_specs=[pl.BlockSpec((count, tile), lambda i, p: (0, i)) for count in outs],
        ),
        out_shape=[jax.ShapeDtypeStruct((count, width), jnp.bfloat16) for count in outs],
        compiler_params=pltpu.CompilerParams(vmem_limit_bytes=VMEM_BYTES),
        cost_estimate=pl.CostEstimate(
            flops=2 * rows * width * columns,
            bytes_accessed=2 * columns * (rows + width) + 4 * whole * width,
            transcendentals=0,
        ),
        name="hidden_term",
    )(place, heads_grad, w_t, out_rows, *gots)
    return made if halves else made[0]


def own_term_kernel(place, heads_grad, w_t, out_rows, before, past, hidden_grad, out_grad):
    rows = heads_grad.shape[1]
    term = dot_tn(heads_grad[...], w_t[...])
    got = before[...].astype(jnp.float32) + past[...].astype(jnp.float32)
    hidden_grad[...] = term + got[:rows]
    out_grad[...] = out_rows[0].astype(jnp.float32) + got[rows:]


def own_term(place, heads_grad, w_t, out_rows, rows, before, past):
    columns, width = w_t.shape
    extra = out_rows.shape[1]
    tile = min(512, width)
    return pl.pallas_call(
        own_term_kernel,
        grid_spec=pltpu.PrefetchScalarGridSpec(
            num_scalar_prefetch=1,
            grid=(width // tile,),
            in_specs=[
                pl.BlockSpec((columns, rows), lambda i, p: (0, p[0])),
                pl.BlockSpec((columns, tile), lambda i, p: (0, i)),
                pl.BlockSpec((1, extra, tile), lambda i, p: (p[0], 0, i)),
                pl.BlockSpec((rows + extra, tile), lambda i, p: (0, i)),
                pl.BlockSpec((rows + extra, tile), lambda i, p: (0, i)),
            ],
            out_specs=[
                pl.BlockSpec((rows, tile), lambda i, p: (0, i)),
                pl.BlockSpec((extra, tile), lambda i, p: (0, i)),
            ],
        ),
        out_shape=[
            jax.ShapeDtypeStruct((rows, width), jnp.float32),
            jax.ShapeDtypeStruct((extra, width), jnp.float32),
        ],
        compiler_params=pltpu.CompilerParams(vmem_limit_bytes=VMEM_BYTES),
        cost_estimate=pl.CostEstimate(
            flops=2 * rows * width * columns,
            bytes_accessed=2 * columns * (rows + width) + 8 * (rows + extra) * width,
            transcendentals=0,
        ),
        name="own_term",
    )(place, heads_grad, w_t, out_rows, before, past)


def out_grad_kernel(branch, w_out, out):
    out[0] = dot_nt(branch[...], w_out[...]).astype(jnp.bfloat16)


def out_grad_of(branch, w_out, contexts):
    rows, width = branch.shape
    columns = w_out.shape[0] // contexts
    return pl.pallas_call(
        out_grad_kernel,
        grid=(contexts,),
        in_specs=[
            pl.BlockSpec((rows, width), lambda i: (0, 0)),
            pl.BlockSpec((columns, width), lambda i: (i, 0)),
        ],
        out_specs=pl.BlockSpec((1, rows, columns), lambda i: (i, 0, 0)),
        out_shape=jax.ShapeDtypeStruct((contexts, rows, columns), jnp.bfloat16),
        compiler_params=pltpu.CompilerParams(vmem_limit_bytes=VMEM_BYTES),
        cost_estimate=pl.CostEstimate(
            flops=2 * rows * width * width, bytes_accessed=2 * width * width, transcendentals=0
        ),
        name="out_grad",
    )(branch, w_out)


def heads_grad_kernel(query_scaled, key_scaled, value_grad, query_pre, key_pre, inverse, dots, out):
    columns = query_scaled.shape[0]
    for k, (scaled, pre) in enumerate(((query_scaled, query_pre), (key_scaled, key_pre))):
        inv = inverse[k : k + 1, :]
        factor = inv * inv * dots[k : k + 1, :]
        out[k * columns : (k + 1) * columns, :] = (inv * (scaled[...] - pre[...] * factor)).astype(
            jnp.bfloat16
        )
    out[2 * columns :, :] = value_grad[...]


def heads_grad_of(query_scaled, key_scaled, value_grad, query_pre, key_pre, inverse, dots):
    columns, total = query_scaled.shape
    tile = total // 4
    wide = pl.BlockSpec((columns, tile), lambda i: (0, i))
    row = pl.BlockSpec((2, tile), lambda i: (0, i))
    return pl.pallas_call(
        heads_grad_kernel,
        grid=(4,),
        in_specs=[wide] * 5 + [row] * 2,
        out_specs=pl.BlockSpec((3 * columns, tile), lambda i: (0, i)),
        out_shape=jax.ShapeDtypeStruct((3 * columns, total), jnp.bfloat16),
        compiler_params=pltpu.CompilerParams(vmem_limit_bytes=VMEM_BYTES),
        cost_estimate=pl.CostEstimate(
            flops=8 * columns * total, bytes_accessed=24 * columns * total, transcendentals=0
        ),
        name="heads_grad",
    )(query_scaled, key_scaled, value_grad, query_pre, key_pre, inverse, dots)


def heads_product_kernel(heads_grad, hidden, others, out):
    columns = heads_grad.shape[0]
    out[0, :, :columns] = dot_nn(heads_grad[...], hidden[...]).T.astype(jnp.bfloat16)
    out[0, :, columns:] = others[...].astype(jnp.bfloat16)


def heads_product_of(heads_grad, hidden_all, others, contexts):
    columns, total = heads_grad.shape
    width = hidden_all.shape[1]
    tile, extra = width // contexts, others.shape[1]
    return pl.pallas_call(
        heads_product_kernel,
        grid=(contexts,),
        in_specs=[
            pl.BlockSpec((columns, total), lambda i: (0, 0), pipeline_mode=pl.Buffered(1)),
            pl.BlockSpec((total, tile), lambda i: (0, i)),
            pl.BlockSpec((tile, extra), lambda i: (i, 0)),
        ],
        out_specs=pl.BlockSpec((1, tile, columns + extra), lambda i: (i, 0, 0)),
        out_shape=jax.ShapeDtypeStruct((contexts, tile, columns + extra), jnp.bfloat16),
        compiler_params=pltpu.CompilerParams(vmem_limit_bytes=VMEM_BYTES),
        cost_estimate=pl.CostEstimate(
            flops=2 * columns * total * width,
            bytes_accessed=2 * total * (columns + width),
            transcendentals=0,
        ),
        name="heads_product",
    )(heads_grad, hidden_all, others)


def gather_pieces_kernel(me, *refs):
    *pieces, out = refs
    for step, piece in enumerate(pieces):
        out[lax.rem(me[0] + step, len(pieces))] = piece[...]


def gather_pieces(me, pieces):
    return pl.pallas_call(
        gather_pieces_kernel,
        grid_spec=pltpu.PrefetchScalarGridSpec(
            num_scalar_prefetch=1,
            grid=(1,),
            in_specs=[pl.BlockSpec(piece.shape, lambda i, m: (0, 0)) for piece in pieces],
            out_specs=pl.BlockSpec((len(pieces),) + pieces[0].shape, lambda i, m: (0, 0, 0)),
        ),
        out_shape=jax.ShapeDtypeStruct((len(pieces),) + pieces[0].shape, pieces[0].dtype),
        compiler_params=pltpu.CompilerParams(vmem_limit_bytes=VMEM_BYTES),
        name="gather_pieces",
    )(me[None], *pieces)


def slot_match(rank_row, slots):
    return lax.broadcasted_iota(jnp.int32, (slots, rank_row.shape[1]), 0) == rank_row


def slot_gates(match, gate_row):
    return jnp.sum(jnp.where(match, gate_row, 0.0), axis=1, keepdims=True)


def experts_forward_kernel(*refs, count, slots, aliased, tiles):
    ranks, gates = refs[:2]
    blocks = refs[2 : 2 + count]
    w_gate, w_up, w_down = refs[2 + count : 5 + count]
    refs = refs[5 + count + aliased :]
    taken, active, gate_slope, up_slope = refs[:4]
    outs = refs[4 : 4 + count]
    made, weights = refs[4 + count :]
    e, f = pl.program_id(0), pl.program_id(1)
    tile, wide_tile = w_gate.shape[2], w_down.shape[2]

    @pl.when(f == 0)
    def _():
        for b in range(count):
            here = slice(b * slots, (b + 1) * slots)
            match = slot_match(ranks[b, e], slots)
            weights[here, :] = slot_gates(match, gates[b, e])
            taken[0, here, :] = dot_nn(match.astype(jnp.bfloat16), blocks[b][...]).astype(
                jnp.bfloat16
            )

    @pl.when(f < tiles)
    def _():
        at = pl.ds(pl.multiple_of(f * tile, tile), tile)
        rows = taken[0]
        gate_pre = dot_nn(rows, w_gate[0])
        up_pre = dot_nn(rows, w_up[0])
        sigmoid_gate = 1.0 / (1.0 + jnp.exp(-gate_pre))
        silu = gate_pre * sigmoid_gate
        active[0, :, at] = (silu * up_pre).astype(jnp.bfloat16)
        up_slope[0, :, at] = silu.astype(jnp.bfloat16)
        gate_slope[0, :, at] = (up_pre * (sigmoid_gate + silu * (1.0 - sigmoid_gate))).astype(
            jnp.bfloat16
        )

    @pl.when(f >= tiles)
    def _():
        at = pl.ds(pl.multiple_of((f - tiles) * wide_tile, wide_tile), wide_tile)
        made[e, :, at] = (dot_nn(active[0], w_down[0]) * weights[...]).astype(jnp.bfloat16)

    @pl.when((f == pl.num_programs(1) - 1) & (e == pl.num_programs(0) - 1))
    def _():
        combine(ranks, made, outs, count, slots)


def combine(ranks, made, outs, count, slots):
    for b in range(count):
        summed = None
        for k in range(made.shape[0]):
            match = slot_match(ranks[b, k], slots).astype(jnp.float32).astype(jnp.bfloat16)
            term = dot_tn(match, made[k, b * slots : (b + 1) * slots, :])
            summed = term if summed is None else summed + term
        outs[b][...] = summed.astype(jnp.bfloat16)


def experts_backward_kernel(*refs, count, slots, aliased, tiles):
    ranks, gates = refs[:2]
    blocks = refs[2 : 2 + count]
    w_gate, w_up, w_down, gate_slope, up_slope = refs[2 + count : 7 + count]
    refs = refs[7 + count + aliased :]
    taken, gate_grad, up_grad = refs[:3]
    outs = refs[3 : 3 + count]
    (made,) = refs[3 + count :]
    e, f = pl.program_id(0), pl.program_id(1)
    tile, wide_tile = w_down.shape[1], w_gate.shape[1]

    @pl.when(f == 0)
    def _():
        for b in range(count):
            match = slot_match(ranks[b, e], slots)
            weight = slot_gates(match, gates[b, e])
            taken[0, b * slots : (b + 1) * slots, :] = (
                dot_nn(match.astype(jnp.bfloat16), blocks[b][...]) * weight
            ).astype(jnp.bfloat16)

    @pl.when(f < tiles)
    def _():
        at = pl.ds(pl.multiple_of(f * tile, tile), tile)
        active_grad = dot_nt(taken[0], w_down[0])
        gate_grad[0, :, at] = (active_grad * gate_slope[0].astype(jnp.float32)).astype(jnp.bfloat16)
        up_grad[0, :, at] = (active_grad * up_slope[0].astype(jnp.float32)).astype(jnp.bfloat16)

    @pl.when(f >= tiles)
    def _():
        at = pl.ds(pl.multiple_of((f - tiles) * wide_tile, wide_tile), wide_tile)
        made[e, :, at] = (dot_nt(gate_grad[0], w_gate[0]) + dot_nt(up_grad[0], w_up[0])).astype(
            jnp.bfloat16
        )

    @pl.when((f == pl.num_programs(1) - 1) & (e == pl.num_programs(0) - 1))
    def _():
        combine(ranks, made, outs, count, slots)


def experts_stage(
    forward, ranks, gates, blocks, weights, slopes, held, place, slots, all_slots, light=False
):
    count = len(blocks)
    rows, width = blocks[0].shape
    experts, _, hidden_units = weights[0].shape
    tile, wide_tile = min(512, hidden_units), min(1024, width)
    tiles, wide_tiles = hidden_units // tile, width // wide_tile
    part = count * slots

    def first(f):
        return jnp.minimum(f, tiles - 1)

    def later(f):
        return jnp.maximum(f - tiles, 0)

    info = pl.BlockSpec((count, experts, 1, rows), lambda e, f: (0, 0, 0, 0))
    block = pl.BlockSpec((rows, width), lambda e, f: (0, 0))
    wide = pl.BlockSpec((1, part, width), lambda e, f: (e, place, 0))
    narrow = pl.BlockSpec((1, part, hidden_units), lambda e, f: (e, place, 0))
    slope = pl.BlockSpec((1, part, tile), lambda e, f: (e, 0, first(f)))
    own = pl.BlockSpec((1, part, hidden_units), lambda e, f: (e, 0, 0))
    if forward:
        kernel, name = experts_forward_kernel, "experts_forward"
        into = pl.BlockSpec((1, width, tile), lambda e, f: (e, 0, first(f)))
        back = pl.BlockSpec((1, hidden_units, wide_tile), lambda e, f: (e, 0, later(f)))
        narrow_outs, own_outs, scratch = 1, 2, [pltpu.VMEM((part, 1), jnp.float32)]
    else:
        kernel, name = experts_backward_kernel, "experts_backward"
        into = pl.BlockSpec((1, wide_tile, hidden_units), lambda e, f: (e, later(f), 0))
        back = pl.BlockSpec((1, tile, width), lambda e, f: (e, first(f), 0))
        narrow_outs, own_outs, scratch = 2, 0, []
    held = () if held is None else tuple(held)
    before = 2 + count + 3 + len(slopes)
    scale = 0 if light else 1
    flops = 2 * experts * part * width * (3 * hidden_units + 2 * rows)
    return pl.pallas_call(
        partial(kernel, count=count, slots=slots, aliased=len(held), tiles=tiles),
        grid=(experts, tiles + wide_tiles),
        in_specs=[info, info]
        + [block] * count
        + [into, into, back]
        + [slope] * len(slopes)
        + [pl.BlockSpec(memory_space=pl.ANY)] * len(held),
        out_specs=[wide] + [narrow] * narrow_outs + [own] * own_outs + [block] * count,
        out_shape=[jax.ShapeDtypeStruct((experts, all_slots, width), jnp.bfloat16)]
        + [jax.ShapeDtypeStruct((experts, all_slots, hidden_units), jnp.bfloat16)] * narrow_outs
        + [jax.ShapeDtypeStruct((experts, part, hidden_units), jnp.bfloat16)] * own_outs
        + [jax.ShapeDtypeStruct((rows, width), jnp.bfloat16)] * count,
        scratch_shapes=[pltpu.VMEM((experts, part, width), jnp.bfloat16)] + scratch,
        input_output_aliases={before + k: k for k in range(len(held))},
        compiler_params=pltpu.CompilerParams(vmem_limit_bytes=VMEM_BYTES),
        cost_estimate=pl.CostEstimate(
            flops=scale * flops,
            bytes_accessed=scale
            * 2
            * (3 * experts * width * hidden_units + 4 * count * rows * width),
            transcendentals=scale * experts * part * hidden_units,
        ),
        name=name,
    )(ranks, gates, *blocks, *weights, *slopes, *held)


def ring_of(contexts):
    order = list(range(0, contexts, 2)) + list(range(contexts - 1, 0, -2))
    place_of = [order.index(c) for c in range(contexts)]
    up = [(order[p], order[(p + 1) % contexts]) for p in range(contexts)]
    down = [(b, a) for a, b in up]
    return order, place_of, up, down


class RingGather:
    def __init__(self, own, ring):
        _, _, self.up, self.down = ring
        self.half = len(self.up) // 2
        self.step = 0
        self.blocks = {0: own}
        self.from_before = self.from_after = own

    def advance(self, *earlier):
        self.step += 1
        before, past = self.from_before, self.from_after
        if earlier:
            before, past = lax.optimization_barrier((before, past) + earlier)[:2]
        if self.step < self.half:
            self.from_before = lax.ppermute(before, "ctx", self.up)
            self.from_after = lax.ppermute(past, "ctx", self.down)
            self.blocks[-self.step] = self.from_before
            self.blocks[self.step] = self.from_after
            return (-self.step, self.step)
        cut = before.shape[0] // 2
        first = lax.ppermute(before[:cut], "ctx", self.up)
        second = lax.ppermute(past[cut:], "ctx", self.down)
        self.blocks[self.half] = jnp.concatenate([first, second], axis=0)
        return (self.half,)


def add_low(left, right):
    return (left.astype(jnp.float32) + right.astype(jnp.float32)).astype(jnp.bfloat16)


class RingScatter:
    def __init__(self, ring):
        _, _, self.up, self.down = ring
        self.half = len(self.up) // 2
        self.step = self.half

    def prepare(self, terms, *earlier):
        if self.step == self.half:
            far = after(terms[self.half], *earlier)
            cut = far.shape[0] // 2
            before, past = far[:cut], far[cut:]
        else:
            before, past = terms[-self.step], terms[self.step]
            got_before, got_past = self.to_before, self.to_after
            if earlier:
                before, past = lax.optimization_barrier((before, past) + earlier)[:2]
            cut = got_before.shape[0]
            if cut < before.shape[0]:
                before = jnp.concatenate([add_low(got_before, before[:cut]), before[cut:]], axis=0)
                past = jnp.concatenate([past[:cut], add_low(got_past, past[cut:])], axis=0)
            else:
                before, past = add_low(got_before, before), add_low(got_past, past)
        self.payload = (before, past)
        return self.payload

    def send(self, *earlier):
        before, past = self.payload
        if earlier:
            before, past = lax.optimization_barrier((before, past) + earlier)[:2]
        self.to_before = lax.ppermute(before, "ctx", self.down)
        self.to_after = lax.ppermute(past, "ctx", self.up)
        self.step -= 1
        return self.payload

    def advance(self, terms, *earlier):
        self.prepare(terms, *earlier)
        return self.send()

    def finish(self, own):
        return (
            own.astype(jnp.float32)
            + self.to_before.astype(jnp.float32)
            + self.to_after.astype(jnp.float32)
        )


def sum_over_ctx(values, contexts):
    bit = 1
    while bit < contexts:
        values = values + lax.ppermute(values, "ctx", [(c, c ^ bit) for c in range(contexts)])
        bit *= 2
    return values


def after(value, *earlier):
    return lax.optimization_barrier((value,) + earlier)[0]


def shards_by_heads(
    tokens,
    cotangent,
    cont_lengths,
    routes,
    gates,
    attn_gain,
    query_gain,
    key_gain,
    ffn_gain,
    w_query,
    w_key,
    w_value,
    w_out,
    w_gate,
    w_up,
    w_down,
):
    both = ("ctx", "fsdp")
    contexts, splits = lax.axis_size("ctx"), lax.axis_size("fsdp")
    rows, width = tokens.shape[1:]
    route_count = routes.shape[2]
    total = rows * contexts
    prompt_rows = total // 2
    columns = width // contexts
    size = min(512, prompt_rows)
    local_experts = w_gate.shape[0]
    expert_total = local_experts * contexts
    slots = max(2, rows * route_count * 5 // (4 * expert_total))
    all_slots = contexts * slots
    score_scale = HEAD ** (-0.5)
    me = lax.axis_index("ctx")
    ring = ring_of(contexts)
    half = contexts // 2
    place = jnp.where(me % 2 == 0, me // 2, contexts - 1 - me // 2)

    def owner(offset):
        at = (place + offset) % contexts
        return jnp.where(at < half, 2 * at, 2 * (contexts - 1 - at) + 1)

    others = [k for step in range(1, half) for k in (-step, step)] + [half]

    own_rows = w_out.shape[0]
    token_ring = RingGather(jnp.concatenate([tokens[0], w_out], axis=0), ring)

    chosen = routes[0].T[None] == jnp.arange(expert_total, dtype=jnp.int32)[:, None, None]
    member = jnp.any(chosen, axis=1)
    gate_rows = jnp.sum(jnp.where(chosen, gates[0].T[None], 0.0), axis=1)
    earlier = jnp.tril(jnp.ones((rows, rows), jnp.bfloat16), -1)
    rank = jnp.einsum(
        "et,ut->eu", member.astype(jnp.bfloat16), earlier, preferred_element_type=jnp.float32
    )
    rank = jnp.where(member, rank, -1.0)
    rank_high = jnp.floor(rank / 16.0)
    gate_high = gate_rows.astype(jnp.bfloat16).astype(jnp.float32)
    routing = jnp.stack([rank_high, rank - 16.0 * rank_high, gate_high, gate_rows - gate_high])
    routing = routing.astype(jnp.bfloat16).reshape(4, contexts, local_experts * rows)
    routing = jnp.transpose(routing, (1, 0, 2)).reshape(contexts, own_rows, -1)
    routing_columns = routing.shape[2]

    cut = jnp.stack([w_query, w_key, w_value]).reshape(3, own_rows, contexts, columns)
    cut = jnp.transpose(cut, (2, 1, 0, 3)).reshape(contexts, own_rows, 3 * columns)
    own_gains = jnp.stack([attn_gain, query_gain, key_gain, ffn_gain], axis=1)
    cut = jnp.concatenate(
        [cut, jnp.broadcast_to(own_gains, (contexts,) + own_gains.shape), routing], axis=2
    )
    spare = -cut.shape[2] % 128
    cut = jnp.pad(cut, ((0, 0), (0, 0), (0, spare)))
    pieces = []
    for step in range(contexts):
        piece = lax.dynamic_index_in_dim(cut, (me - step) % contexts, 0, keepdims=False)
        if step:
            pairs = [(c, (c - step) % contexts) for c in range(contexts)]
            piece = lax.ppermute(piece, "ctx", pairs)
        pieces.append(piece)
    first_piece = pieces[1]
    pieces = gather_pieces(me, pieces)
    token_ring.advance(first_piece)
    gate_all = lax.all_gather(after(w_gate, pieces), "fsdp", axis=1, tiled=True)
    w_all = lax.all_gather(pieces, "fsdp", axis=1, tiled=True).reshape(width, -1)
    up_all = lax.all_gather(w_up, "fsdp", axis=1, tiled=True)
    for _ in range(2, half):
        token_ring.advance()
    w_t = w_all[:, : 3 * columns].T
    all_gains = w_all[:, 3 * columns : 3 * columns + 4].astype(jnp.float32).T
    gain_attn, gain_ffn = all_gains[0], all_gains[3]
    gain_query = lax.dynamic_slice_in_dim(all_gains[1], me * columns, columns)[:, None]
    gain_key = lax.dynamic_slice_in_dim(all_gains[2], me * columns, columns)[:, None]

    owners = owner(jnp.arange(contexts, dtype=jnp.int32))
    routing = pieces[:, :, 3 * columns + 4 : 3 * columns + 4 + routing_columns]
    routing = routing.reshape(contexts, 4, local_experts, 1, rows)[owners].astype(jnp.float32)
    all_ranks = (16.0 * routing[:, 0] + routing[:, 1]).astype(jnp.int32)
    all_gates = routing[:, 2] + routing[:, 3]

    lengths_in = cont_lengths[0]
    token_index = jnp.arange(total, dtype=jnp.int32)
    _, position = places(token_index, lengths_in, prompt_rows)
    starts = prompt_rows + jnp.cumsum(lengths_in) - lengths_in
    frequency = ROPE_BASE ** (-jnp.arange(HEAD // 2).astype(jnp.float32) / (HEAD // 2))
    angles = frequency[:, None] * position.astype(jnp.float32)[None, :]
    cosine, sine = jnp.cos(angles), jnp.sin(angles)

    def project_all(offsets, made):
        blocks = [token_ring.blocks[offset] for offset in offsets]
        places_of = owner(jnp.asarray(offsets, jnp.int32))
        return project(places_of, blocks, rows, w_t, gain_attn[None], made, total)

    made = project_all([0] + others[: 2 * (half - 2)], None)
    token_ring.advance(made[-1], up_all)
    made = project_all(others[2 * (half - 2) : -1], made)
    made = project_all(others[-1:], made)
    hidden_all, query_pre, key_pre, value_t, squares = made
    w_out_rows = place_rows(
        owners, [token_ring.blocks[k if k <= half else k - contexts] for k in range(contexts)], rows, own_rows
    )
    out_all = lax.all_gather(w_out_rows, "fsdp", axis=1, tiled=True).reshape(width, width)
    down_all = lax.all_gather(w_down, "fsdp", axis=1, tiled=True)

    squares = sum_over_ctx(squares, contexts)
    inverse = lax.rsqrt(squares / width + EPSILON)
    query_inv, key_inv = inverse[0:1], inverse[1:2]
    grad_ring = RingGather(cotangent[0], ring)
    grad_ring.advance(squares)

    attended, query, key, key_t, log_rows = attend_forward(
        starts, query_pre, key_pre, value_t, query_inv, key_inv, gain_query, gain_key, cosine, sine, size, prompt_rows, score_scale
    )
    sent = after(attended, grad_ring.from_before, grad_ring.from_after)
    back = lax.all_to_all(
        sent.reshape(contexts, rows, columns), "ctx", split_axis=0, concat_axis=0, tiled=True
    )
    grad_ring.advance(attended)
    own_attended = jnp.transpose(back, (1, 0, 2)).reshape(rows, width)
    inputs = tokens[0].astype(jnp.float32)
    mixed = inputs + jnp.dot(own_attended, out_all, preferred_element_type=jnp.float32)
    mixed_inv = lax.rsqrt(jnp.mean(mixed * mixed, axis=-1, keepdims=True) + EPSILON)
    second = (mixed * mixed_inv * gain_ffn).astype(jnp.bfloat16)

    second_ring = RingGather(second, ring)
    weights = (gate_all, up_all, down_all)

    def stage_info(offsets):
        ranks = jnp.stack([all_ranks[k] for k in offsets])
        stage_gates = jnp.stack([all_gates[k] for k in offsets])
        if len(offsets) == 2:
            return ranks, stage_gates, offsets[1] - 1
        return ranks, stage_gates, contexts - (2 if offsets[0] == 0 else 1)

    stages = [(0,)] + [(-step, step) for step in range(1, half)] + [(half,)]
    infos = [stage_info(stage) for stage in stages]
    result_terms, second_terms, slopes = {}, {}, {}
    kept = kept_grads = None

    def forward(step, *earlier):
        nonlocal kept
        ranks, stage_gates, at = infos[step]
        ranks = after(ranks, *earlier) if earlier else ranks
        blocks = [second_ring.blocks[k] for k in stages[step]]
        made = experts_stage(
            True, ranks, stage_gates, blocks, weights, (), kept, at, slots, all_slots
        )
        kept, slopes[step], terms = made[:2], made[2:4], made[4:]
        result_terms.update(zip(stages[step], terms))
        return terms[0]

    def backward(step, *earlier, light=False):
        nonlocal kept_grads
        ranks, stage_gates, at = infos[step]
        ranks = after(ranks, *earlier) if earlier else ranks
        blocks = [grad_ring.blocks[k] for k in stages[step]]
        made = experts_stage(
            False,
            ranks,
            stage_gates,
            blocks,
            weights,
            slopes[step],
            kept_grads,
            at,
            slots,
            all_slots,
            light,
        )
        kept_grads, terms = made[:3], made[3:]
        second_terms.update(zip(stages[step], terms))
        return terms[0]

    def weight_grad(left, right):
        return jnp.einsum("emd,emf->edf", left, right, preferred_element_type=jnp.float32).astype(
            jnp.bfloat16
        )

    second_ring.advance()
    grad_second = (grad_ring.from_before, grad_ring.from_after)
    done = forward(0)
    done = backward(0, done, *grad_second, light=True)
    for step in range(1, half):
        near = [second_ring.blocks[k] for k in stages[step]]
        second_ring.advance(done)
        waits = (done,)
        if step > 1:
            waits += (grad_ring.from_before, grad_ring.from_after)
        if step == half - 1:
            waits = (done, grad_ring.blocks[half])
        else:
            grad_ring.advance(done, *near)
        done = forward(step, *waits)
        if step < half - 1:
            done = backward(step, done, light=True)
    done = forward(half, done)

    second_sum, result_sum = RingScatter(ring), RingScatter(ring)
    result_sum.advance(result_terms)
    backward(half, done)
    sent = second_sum.advance(second_terms, result_sum.to_before, result_sum.to_after)
    sent += result_sum.prepare(result_terms, *sent)
    result_sum.send()
    backward(half - 1, *sent)
    rows_taken, active = kept
    route_grad, gate_grad, up_grad = kept_grads
    sent = second_sum.advance(second_terms)
    gate_product = weight_grad(
        after(rows_taken, result_sum.to_before, result_sum.to_after, *sent), gate_grad
    )
    sent = second_sum.advance(second_terms, gate_product)
    up_product = weight_grad(after(rows_taken, *sent), up_grad)
    sent = second_sum.advance(second_terms, up_product)
    result_sum.prepare(result_terms, *sent)
    down_product = weight_grad(after(active, *result_sum.payload), route_grad)
    second_grad = second_sum.finish(after(second_terms[0], down_product))

    def fsdp_sum_low(product):
        return lax.psum_scatter(product, "fsdp", scatter_dimension=1, tiled=True)

    def fsdp_sum(product):
        return fsdp_sum_low(product).astype(jnp.float32)

    gate_w_grad = fsdp_sum(gate_product)
    up_w_grad = fsdp_sum(up_product)

    upstream = cotangent[0].astype(jnp.float32)
    mixed_normed = mixed * mixed_inv
    ffn_gain_grad = jnp.sum(second_grad * mixed_normed, axis=0)
    scaled = second_grad * gain_ffn
    mixed_grad = upstream + mixed_inv * (
        scaled - mixed_normed * jnp.mean(scaled * mixed_normed, axis=-1, keepdims=True)
    )
    branch = mixed_grad.astype(jnp.bfloat16)
    out_grad = out_grad_of(branch, out_all, contexts)
    w_out_grad = lax.dot_general(
        own_attended, after(branch, out_grad), (((0,), (0,)), ((), ())), preferred_element_type=jnp.float32
    ).astype(jnp.bfloat16)
    out_grad = lax.all_to_all(out_grad, "ctx", split_axis=0, concat_axis=0, tiled=True)
    out_grad = out_grad.reshape(total, columns)
    w_out_grad = fsdp_sum_low(
        w_out_grad.reshape(contexts, splits * own_rows, width)
    )
    result_sum.send(out_grad)

    query_scaled, key_scaled, value_grad, dots, query_gain_grad, key_gain_grad = attend_backward(
        starts, query, key, key_t, value_t, out_grad, attended, log_rows, query_pre, key_pre, query_inv, key_inv, gain_query, gain_key, cosine, sine, size, prompt_rows, score_scale
    )
    dots = after(dots, result_sum.to_before, result_sum.to_after)
    result_sum.prepare(result_terms, dots)
    dots = sum_over_ctx(dots, contexts) / width
    dots = after(dots, *result_sum.payload)
    heads_grad = heads_grad_of(
        query_scaled, key_scaled, value_grad, query_pre, key_pre, inverse, dots
    )

    def own_columns(grad):
        return lax.dynamic_update_slice_in_dim(
            jnp.zeros((width, 1), jnp.float32), grad, me * columns, 0
        )

    other_grads = jnp.concatenate(
        [
            ffn_gain_grad[:, None],
            own_columns(query_gain_grad),
            own_columns(key_gain_grad),
            jnp.zeros((width, 125), jnp.float32),
        ],
        axis=1,
    )
    def term(offset, *earlier, **got):
        at = after(owner(offset)[None], *earlier)
        return hidden_term(at, heads_grad, w_t, w_out_grad, rows, **got)

    down_w_grad = fsdp_sum(down_product)
    hidden_sum = RingScatter(ring)
    hidden_sum.payload = far = term(half)
    hidden_sum.send()
    result_sum.send(*far)
    heads_product = heads_product_of(
        heads_grad, hidden_all, after(other_grads, *far), contexts
    )
    heads_w_grad = fsdp_sum_low(after(heads_product, hidden_sum.to_before, hidden_sum.to_after))
    done = (heads_product,)
    for step in range(half - 1, 0, -1):
        start = far[0].shape[0] if step == half - 1 else 0
        if step == 1:
            done = (result_sum.to_before, result_sum.to_after)
        if step == half - 2:
            done = (down_w_grad,)
        hidden_sum.payload = (
            term(-step, *done, got=hidden_sum.to_before),
            term(step, *done, got=hidden_sum.to_after, start=start),
        )
        hidden_sum.send()
        done = ()
    hidden_grad, w_out_grad = own_term(
        owner(0)[None], heads_grad, w_t, w_out_grad, rows, hidden_sum.to_before, hidden_sum.to_after
    )
    routed = result_sum.finish(result_terms[0])
    output = (mixed + routed)[None]

    heads_w_grad = lax.all_to_all(
        heads_w_grad, "ctx", split_axis=0, concat_axis=0, tiled=True
    ).astype(jnp.float32)
    other_grads = jnp.sum(heads_w_grad[:, :, 3 * columns : 3 * columns + 3], axis=0)
    heads_w_grad = jnp.transpose(
        heads_w_grad[:, :, : 3 * columns].reshape(contexts, own_rows, 3, columns), (2, 1, 0, 3)
    ).reshape(3, own_rows, width)

    attn_gain_grad = jnp.sum(
        w_query.astype(jnp.float32) * heads_w_grad[0]
        + w_key.astype(jnp.float32) * heads_w_grad[1]
        + w_value.astype(jnp.float32) * heads_w_grad[2],
        axis=1,
    ) / attn_gain.astype(jnp.float32)

    attn_inv = lax.rsqrt(jnp.mean(inputs * inputs, axis=-1, keepdims=True) + EPSILON)
    normed = inputs * attn_inv
    scaled = hidden_grad * gain_attn
    input_grad = mixed_grad + attn_inv * (
        scaled - normed * jnp.mean(scaled * normed, axis=-1, keepdims=True)
    )
    return (
        output,
        input_grad[None],
        attn_gain_grad,
        other_grads[:, 1],
        other_grads[:, 2],
        other_grads[:, 0],
        heads_w_grad[0],
        heads_w_grad[1],
        heads_w_grad[2],
        w_out_grad,
        gate_w_grad,
        up_w_grad,
        down_w_grad,
    )


def solution(mesh):
    contexts = mesh.shape["ctx"]
    fits = contexts == 8
    placed = (
        P("fsdp", "ctx", None),
        P("fsdp", "ctx", None),
        P("fsdp", None),
        P("fsdp", "ctx", None),
        P("fsdp", "ctx", None),
        P(("ctx", "fsdp")),
        P(("ctx", "fsdp")),
        P(("ctx", "fsdp")),
        P(("ctx", "fsdp")),
        P(("ctx", "fsdp"), None),
        P(("ctx", "fsdp"), None),
        P(("ctx", "fsdp"), None),
        P(("ctx", "fsdp"), None),
        P("ctx", "fsdp", None),
        P("ctx", "fsdp", None),
        P("ctx", "fsdp", None),
    )
    return jax.shard_map(
        shards_by_heads if fits else shards_wide,
        mesh=mesh,
        in_specs=placed,
        out_specs=(
            P("fsdp", "ctx", None),
            P("fsdp", "ctx", None),
            P(("ctx", "fsdp")),
            P(("ctx", "fsdp")),
            P(("ctx", "fsdp")),
            P(("ctx", "fsdp")),
            P(("ctx", "fsdp"), None),
            P(("ctx", "fsdp"), None),
            P(("ctx", "fsdp"), None),
            P(("ctx", "fsdp"), None),
            P("ctx", "fsdp", None),
            P("ctx", "fsdp", None),
            P("ctx", "fsdp", None),
        ),
        check_vma=False,
    )
```

```python
from functools import partial

import jax
import jax.numpy as jnp
from jax import lax
from jax.experimental import pallas as pl
from jax.experimental.pallas import tpu as pltpu
from jax.sharding import PartitionSpec as P

HEAD = 128


EPSILON = 1e-05
ROPE_BASE = 10000.0
MASKED = -1e30


def norm_rows(values_in, gain_in):
    return (
        values_in
        * lax.rsqrt(jnp.mean(values_in * values_in, axis=-1, keepdims=True) + EPSILON)
        * gain_in
    )


def places(token_index, lengths_in, prompt_rows):
    ends = prompt_rows + jnp.cumsum(lengths_in)
    passed = (token_index[:, None] >= ends[None, :]).astype(jnp.int32)
    before = jnp.sum(passed * lengths_in[None, :], axis=1)
    inside = token_index >= prompt_rows
    segment = jnp.where(inside, 1 + jnp.sum(passed, axis=1), 0)
    position = jnp.where(inside, token_index - before, token_index)
    return (segment, position)


def rotate(values_in, positions):
    full_shape = values_in.shape
    per_head = values_in.reshape(full_shape[:-1] + (full_shape[-1] // HEAD, HEAD))
    half_dim = HEAD // 2
    frequency = ROPE_BASE ** (-jnp.arange(half_dim).astype(values_in.dtype) / half_dim)
    angles = positions.astype(values_in.dtype)[..., None] * frequency
    cosine = jnp.cos(angles)[..., None, :]
    sine = jnp.sin(angles)[..., None, :]
    former = per_head[..., :half_dim]
    latter = per_head[..., half_dim:]
    turned = jnp.concatenate(
        [former * cosine - latter * sine, latter * cosine + former * sine], axis=-1
    )
    return turned.reshape(full_shape)


def allowed_pairs(query_index, query_seg, key_index, key_seg):
    return (key_index[None, :] <= query_index[:, None]) & (
        (key_seg[None, :] == 0) | (key_seg[None, :] == query_seg[:, None])
    )


def attend_fold(
    state_in,
    shard_piece,
    first_row,
    query_heads,
    own_index,
    own_seg,
    lengths_in,
    prompt_rows,
    score_scale,
):
    highest, denominator, weighted = state_in
    key_rows, value_rows = shard_piece
    piece_count = key_rows.shape[0]
    key_index = jnp.arange(piece_count, dtype=jnp.int32)
    key_seg, _ = places(key_index, lengths_in, prompt_rows)
    key_heads = key_rows.reshape(piece_count, -1, HEAD)
    value_heads = value_rows.reshape(piece_count, -1, HEAD)
    scores = (
        jnp.einsum("qhd,khd->hqk", query_heads, key_heads, preferred_element_type=jnp.float32)
        * score_scale
    )
    allowed = allowed_pairs(own_index, own_seg, key_index, key_seg)
    masked = jnp.where(allowed[None], scores, MASKED)
    new_high = jnp.maximum(highest, jnp.max(masked, axis=-1))
    shrink = jnp.exp(highest - new_high)
    unnormed = jnp.where(allowed[None], jnp.exp(masked - new_high[..., None]), 0.0)
    denominator = jnp.sum(unnormed, axis=-1)
    weighted = jnp.einsum(
        "hqk,khd->hqd",
        unnormed.astype(jnp.bfloat16),
        value_heads,
        preferred_element_type=jnp.float32,
    )
    return (new_high, denominator, weighted)


def pair_terms(
    query_heads,
    grad_heads,
    log_rows,
    dot_rows,
    query_index,
    query_seg,
    key_heads,
    value_heads,
    key_index,
    key_seg,
    score_scale,
):
    scores = (
        jnp.einsum("qhd,khd->hqk", query_heads, key_heads, preferred_element_type=jnp.float32)
        * score_scale
    )
    allowed = allowed_pairs(query_index, query_seg, key_index, key_seg)
    prob = jnp.where(
        allowed[None], jnp.exp(jnp.where(allowed[None], scores, MASKED) - log_rows[..., None]), 0.0
    )
    prob_grad = jnp.einsum(
        "qhd,khd->hqk", grad_heads, value_heads, preferred_element_type=jnp.float32
    )
    score_grad = (prob * (prob_grad - dot_rows[..., None])).astype(jnp.bfloat16)
    return (prob, score_grad)


def slot_targets(route_list, expert_total, capacity):
    onehot = (route_list[:, None] == jnp.arange(expert_total, dtype=jnp.int32)[None, :]).astype(
        jnp.int32
    )
    slot_rank = jnp.sum((jnp.cumsum(onehot, axis=0) - 1) * onehot, axis=1)
    return route_list * capacity + slot_rank


def shards_wide(
    tokens,
    cotangent,
    cont_lengths,
    routes,
    gates,
    attn_gain,
    query_gain,
    key_gain,
    ffn_gain,
    w_query,
    w_key,
    w_value,
    w_out,
    w_gate,
    w_up,
    w_down,
):
    row_count = tokens.shape[1]
    model_width = tokens.shape[2]
    route_count = routes.shape[2]
    context_size = lax.axis_size("ctx")
    all_rows = row_count * context_size
    prompt_rows = all_rows // 2
    local_experts = w_gate.shape[0]
    expert_total = local_experts * context_size
    capacity = max(2, row_count * route_count * 5 // (4 * expert_total))
    head_count = model_width // HEAD
    score_scale = HEAD ** (-0.5)
    lengths_in = cont_lengths[0]
    own_index = lax.axis_index("ctx") * row_count + jnp.arange(row_count, dtype=jnp.int32)
    own_seg, own_pos = places(own_index, lengths_in, prompt_rows)
    attention_set = (
        lax.all_gather(w_query, ("ctx", "fsdp"), axis=0, tiled=True),
        lax.all_gather(w_key, ("ctx", "fsdp"), axis=0, tiled=True),
        lax.all_gather(w_value, ("ctx", "fsdp"), axis=0, tiled=True),
        lax.all_gather(w_out, ("ctx", "fsdp"), axis=0, tiled=True),
        lax.all_gather(attn_gain, ("ctx", "fsdp"), axis=0, tiled=True),
        lax.all_gather(query_gain, ("ctx", "fsdp"), axis=0, tiled=True),
        lax.all_gather(key_gain, ("ctx", "fsdp"), axis=0, tiled=True),
        lax.all_gather(ffn_gain, ("ctx", "fsdp"), axis=0, tiled=True),
    )
    query_all, key_all, value_all, out_all = (
        attention_set[0],
        attention_set[1],
        attention_set[2],
        attention_set[3],
    )
    gain_attn = attention_set[4].astype(jnp.float32)
    gain_query = attention_set[5].astype(jnp.float32)
    gain_key = attention_set[6].astype(jnp.float32)
    gain_ffn = attention_set[7].astype(jnp.float32)
    expert_set = (
        lax.all_gather(w_gate, "fsdp", axis=1, tiled=True),
        lax.all_gather(w_up, "fsdp", axis=1, tiled=True),
        lax.all_gather(w_down, "fsdp", axis=1, tiled=True),
    )
    gate_all, up_all, down_all = expert_set
    inputs = tokens[0].astype(jnp.float32)
    normed, attn_pull = jax.vjp(norm_rows, inputs, gain_attn)
    hidden = normed.astype(jnp.bfloat16)
    query_pre = jnp.dot(hidden, query_all, preferred_element_type=jnp.float32)
    key_pre = jnp.dot(hidden, key_all, preferred_element_type=jnp.float32)
    values = jnp.dot(hidden, value_all, preferred_element_type=jnp.float32).astype(jnp.bfloat16)
    query_rot, query_pull = jax.vjp(
        lambda pre_in, gain_in: rotate(norm_rows(pre_in, gain_in), own_pos), query_pre, gain_query
    )
    key_rot, key_pull = jax.vjp(
        lambda pre_in, gain_in: rotate(norm_rows(pre_in, gain_in), own_pos), key_pre, gain_key
    )
    query_low = query_rot.astype(jnp.bfloat16)
    key_low = key_rot.astype(jnp.bfloat16)
    query_heads = query_low.reshape(row_count, head_count, HEAD)
    folder = partial(
        attend_fold,
        query_heads=query_heads,
        own_index=own_index,
        own_seg=own_seg,
        lengths_in=lengths_in,
        prompt_rows=prompt_rows,
        score_scale=score_scale,
    )
    start_state = (
        jnp.full((head_count, row_count), MASKED, jnp.float32),
        jnp.zeros((head_count, row_count), jnp.float32),
        jnp.zeros((head_count, row_count, HEAD), jnp.float32),
    )
    final_state = folder(
        start_state,
        (
            lax.all_gather(key_low, "ctx", axis=0, tiled=True),
            lax.all_gather(values, "ctx", axis=0, tiled=True),
        ),
        jnp.int32(0),
    )
    highest, denominator, weighted = final_state
    log_total = highest + jnp.log(denominator)
    attn_heads = jnp.transpose(weighted / denominator[..., None], (1, 0, 2))
    attended = attn_heads.reshape(row_count, model_width).astype(jnp.bfloat16)
    mixed = inputs + jnp.dot(attended, out_all, preferred_element_type=jnp.float32)
    normed_second, ffn_pull = jax.vjp(norm_rows, mixed, gain_ffn)
    second = normed_second.astype(jnp.bfloat16)
    route_list = routes[0].reshape(-1)
    targets = slot_targets(route_list, expert_total, capacity)

    def dispatch_rows(route_rows):
        buffer = (
            jnp.zeros((expert_total * capacity, model_width), jnp.bfloat16)
            .at[targets]
            .set(route_rows)
        )
        return buffer.reshape(context_size, local_experts * capacity, model_width)

    sent_rows = dispatch_rows(jnp.repeat(second, route_count, axis=0))
    arrived = lax.all_to_all(sent_rows, "ctx", split_axis=0, concat_axis=0, tiled=True).reshape(
        context_size, local_experts, capacity, model_width
    )
    gate_pre = jnp.einsum("sekd,edf->sekf", arrived, gate_all, preferred_element_type=jnp.float32)
    up_pre = jnp.einsum("sekd,edf->sekf", arrived, up_all, preferred_element_type=jnp.float32)
    active = (jax.nn.silu(gate_pre) * up_pre).astype(jnp.bfloat16)
    expert_out = jnp.einsum(
        "sekf,efd->sekd", active, down_all, preferred_element_type=jnp.float32
    ).astype(jnp.bfloat16)
    returned = lax.all_to_all(
        expert_out.reshape(context_size, local_experts * capacity, model_width),
        "ctx",
        split_axis=0,
        concat_axis=0,
        tiled=True,
    )
    per_route = (
        returned.reshape(expert_total * capacity, model_width)[targets]
        .astype(jnp.float32)
        .reshape(row_count, route_count, model_width)
    )
    gate_values = gates[0]
    result = mixed + jnp.sum(gate_values[..., None] * per_route, axis=1)
    output = result[None]
    upstream = cotangent[0].astype(jnp.float32)
    route_grad = (
        (gate_values[..., None] * upstream[:, None, :])
        .astype(jnp.bfloat16)
        .reshape(row_count * route_count, model_width)
    )
    grad_arrived = lax.all_to_all(
        dispatch_rows(route_grad), "ctx", split_axis=0, concat_axis=0, tiled=True
    ).reshape(context_size, local_experts, capacity, model_width)
    active_grad = jnp.einsum(
        "sekd,efd->sekf", grad_arrived, down_all, preferred_element_type=jnp.float32
    )
    down_w_grad = jnp.einsum(
        "sekf,sekd->efd", active, grad_arrived, preferred_element_type=jnp.float32
    )
    sigmoid_gate = jax.nn.sigmoid(gate_pre)
    gate_grad = (
        active_grad * up_pre * sigmoid_gate * (1.0 + gate_pre * (1.0 - sigmoid_gate))
    ).astype(jnp.bfloat16)
    up_grad = (active_grad * gate_pre * sigmoid_gate).astype(jnp.bfloat16)
    gate_w_grad = jnp.einsum(
        "sekd,sekf->edf", arrived, gate_grad, preferred_element_type=jnp.float32
    )
    up_w_grad = jnp.einsum("sekd,sekf->edf", arrived, up_grad, preferred_element_type=jnp.float32)
    arrived_grad = jnp.einsum(
        "sekf,edf->sekd", gate_grad, gate_all, preferred_element_type=jnp.float32
    )
    arrived_grad = (
        arrived_grad
        + jnp.einsum("sekf,edf->sekd", up_grad, up_all, preferred_element_type=jnp.float32)
    ).astype(jnp.bfloat16)
    grad_back = lax.all_to_all(
        arrived_grad.reshape(context_size, local_experts * capacity, model_width),
        "ctx",
        split_axis=0,
        concat_axis=0,
        tiled=True,
    )
    second_grad = jnp.sum(
        grad_back.reshape(expert_total * capacity, model_width)[targets]
        .astype(jnp.float32)
        .reshape(row_count, route_count, model_width),
        axis=1,
    )
    expert_grads = (
        lax.psum_scatter(
            gate_w_grad.astype(jnp.bfloat16), "fsdp", scatter_dimension=1, tiled=True
        ).astype(jnp.float32),
        lax.psum_scatter(
            up_w_grad.astype(jnp.bfloat16), "fsdp", scatter_dimension=1, tiled=True
        ).astype(jnp.float32),
        lax.psum_scatter(
            down_w_grad.astype(jnp.bfloat16), "fsdp", scatter_dimension=1, tiled=True
        ).astype(jnp.float32),
    )
    mixed_norm_grad, ffn_gain_grad = ffn_pull(second_grad)
    mixed_grad = upstream + mixed_norm_grad
    branch_grad = mixed_grad.astype(jnp.bfloat16)
    out_w_grad = jnp.dot(attended.T, branch_grad, preferred_element_type=jnp.float32)
    attended_grad = jnp.dot(branch_grad, out_all.T, preferred_element_type=jnp.float32).astype(
        jnp.bfloat16
    )
    grad_heads = attended_grad.reshape(row_count, head_count, HEAD)
    row_dot = jnp.transpose(jnp.sum(grad_heads.astype(jnp.float32) * attn_heads, axis=-1))
    keys_whole, values_whole = (
        lax.all_gather(key_low, "ctx", axis=0, tiled=True),
        lax.all_gather(values, "ctx", axis=0, tiled=True),
    )
    block_rows = min(1024, all_rows)
    block_count = all_rows // block_rows
    block_index = jnp.arange(all_rows, dtype=jnp.int32).reshape(block_count, block_rows)
    key_blocks = keys_whole.reshape(block_count, block_rows, model_width)
    value_blocks = values_whole.reshape(block_count, block_rows, model_width)

    def query_side(key_rows, value_rows, key_index):
        key_seg, _ = places(key_index, lengths_in, prompt_rows)
        key_heads = key_rows.reshape(block_rows, head_count, HEAD)
        value_heads = value_rows.reshape(block_rows, head_count, HEAD)
        prob, score_grad = pair_terms(
            query_heads,
            grad_heads,
            log_total,
            row_dot,
            own_index,
            own_seg,
            key_heads,
            value_heads,
            key_index,
            key_seg,
            score_scale,
        )
        query_term = (
            jnp.einsum("hqk,khd->qhd", score_grad, key_heads, preferred_element_type=jnp.float32)
            * score_scale
        )
        return (prob, score_grad, query_term)

    def back_block(query_grad, block_args):
        key_rows, value_rows, key_index = block_args
        prob, score_grad, query_term = query_side(key_rows, value_rows, key_index)
        key_term = (
            jnp.einsum("hqk,qhd->khd", score_grad, query_heads, preferred_element_type=jnp.float32)
            * score_scale
        )
        value_term = jnp.einsum(
            "hqk,qhd->khd",
            prob.astype(jnp.bfloat16),
            grad_heads,
            preferred_element_type=jnp.float32,
        )
        return (
            query_grad + query_term,
            (
                key_term.reshape(block_rows, model_width),
                value_term.reshape(block_rows, model_width),
            ),
        )

    query_grad, (key_terms, value_terms) = lax.scan(
        back_block,
        jnp.zeros((row_count, head_count, HEAD), jnp.float32),
        (key_blocks, value_blocks, block_index),
    )
    key_grad, value_grad = (
        lax.psum_scatter(
            key_terms.reshape(all_rows, model_width).astype(jnp.bfloat16),
            "ctx",
            scatter_dimension=0,
            tiled=True,
        ).astype(jnp.float32),
        lax.psum_scatter(
            value_terms.reshape(all_rows, model_width).astype(jnp.bfloat16),
            "ctx",
            scatter_dimension=0,
            tiled=True,
        ).astype(jnp.float32),
    )
    query_pre_grad, query_gain_grad = query_pull(query_grad.reshape(row_count, model_width))
    key_pre_grad, key_gain_grad = key_pull(key_grad)
    query_low_grad = query_pre_grad.astype(jnp.bfloat16)
    key_low_grad = key_pre_grad.astype(jnp.bfloat16)
    value_low_grad = value_grad.astype(jnp.bfloat16)
    query_w_grad = jnp.dot(hidden.T, query_low_grad, preferred_element_type=jnp.float32)
    key_w_grad = jnp.dot(hidden.T, key_low_grad, preferred_element_type=jnp.float32)
    value_w_grad = jnp.dot(hidden.T, value_low_grad, preferred_element_type=jnp.float32)
    hidden_grad = jnp.dot(query_low_grad, query_all.T, preferred_element_type=jnp.float32)
    hidden_grad = hidden_grad + jnp.dot(key_low_grad, key_all.T, preferred_element_type=jnp.float32)
    hidden_grad = hidden_grad + jnp.dot(
        value_low_grad, value_all.T, preferred_element_type=jnp.float32
    )
    input_norm_grad, attn_gain_grad = attn_pull(hidden_grad)
    input_grad = (mixed_grad + input_norm_grad)[None]
    summed_grads = (
        lax.psum_scatter(query_w_grad, ("ctx", "fsdp"), scatter_dimension=0, tiled=True),
        lax.psum_scatter(key_w_grad, ("ctx", "fsdp"), scatter_dimension=0, tiled=True),
        lax.psum_scatter(value_w_grad, ("ctx", "fsdp"), scatter_dimension=0, tiled=True),
        lax.psum_scatter(out_w_grad, ("ctx", "fsdp"), scatter_dimension=0, tiled=True),
        lax.psum_scatter(attn_gain_grad, ("ctx", "fsdp"), scatter_dimension=0, tiled=True),
        lax.psum_scatter(query_gain_grad, ("ctx", "fsdp"), scatter_dimension=0, tiled=True),
        lax.psum_scatter(key_gain_grad, ("ctx", "fsdp"), scatter_dimension=0, tiled=True),
        lax.psum_scatter(ffn_gain_grad, ("ctx", "fsdp"), scatter_dimension=0, tiled=True),
    )
    return (
        output,
        input_grad,
        summed_grads[4],
        summed_grads[5],
        summed_grads[6],
        summed_grads[7],
        summed_grads[0],
        summed_grads[1],
        summed_grads[2],
        summed_grads[3],
        expert_grads[0],
        expert_grads[1],
        expert_grads[2],
    )


HEADS = 16
LOG2E = 1.4426950408889634
VMEM_BYTES = 60 * 2**20


def dot_nn(left, right):
    return lax.dot_general(
        left, right, (((1,), (0,)), ((), ())), preferred_element_type=jnp.float32
    )


def dot_nt(left, right):
    return lax.dot_general(
        left, right, (((1,), (1,)), ((), ())), preferred_element_type=jnp.float32
    )


def dot_tn(left, right):
    return lax.dot_general(
        left, right, (((0,), (0,)), ((), ())), preferred_element_type=jnp.float32
    )


def segment_start(starts, index):
    first = starts[0]
    for c in range(1, starts.shape[0]):
        first = jnp.where(index >= starts[c], starts[c], first)
    return first


def segment_end(starts, index, total):
    last = jnp.int32(total)
    for c in range(starts.shape[0] - 1, 0, -1):
        last = jnp.where(index < starts[c], starts[c], last)
    return last


def allowed_tile(starts, key_first, query_first, size, prompt_rows):
    key_index = key_first + lax.broadcasted_iota(jnp.int32, (size, size), 0)
    query_index = query_first + lax.broadcasted_iota(jnp.int32, (1, size), 1)
    own_start = jnp.full((1, size), prompt_rows, jnp.int32)
    for c in range(1, starts.shape[0]):
        own_start = jnp.where(query_index >= starts[c], starts[c], own_start)
    return (key_index <= query_index) & ((key_index < prompt_rows) | (key_index >= own_start))


def attend_forward_kernel(
    starts,
    query_pre,
    key_pre,
    value_t,
    query_inv,
    key_inv,
    query_gain,
    key_gain,
    cosine,
    sine,
    out,
    query,
    key,
    key_t,
    log_rows,
    *,
    size,
    prompt_rows,
    score_scale,
):
    i = pl.program_id(0)
    half = HEAD // 2
    total, columns = key.shape
    spans = [slice(h * HEAD, (h + 1) * HEAD) for h in range(columns // HEAD)]
    prompt_blocks = prompt_rows // size

    @pl.when(i == 0)
    def _():
        @pl.loop(0, total // size)
        def _(b):
            at = pl.ds(pl.multiple_of(b * size, size), size)
            cos, sin = cosine[:, at], sine[:, at]
            for span in spans:
                for pre, inv, gain, is_key in (
                    (query_pre, query_inv, query_gain, False),
                    (key_pre, key_inv, key_gain, True),
                ):
                    normed = pre[span, at] * inv[:, at] * gain[span, :]
                    former, latter = normed[:half], normed[half:]
                    turned = jnp.concatenate(
                        [former * cos - latter * sin, latter * cos + former * sin], axis=0
                    )
                    if is_key:
                        key_t[span, at] = turned.astype(jnp.bfloat16)
                        key[at, span] = turned.T.astype(jnp.bfloat16)
                    else:
                        turned = turned * (score_scale * LOG2E)
                        query[at, span] = turned.T.astype(jnp.bfloat16)

    query_first = i * size
    here = pl.ds(pl.multiple_of(query_first, size), size)
    chunk = size // 2
    parts = [slice(c * chunk, (c + 1) * chunk) for c in range(2)]
    work = [(span, part) for span in spans for part in parts]
    query_all = [query[here, span] for span in spans]
    query_rows = [rows[part] for rows in query_all for part in parts]

    def fold(j, states, masked):
        at = pl.ds(pl.multiple_of(j * size, size), size)
        scores = [dot_nt(key[at, span], rows) for (span, _), rows in zip(work, query_rows)]
        if masked:
            allowed = allowed_tile(starts, j * size, query_first, size, prompt_rows)
        made = []
        for (span, part), score, (highest, denominator, weighted) in zip(work, scores, states):
            if masked:
                score = jnp.where(allowed[:, part], score, MASKED)
            new_high = jnp.maximum(highest, jnp.max(score, axis=0, keepdims=True))
            shrink = jnp.exp2(highest - new_high)
            unnormed = jnp.exp2(score - new_high)
            denominator = denominator * shrink + jnp.sum(unnormed, axis=0, keepdims=True)
            weighted = weighted * shrink + dot_nn(value_t[span, at], unnormed.astype(jnp.bfloat16))
            made.append((new_high, denominator, weighted))
        return tuple(made)

    states = tuple(
        (
            jnp.full((1, chunk), MASKED, jnp.float32),
            jnp.zeros((1, chunk), jnp.float32),
            jnp.zeros((HEAD, chunk), jnp.float32),
        )
        for _ in work
    )
    in_prompt = i < prompt_blocks
    whole = jnp.where(in_prompt, i, prompt_blocks)
    states = lax.fori_loop(0, whole, lambda j, s: fold(j, s, False), states)
    own_first = jnp.where(in_prompt, i, segment_start(starts, query_first) // size)
    states = lax.fori_loop(own_first, i + 1, lambda j, s: fold(j, s, True), states)
    for k, ((span, part), (highest, denominator, weighted)) in enumerate(zip(work, states)):
        out[part, span] = (weighted / denominator).T.astype(jnp.bfloat16)
        log_rows[k // 2 : k // 2 + 1, part] = highest + jnp.log2(denominator)


def attend_forward(starts, query_pre, key_pre, value_t, query_inv, key_inv, query_gain, key_gain, cosine, sine, size, prompt_rows, score_scale):
    columns, total = query_pre.shape
    heads = columns // HEAD
    pairs = total * total // 2

    def once(shape):
        return pl.BlockSpec(shape, lambda i, s: (0, 0), pipeline_mode=pl.Buffered(1))

    wide, tall, row = (columns, total), (total, columns), (1, total)
    gain, table = (columns, 1), (HEAD // 2, total)
    return pl.pallas_call(
        partial(attend_forward_kernel, size=size, prompt_rows=prompt_rows, score_scale=score_scale),
        grid_spec=pltpu.PrefetchScalarGridSpec(
            num_scalar_prefetch=1,
            grid=(total // size,),
            in_specs=[once(k) for k in (wide, wide, wide, row, row, gain, gain, table, table)],
            out_specs=[
                pl.BlockSpec((size, columns), lambda i, s: (i, 0)),
                pl.BlockSpec(tall, lambda i, s: (0, 0)),
                pl.BlockSpec(tall, lambda i, s: (0, 0)),
                pl.BlockSpec(wide, lambda i, s: (0, 0)),
                pl.BlockSpec((heads, size), lambda i, s: (0, i)),
            ],
        ),
        out_shape=[
            jax.ShapeDtypeStruct(tall, jnp.bfloat16),
            jax.ShapeDtypeStruct(tall, jnp.bfloat16),
            jax.ShapeDtypeStruct(tall, jnp.bfloat16),
            jax.ShapeDtypeStruct(wide, jnp.bfloat16),
            jax.ShapeDtypeStruct((heads, total), jnp.float32),
        ],
        compiler_params=pltpu.CompilerParams(vmem_limit_bytes=VMEM_BYTES),
        cost_estimate=pl.CostEstimate(
            flops=12 * pairs * columns, bytes_accessed=20 * total * columns, transcendentals=pairs * heads
        ),
        name="attend_forward",
    )(starts, query_pre, key_pre, value_t, query_inv, key_inv, query_gain, key_gain, cosine, sine)


def attend_backward_kernel(
    starts,
    query,
    key,
    key_t,
    value_t,
    out_grad,
    out,
    log_rows,
    query_pre,
    key_pre,
    query_inv,
    key_inv,
    query_gain,
    key_gain,
    cosine,
    sine,
    *refs,
    size,
    prompt_rows,
    score_scale,
):
    query_scaled, key_scaled, value_grad, query_gain_grad, key_gain_grad, dots = refs[-9:-3]
    query_sum, key_sum, row_dot = refs[-3:]
    j = pl.program_id(0)
    half = HEAD // 2
    total, columns = key.shape
    spans = [slice(h * HEAD, (h + 1) * HEAD) for h in range(columns // HEAD)]
    blocks = total // size
    prompt_blocks = prompt_rows // size

    @pl.when(j == 0)
    def _():
        query_sum[...] = jnp.zeros_like(query_sum)

        @pl.loop(0, blocks)
        def _(b):
            at = pl.ds(pl.multiple_of(b * size, size), size)
            for h, span in enumerate(spans):
                product = out_grad[at, span].astype(jnp.float32) * out[at, span].astype(jnp.float32)
                row_dot[h : h + 1, at] = jnp.sum(product.T, axis=0, keepdims=True)

    chunk = size // 2
    here = pl.ds(pl.multiple_of(j * size, size), size)
    key_rows = [key[here, span] for span in spans]
    key_cols = [key_t[span, here] for span in spans]
    value_rows = [value_t[span, here].T for span in spans]

    def fold(i, states, masked):
        if masked:
            allowed = allowed_tile(starts, j * size, i * size, size, prompt_rows)
        made = list(states)
        for c in range(2):
            at = pl.ds(pl.multiple_of(i * size + c * chunk, chunk), chunk)
            query_rows = [query[at, span] for span in spans]
            grad_rows = [out_grad[at, span] for span in spans]
            scores = [dot_nt(k, q) for k, q in zip(key_rows, query_rows)]
            prob_grads = [dot_nt(v, g) for v, g in zip(value_rows, grad_rows)]
            for h, span in enumerate(spans):
                key_part, value_part = made[h]
                prob = jnp.exp2(scores[h] - log_rows[h, :, at])
                if masked:
                    prob = jnp.where(allowed[:, c * chunk : (c + 1) * chunk], prob, 0.0)
                score_grad = (prob * (prob_grads[h] - row_dot[h : h + 1, at])).astype(jnp.bfloat16)
                value_part = value_part + dot_nn(prob.astype(jnp.bfloat16), grad_rows[h])
                key_part = key_part + dot_nn(score_grad, query_rows[h])
                query_sum[span, at] += dot_nn(key_cols[h], score_grad)
                made[h] = (key_part, value_part)
        return tuple(made)

    states = tuple(
        (jnp.zeros((size, HEAD), jnp.float32), jnp.zeros((size, HEAD), jnp.float32)) for _ in spans
    )
    in_prompt = j < prompt_blocks
    last_own = (segment_end(starts, (j + 1) * size - 1, total) - 1) // size + 1
    masked_end = jnp.where(in_prompt, j + 1, last_own)
    states = lax.fori_loop(j, masked_end, lambda i, s: fold(i, s, True), states)
    whole_end = jnp.where(in_prompt, blocks, masked_end)
    states = lax.fori_loop(masked_end, whole_end, lambda i, s: fold(i, s, False), states)
    for span, (key_part, value_part) in zip(spans, states):
        key_sum[span, here] = key_part.T
        value_grad[span, here] = value_part.T.astype(jnp.bfloat16)

    @pl.when(j == blocks - 1)
    def _():
        query_gain_grad[...] = jnp.zeros_like(query_gain_grad)
        key_gain_grad[...] = jnp.zeros_like(key_gain_grad)

        @pl.loop(0, blocks)
        def _(b):
            at = pl.ds(pl.multiple_of(b * size, size), size)
            cos, sin = cosine[:, at], sine[:, at]
            for place, (grad, factor, pre, inv, gain, scaled, gain_grad) in enumerate(
                (
                    (query_sum, score_scale, query_pre, query_inv, query_gain, query_scaled, query_gain_grad),
                    (key_sum, 1.0 / LOG2E, key_pre, key_inv, key_gain, key_scaled, key_gain_grad),
                )
            ):
                summed = None
                for span in spans:
                    turned = grad[span, at] * factor
                    former, latter = turned[:half], turned[half:]
                    back = jnp.concatenate(
                        [former * cos + latter * sin, latter * cos - former * sin], axis=0
                    )
                    before = pre[span, at]
                    gain_grad[span, :] += jnp.sum(
                        back * (before * inv[:, at]), axis=1, keepdims=True
                    )
                    back = back * gain[span, :]
                    scaled[span, at] = back
                    dot = jnp.sum(back * before, axis=0, keepdims=True)
                    summed = dot if summed is None else summed + dot
                dots[place : place + 1, at] = summed


def attend_backward(starts, head, held, query, key, key_t, value_t, out_grad, out, log_rows, query_pre, key_pre, query_inv, key_inv, query_gain, key_gain, cosine, sine, size, prompt_rows, score_scale):
    columns, total = query_pre.shape
    pairs = total * total // 2
    held = () if held is None else tuple(held)

    def once(shape, index):
        return pl.BlockSpec(shape, lambda j, s: index, pipeline_mode=pl.Buffered(1))

    wide, tall = once((HEAD, total), (head, 0)), once((total, HEAD), (0, head))
    row, table = once((1, total), (0, 0)), once((HEAD // 2, total), (0, 0))
    gain, per_head = once((HEAD, 1), (head, 0)), once((1, 1, total), (head, 0, 0))
    return pl.pallas_call(
        partial(attend_backward_kernel, size=size, prompt_rows=prompt_rows, score_scale=score_scale),
        grid_spec=pltpu.PrefetchScalarGridSpec(
            num_scalar_prefetch=1,
            grid=(total // size,),
            in_specs=[tall, tall, wide, wide, tall, tall, per_head, wide, wide, row, row, gain, gain, table, table]
            + [pl.BlockSpec(memory_space=pl.ANY)] * len(held),
            out_specs=[wide, wide, wide, gain, gain, once((2, total), (0, 0))],
            scratch_shapes=[
                pltpu.VMEM((HEAD, total), jnp.float32),
                pltpu.VMEM((HEAD, total), jnp.float32),
                pltpu.VMEM((1, total), jnp.float32),
            ],
        ),
        out_shape=[
            jax.ShapeDtypeStruct((columns, total), jnp.float32),
            jax.ShapeDtypeStruct((columns, total), jnp.float32),
            jax.ShapeDtypeStruct((columns, total), jnp.bfloat16),
            jax.ShapeDtypeStruct((columns, 1), jnp.float32),
            jax.ShapeDtypeStruct((columns, 1), jnp.float32),
            jax.ShapeDtypeStruct((2, total), jnp.float32),
        ],
        input_output_aliases={16 + k: k for k in range(len(held))},
        compiler_params=pltpu.CompilerParams(vmem_limit_bytes=VMEM_BYTES),
        cost_estimate=pl.CostEstimate(
            flops=24 * pairs * HEAD, bytes_accessed=40 * total * HEAD, transcendentals=pairs
        ),
        name="attend_backward",
    )(starts, query, key, key_t, value_t, out_grad, out, log_rows, query_pre, key_pre, query_inv, key_inv, query_gain, key_gain, cosine, sine, *held)


def project_kernel(places, *refs, count):
    blocks = refs[:count]
    w_t, gain = refs[count : count + 2]
    hidden, query_pre, key_pre, value_t, squares = refs[-5:]
    columns = query_pre.shape[0]
    for b, block in enumerate(blocks):

        @pl.when(pl.program_id(0) // 2 == b)
        def _(block=block):
            rows = block[...].astype(jnp.float32)
            inverse = lax.rsqrt(jnp.mean(rows * rows, axis=-1, keepdims=True) + EPSILON)
            hidden[...] = (rows * inverse * gain[...]).astype(jnp.bfloat16)

    for k, out in enumerate((query_pre, key_pre)):
        made = dot_nt(w_t[k * columns : (k + 1) * columns, :], hidden[...])
        out[...] = made
        squares[k : k + 1, :] = jnp.sum(made * made, axis=0, keepdims=True)
    value_t[...] = dot_nt(w_t[2 * columns :, :], hidden[...]).astype(jnp.bfloat16)


def project(places, blocks, rows, w_t, gain, held, total):
    count, width = len(blocks), blocks[0].shape[1]
    columns = w_t.shape[0] // 3
    tile = rows // 2
    held = () if held is None else tuple(held)

    def block_spec(b):
        return pl.BlockSpec((tile, width), lambda i, p: (jnp.clip(i - 2 * b, 0, 1), 0))

    def there(shape, along):
        if along == 0:
            return pl.BlockSpec(shape, lambda i, p: (2 * p[i // 2] + i % 2, 0))
        return pl.BlockSpec(shape, lambda i, p: (0, 2 * p[i // 2] + i % 2))

    return pl.pallas_call(
        partial(project_kernel, count=count),
        grid_spec=pltpu.PrefetchScalarGridSpec(
            num_scalar_prefetch=1,
            grid=(2 * count,),
            in_specs=[block_spec(b) for b in range(count)]
            + [
                pl.BlockSpec(w_t.shape, lambda i, p: (0, 0)),
                pl.BlockSpec((1, width), lambda i, p: (0, 0)),
            ]
            + [pl.BlockSpec(memory_space=pl.ANY)] * len(held),
            out_specs=[
                there((tile, width), 0),
                there((columns, tile), 1),
                there((columns, tile), 1),
                there((columns, tile), 1),
                there((2, tile), 1),
            ],
        ),
        out_shape=[
            jax.ShapeDtypeStruct((total, width), jnp.bfloat16),
            jax.ShapeDtypeStruct((columns, total), jnp.float32),
            jax.ShapeDtypeStruct((columns, total), jnp.float32),
            jax.ShapeDtypeStruct((columns, total), jnp.bfloat16),
            jax.ShapeDtypeStruct((2, total), jnp.float32),
        ],
        input_output_aliases={3 + count + k: k for k in range(len(held))},
        compiler_params=pltpu.CompilerParams(vmem_limit_bytes=VMEM_BYTES),
        cost_estimate=pl.CostEstimate(
            flops=6 * count * rows * width * columns,
            bytes_accessed=count * (4 * rows * width + 10 * rows * columns) + 6 * width * columns,
            transcendentals=count * rows,
        ),
        name="project",
    )(places, *blocks, w_t, gain, *held)


def place_rows_kernel(places, *refs):
    *pieces, out = refs
    for k, piece in enumerate(pieces):
        out[places[k]] = piece[...]


def place_rows(places, blocks, first, rows):
    width = blocks[0].shape[1]
    return pl.pallas_call(
        place_rows_kernel,
        grid_spec=pltpu.PrefetchScalarGridSpec(
            num_scalar_prefetch=1,
            grid=(1,),
            in_specs=[pl.BlockSpec((rows, width), lambda i, p: (first // rows, 0))] * len(blocks),
            out_specs=pl.BlockSpec((len(blocks), rows, width), lambda i, p: (0, 0, 0)),
        ),
        out_shape=jax.ShapeDtypeStruct((len(blocks), rows, width), blocks[0].dtype),
        compiler_params=pltpu.CompilerParams(vmem_limit_bytes=VMEM_BYTES),
        name="place_rows",
    )(places, *blocks)


def hidden_term_kernel(place, heads_grad, w_t, out_rows, *refs, start, halves):
    outs = refs[-2:] if halves else refs[-1:]
    rows = heads_grad.shape[1]
    term = dot_tn(heads_grad[...], w_t[...])
    below = out_rows[0]
    if halves:
        cut = outs[0].shape[0]
        outs[0][...] = term[:cut].astype(jnp.bfloat16)
        outs[1][: rows - cut, :] = term[cut:].astype(jnp.bfloat16)
        outs[1][rows - cut :, :] = below
        return
    (out,) = outs
    got = refs[0]
    stop = start + got.shape[0]
    upper = min(stop, rows)
    if start:
        out[:start, :] = term[:start].astype(jnp.bfloat16)
    if upper < rows:
        out[upper:rows, :] = term[upper:].astype(jnp.bfloat16)
    out[start:upper, :] = (
        term[start:upper] + got[: upper - start, :].astype(jnp.float32)
    ).astype(jnp.bfloat16)
    if stop > rows:
        below = below.astype(jnp.float32) + got[rows - start :, :].astype(jnp.float32)
    out[rows:, :] = below.astype(jnp.bfloat16)


def hidden_term(place, heads_grad, w_t, out_rows, rows, got=None, start=0):
    columns, width = w_t.shape
    whole = rows + out_rows.shape[1]
    tile = min(512, width)
    halves = got is None
    gots, outs = ([], [whole // 2] * 2) if halves else ([got], [whole])
    made = pl.pallas_call(
        partial(hidden_term_kernel, start=start, halves=halves),
        grid_spec=pltpu.PrefetchScalarGridSpec(
            num_scalar_prefetch=1,
            grid=(width // tile,),
            in_specs=[
                pl.BlockSpec((columns, rows), lambda i, p: (0, p[0])),
                pl.BlockSpec((columns, tile), lambda i, p: (0, i)),
                pl.BlockSpec((1, whole - rows, tile), lambda i, p: (p[0], 0, i)),
            ]
            + [pl.BlockSpec((g.shape[0], tile), lambda i, p: (0, i)) for g in gots],
            out_specs=[pl.BlockSpec((count, tile), lambda i, p: (0, i)) for count in outs],
        ),
        out_shape=[jax.ShapeDtypeStruct((count, width), jnp.bfloat16) for count in outs],
        compiler_params=pltpu.CompilerParams(vmem_limit_bytes=VMEM_BYTES),
        cost_estimate=pl.CostEstimate(
            flops=0, bytes_accessed=0, transcendentals=0
        ),
        name="hidden_term",
    )(place, heads_grad, w_t, out_rows, *gots)
    return made if halves else made[0]


def own_term_kernel(place, heads_grad, w_t, out_rows, before, past, hidden_grad, out_grad):
    rows = heads_grad.shape[1]
    term = dot_tn(heads_grad[...], w_t[...])
    got = before[...].astype(jnp.float32) + past[...].astype(jnp.float32)
    hidden_grad[...] = term + got[:rows]
    out_grad[...] = out_rows[0].astype(jnp.float32) + got[rows:]


def own_term(place, heads_grad, w_t, out_rows, rows, before, past):
    columns, width = w_t.shape
    extra = out_rows.shape[1]
    tile = min(512, width)
    return pl.pallas_call(
        own_term_kernel,
        grid_spec=pltpu.PrefetchScalarGridSpec(
            num_scalar_prefetch=1,
            grid=(width // tile,),
            in_specs=[
                pl.BlockSpec((columns, rows), lambda i, p: (0, p[0])),
                pl.BlockSpec((columns, tile), lambda i, p: (0, i)),
                pl.BlockSpec((1, extra, tile), lambda i, p: (p[0], 0, i)),
                pl.BlockSpec((rows + extra, tile), lambda i, p: (0, i)),
                pl.BlockSpec((rows + extra, tile), lambda i, p: (0, i)),
            ],
            out_specs=[
                pl.BlockSpec((rows, tile), lambda i, p: (0, i)),
                pl.BlockSpec((extra, tile), lambda i, p: (0, i)),
            ],
        ),
        out_shape=[
            jax.ShapeDtypeStruct((rows, width), jnp.float32),
            jax.ShapeDtypeStruct((extra, width), jnp.float32),
        ],
        compiler_params=pltpu.CompilerParams(vmem_limit_bytes=VMEM_BYTES),
        cost_estimate=pl.CostEstimate(
            flops=2 * rows * width * columns,
            bytes_accessed=2 * columns * (rows + width) + 8 * (rows + extra) * width,
            transcendentals=0,
        ),
        name="own_term",
    )(place, heads_grad, w_t, out_rows, before, past)


def out_grad_kernel(branch, w_out, out):
    made = dot_nt(branch[...], w_out[...]).astype(jnp.bfloat16)
    columns = out.shape[2]
    for k in range(out.shape[0]):
        out[k] = made[:, k * columns : (k + 1) * columns]


def out_grad_of(branch, w_out, contexts):
    rows, width = branch.shape
    columns = w_out.shape[0] // contexts
    return pl.pallas_call(
        out_grad_kernel,
        grid=(contexts // 2,),
        in_specs=[
            pl.BlockSpec((rows, width), lambda i: (0, 0)),
            pl.BlockSpec((2 * columns, width), lambda i: (i, 0)),
        ],
        out_specs=pl.BlockSpec((2, rows, columns), lambda i: (i, 0, 0)),
        out_shape=jax.ShapeDtypeStruct((contexts, rows, columns), jnp.bfloat16),
        compiler_params=pltpu.CompilerParams(vmem_limit_bytes=VMEM_BYTES),
        cost_estimate=pl.CostEstimate(
            flops=2 * rows * width * width, bytes_accessed=2 * width * width, transcendentals=0
        ),
        name="out_grad",
    )(branch, w_out)


def heads_grad_kernel(query_scaled, key_scaled, value_grad, query_pre, key_pre, inverse, dots, out):
    columns = query_scaled.shape[0]
    for k, (scaled, pre) in enumerate(((query_scaled, query_pre), (key_scaled, key_pre))):
        inv = inverse[k : k + 1, :]
        factor = inv * inv * dots[k : k + 1, :]
        out[k * columns : (k + 1) * columns, :] = (inv * (scaled[...] - pre[...] * factor)).astype(
            jnp.bfloat16
        )
    out[2 * columns :, :] = value_grad[...]


def heads_grad_of(query_scaled, key_scaled, value_grad, query_pre, key_pre, inverse, dots):
    columns, total = query_scaled.shape
    tile = total // 4
    wide = pl.BlockSpec((columns, tile), lambda i: (0, i))
    row = pl.BlockSpec((2, tile), lambda i: (0, i))
    return pl.pallas_call(
        heads_grad_kernel,
        grid=(4,),
        in_specs=[wide] * 5 + [row] * 2,
        out_specs=pl.BlockSpec((3 * columns, tile), lambda i: (0, i)),
        out_shape=jax.ShapeDtypeStruct((3 * columns, total), jnp.bfloat16),
        compiler_params=pltpu.CompilerParams(vmem_limit_bytes=VMEM_BYTES),
        cost_estimate=pl.CostEstimate(
            flops=8 * columns * total, bytes_accessed=24 * columns * total, transcendentals=0
        ),
        name="heads_grad",
    )(query_scaled, key_scaled, value_grad, query_pre, key_pre, inverse, dots)


def heads_product_kernel(heads_grad, hidden, others, out):
    columns = heads_grad.shape[0]
    out[0, :, :columns] = dot_nn(heads_grad[...], hidden[...]).T.astype(jnp.bfloat16)
    out[0, :, columns:] = others[...].astype(jnp.bfloat16)


def heads_product_of(heads_grad, hidden_all, others, contexts):
    columns, total = heads_grad.shape
    width = hidden_all.shape[1]
    tile, extra = width // contexts, others.shape[1]
    return pl.pallas_call(
        heads_product_kernel,
        grid=(contexts,),
        in_specs=[
            pl.BlockSpec((columns, total), lambda i: (0, 0), pipeline_mode=pl.Buffered(1)),
            pl.BlockSpec((total, tile), lambda i: (0, i)),
            pl.BlockSpec((tile, extra), lambda i: (i, 0)),
        ],
        out_specs=pl.BlockSpec((1, tile, columns + extra), lambda i: (i, 0, 0)),
        out_shape=jax.ShapeDtypeStruct((contexts, tile, columns + extra), jnp.bfloat16),
        compiler_params=pltpu.CompilerParams(vmem_limit_bytes=VMEM_BYTES),
        cost_estimate=pl.CostEstimate(
            flops=2 * columns * total * width,
            bytes_accessed=2 * total * (columns + width),
            transcendentals=0,
        ),
        name="heads_product",
    )(heads_grad, hidden_all, others)


def gather_pieces_kernel(me, *refs):
    *pieces, out = refs
    for step, piece in enumerate(pieces):
        out[lax.rem(me[0] + step, len(pieces))] = piece[...]


def gather_pieces(me, pieces):
    return pl.pallas_call(
        gather_pieces_kernel,
        grid_spec=pltpu.PrefetchScalarGridSpec(
            num_scalar_prefetch=1,
            grid=(1,),
            in_specs=[pl.BlockSpec(piece.shape, lambda i, m: (0, 0)) for piece in pieces],
            out_specs=pl.BlockSpec((len(pieces),) + pieces[0].shape, lambda i, m: (0, 0, 0)),
        ),
        out_shape=jax.ShapeDtypeStruct((len(pieces),) + pieces[0].shape, pieces[0].dtype),
        compiler_params=pltpu.CompilerParams(vmem_limit_bytes=VMEM_BYTES),
        name="gather_pieces",
    )(me[None], *pieces)


def slot_match(rank_row, slots):
    return lax.broadcasted_iota(jnp.int32, (slots, rank_row.shape[1]), 0) == rank_row


def slot_gates(match, gate_row):
    return jnp.sum(jnp.where(match, gate_row, 0.0), axis=1, keepdims=True)


def experts_forward_kernel(*refs, count, slots, aliased, tiles):
    ranks, gates = refs[:2]
    blocks = refs[2 : 2 + count]
    w_gate, w_up, w_down = refs[2 + count : 5 + count]
    refs = refs[5 + count + aliased :]
    taken, active, gate_slope, up_slope = refs[:4]
    outs = refs[4 : 4 + count]
    made, weights = refs[4 + count :]
    e, f = pl.program_id(0), pl.program_id(1)
    tile, wide_tile = w_gate.shape[2], w_down.shape[2]

    @pl.when(f == 0)
    def _():
        for b in range(count):
            here = slice(b * slots, (b + 1) * slots)
            match = slot_match(ranks[b, e], slots)
            weights[here, :] = slot_gates(match, gates[b, e])
            taken[0, here, :] = dot_nn(match.astype(jnp.bfloat16), blocks[b][...]).astype(
                jnp.bfloat16
            )

    @pl.when(f < tiles)
    def _():
        at = pl.ds(pl.multiple_of(f * tile, tile), tile)
        rows = taken[0]
        gate_pre = dot_nn(rows, w_gate[0])
        up_pre = dot_nn(rows, w_up[0])
        sigmoid_gate = 1.0 / (1.0 + jnp.exp(-gate_pre))
        silu = gate_pre * sigmoid_gate
        active[0, :, at] = (silu * up_pre).astype(jnp.bfloat16)
        up_slope[0, :, at] = silu.astype(jnp.bfloat16)
        gate_slope[0, :, at] = (up_pre * (sigmoid_gate + silu * (1.0 - sigmoid_gate))).astype(
            jnp.bfloat16
        )

    @pl.when(f >= tiles)
    def _():
        at = pl.ds(pl.multiple_of((f - tiles) * wide_tile, wide_tile), wide_tile)
        made[e, :, at] = (dot_nn(active[0], w_down[0]) * weights[...]).astype(jnp.bfloat16)

    @pl.when((f == pl.num_programs(1) - 1) & (e == pl.num_programs(0) - 1))
    def _():
        combine(ranks, made, outs, count, slots)


def combine(ranks, made, outs, count, slots):
    for b in range(count):
        summed = None
        for k in range(made.shape[0]):
            match = slot_match(ranks[b, k], slots).astype(jnp.float32).astype(jnp.bfloat16)
            term = dot_tn(match, made[k, b * slots : (b + 1) * slots, :])
            summed = term if summed is None else summed + term
        outs[b][...] = summed.astype(jnp.bfloat16)


def experts_backward_kernel(*refs, count, slots, aliased, tiles):
    ranks, gates = refs[:2]
    blocks = refs[2 : 2 + count]
    w_gate, w_up, w_down, gate_slope, up_slope = refs[2 + count : 7 + count]
    refs = refs[7 + count + aliased :]
    taken, gate_grad, up_grad = refs[:3]
    outs = refs[3 : 3 + count]
    (made,) = refs[3 + count :]
    e, f = pl.program_id(0), pl.program_id(1)
    tile, wide_tile = w_down.shape[1], w_gate.shape[1]

    @pl.when(f == 0)
    def _():
        for b in range(count):
            match = slot_match(ranks[b, e], slots)
            weight = slot_gates(match, gates[b, e])
            taken[0, b * slots : (b + 1) * slots, :] = (
                dot_nn(match.astype(jnp.bfloat16), blocks[b][...]) * weight
            ).astype(jnp.bfloat16)

    @pl.when(f < tiles)
    def _():
        at = pl.ds(pl.multiple_of(f * tile, tile), tile)
        active_grad = dot_nt(taken[0], w_down[0])
        gate_grad[0, :, at] = (active_grad * gate_slope[0].astype(jnp.float32)).astype(jnp.bfloat16)
        up_grad[0, :, at] = (active_grad * up_slope[0].astype(jnp.float32)).astype(jnp.bfloat16)

    @pl.when(f >= tiles)
    def _():
        at = pl.ds(pl.multiple_of((f - tiles) * wide_tile, wide_tile), wide_tile)
        made[e, :, at] = (dot_nt(gate_grad[0], w_gate[0]) + dot_nt(up_grad[0], w_up[0])).astype(
            jnp.bfloat16
        )

    @pl.when((f == pl.num_programs(1) - 1) & (e == pl.num_programs(0) - 1))
    def _():
        combine(ranks, made, outs, count, slots)


def experts_stage(
    forward, ranks, gates, blocks, weights, slopes, held, place, slots, all_slots, light=False
):
    count = len(blocks)
    rows, width = blocks[0].shape
    experts, _, hidden_units = weights[0].shape
    tile, wide_tile = min(512, hidden_units), min(1024, width)
    tiles, wide_tiles = hidden_units // tile, width // wide_tile
    part = count * slots

    def first(f):
        return jnp.minimum(f, tiles - 1)

    def later(f):
        return jnp.maximum(f - tiles, 0)

    info = pl.BlockSpec((count, experts, 1, rows), lambda e, f: (0, 0, 0, 0))
    block = pl.BlockSpec((rows, width), lambda e, f: (0, 0))
    wide = pl.BlockSpec((1, part, width), lambda e, f: (e, place, 0))
    narrow = pl.BlockSpec((1, part, hidden_units), lambda e, f: (e, place, 0))
    slope = pl.BlockSpec((1, part, tile), lambda e, f: (e, 0, first(f)))
    own = pl.BlockSpec((1, part, hidden_units), lambda e, f: (e, 0, 0))
    if forward:
        kernel, name = experts_forward_kernel, "experts_forward"
        into = pl.BlockSpec((1, width, tile), lambda e, f: (e, 0, first(f)))
        back = pl.BlockSpec((1, hidden_units, wide_tile), lambda e, f: (e, 0, later(f)))
        narrow_outs, own_outs, scratch = 1, 2, [pltpu.VMEM((part, 1), jnp.float32)]
    else:
        kernel, name = experts_backward_kernel, "experts_backward"
        into = pl.BlockSpec((1, wide_tile, hidden_units), lambda e, f: (e, later(f), 0))
        back = pl.BlockSpec((1, tile, width), lambda e, f: (e, first(f), 0))
        narrow_outs, own_outs, scratch = 2, 0, []
    held = () if held is None else tuple(held)
    before = 2 + count + 3 + len(slopes)
    scale = 0 if light else 1
    flops = 2 * experts * part * width * (3 * hidden_units + 2 * rows)
    return pl.pallas_call(
        partial(kernel, count=count, slots=slots, aliased=len(held), tiles=tiles),
        grid=(experts, tiles + wide_tiles),
        in_specs=[info, info]
        + [block] * count
        + [into, into, back]
        + [slope] * len(slopes)
        + [pl.BlockSpec(memory_space=pl.ANY)] * len(held),
        out_specs=[wide] + [narrow] * narrow_outs + [own] * own_outs + [block] * count,
        out_shape=[jax.ShapeDtypeStruct((experts, all_slots, width), jnp.bfloat16)]
        + [jax.ShapeDtypeStruct((experts, all_slots, hidden_units), jnp.bfloat16)] * narrow_outs
        + [jax.ShapeDtypeStruct((experts, part, hidden_units), jnp.bfloat16)] * own_outs
        + [jax.ShapeDtypeStruct((rows, width), jnp.bfloat16)] * count,
        scratch_shapes=[pltpu.VMEM((experts, part, width), jnp.bfloat16)] + scratch,
        input_output_aliases={before + k: k for k in range(len(held))},
        compiler_params=pltpu.CompilerParams(vmem_limit_bytes=VMEM_BYTES),
        cost_estimate=pl.CostEstimate(
            flops=scale * flops,
            bytes_accessed=scale
            * 2
            * (3 * experts * width * hidden_units + 4 * count * rows * width),
            transcendentals=scale * experts * part * hidden_units,
        ),
        name=name,
    )(ranks, gates, *blocks, *weights, *slopes, *held)


def ring_of(contexts):
    order = list(range(0, contexts, 2)) + list(range(contexts - 1, 0, -2))
    place_of = [order.index(c) for c in range(contexts)]
    up = [(order[p], order[(p + 1) % contexts]) for p in range(contexts)]
    down = [(b, a) for a, b in up]
    return order, place_of, up, down


class RingGather:
    def __init__(self, own, ring):
        _, _, self.up, self.down = ring
        self.half = len(self.up) // 2
        self.step = 0
        self.blocks = {0: own}
        self.from_before = self.from_after = own

    def advance(self, *earlier):
        self.step += 1
        before, past = self.from_before, self.from_after
        if earlier:
            before, past = lax.optimization_barrier((before, past) + earlier)[:2]
        if self.step < self.half:
            self.from_before = lax.ppermute(before, "ctx", self.up)
            self.from_after = lax.ppermute(past, "ctx", self.down)
            self.blocks[-self.step] = self.from_before
            self.blocks[self.step] = self.from_after
            return (-self.step, self.step)
        cut = before.shape[0] // 2
        first = lax.ppermute(before[:cut], "ctx", self.up)
        second = lax.ppermute(past[cut:], "ctx", self.down)
        self.blocks[self.half] = jnp.concatenate([first, second], axis=0)
        return (self.half,)


def add_low(left, right):
    return (left.astype(jnp.float32) + right.astype(jnp.float32)).astype(jnp.bfloat16)


class RingScatter:
    def __init__(self, ring):
        _, _, self.up, self.down = ring
        self.half = len(self.up) // 2
        self.step = self.half

    def prepare(self, terms, *earlier):
        if self.step == self.half:
            far = after(terms[self.half], *earlier)
            cut = far.shape[0] // 2
            before, past = far[:cut], far[cut:]
        else:
            before, past = terms[-self.step], terms[self.step]
            got_before, got_past = self.to_before, self.to_after
            if earlier:
                before, past = lax.optimization_barrier((before, past) + earlier)[:2]
            cut = got_before.shape[0]
            if cut < before.shape[0]:
                before = jnp.concatenate([add_low(got_before, before[:cut]), before[cut:]], axis=0)
                past = jnp.concatenate([past[:cut], add_low(got_past, past[cut:])], axis=0)
            else:
                before, past = add_low(got_before, before), add_low(got_past, past)
        self.payload = (before, past)
        return self.payload

    def send(self, *earlier):
        before, past = self.payload
        if earlier:
            before, past = lax.optimization_barrier((before, past) + earlier)[:2]
        self.to_before = lax.ppermute(before, "ctx", self.down)
        self.to_after = lax.ppermute(past, "ctx", self.up)
        self.step -= 1
        return self.payload

    def advance(self, terms, *earlier):
        self.prepare(terms, *earlier)
        return self.send()

    def finish(self, own):
        return (
            own.astype(jnp.float32)
            + self.to_before.astype(jnp.float32)
            + self.to_after.astype(jnp.float32)
        )


def sum_over_ctx(values, contexts):
    bit = 1
    while bit < contexts:
        values = values + lax.ppermute(values, "ctx", [(c, c ^ bit) for c in range(contexts)])
        bit *= 2
    return values


def after(value, *earlier):
    return lax.optimization_barrier((value,) + earlier)[0]


def shards_by_heads(
    tokens,
    cotangent,
    cont_lengths,
    routes,
    gates,
    attn_gain,
    query_gain,
    key_gain,
    ffn_gain,
    w_query,
    w_key,
    w_value,
    w_out,
    w_gate,
    w_up,
    w_down,
):
    both = ("ctx", "fsdp")
    contexts, splits = lax.axis_size("ctx"), lax.axis_size("fsdp")
    rows, width = tokens.shape[1:]
    route_count = routes.shape[2]
    total = rows * contexts
    prompt_rows = total // 2
    columns = width // contexts
    size = min(512, prompt_rows)
    local_experts = w_gate.shape[0]
    expert_total = local_experts * contexts
    slots = max(2, rows * route_count * 5 // (4 * expert_total))
    all_slots = contexts * slots
    score_scale = HEAD ** (-0.5)
    me = lax.axis_index("ctx")
    ring = ring_of(contexts)
    half = contexts // 2
    place = jnp.where(me % 2 == 0, me // 2, contexts - 1 - me // 2)

    def owner(offset):
        at = (place + offset) % contexts
        return jnp.where(at < half, 2 * at, 2 * (contexts - 1 - at) + 1)

    others = [k for step in range(1, half) for k in (-step, step)] + [half]

    own_rows = w_out.shape[0]
    token_ring = RingGather(jnp.concatenate([tokens[0], w_out], axis=0), ring)

    chosen = routes[0].T[None] == jnp.arange(expert_total, dtype=jnp.int32)[:, None, None]
    member = jnp.any(chosen, axis=1)
    gate_rows = jnp.sum(jnp.where(chosen, gates[0].T[None], 0.0), axis=1)
    earlier = jnp.tril(jnp.ones((rows, rows), jnp.bfloat16), -1)
    rank = jnp.einsum(
        "et,ut->eu", member.astype(jnp.bfloat16), earlier, preferred_element_type=jnp.float32
    )
    rank = jnp.where(member, rank, -1.0)
    rank_high = jnp.floor(rank / 16.0)
    gate_high = gate_rows.astype(jnp.bfloat16).astype(jnp.float32)
    routing = jnp.stack([rank_high, rank - 16.0 * rank_high, gate_high, gate_rows - gate_high])
    routing = routing.astype(jnp.bfloat16).reshape(4, contexts, local_experts * rows)
    routing = jnp.transpose(routing, (1, 0, 2)).reshape(contexts, own_rows, -1)
    routing_columns = routing.shape[2]

    cut = jnp.stack([w_query, w_key, w_value]).reshape(3, own_rows, contexts, columns)
    cut = jnp.transpose(cut, (2, 1, 0, 3)).reshape(contexts, own_rows, 3 * columns)
    own_gains = jnp.stack([attn_gain, query_gain, key_gain, ffn_gain], axis=1)
    cut = jnp.concatenate(
        [cut, jnp.broadcast_to(own_gains, (contexts,) + own_gains.shape), routing], axis=2
    )
    spare = -cut.shape[2] % 128
    cut = jnp.pad(cut, ((0, 0), (0, 0), (0, spare)))
    pieces = []
    for step in range(contexts):
        piece = lax.dynamic_index_in_dim(cut, (me - step) % contexts, 0, keepdims=False)
        if step:
            pairs = [(c, (c - step) % contexts) for c in range(contexts)]
            piece = lax.ppermute(piece, "ctx", pairs)
        pieces.append(piece)
    first_piece = pieces[1]
    pieces = gather_pieces(me, pieces)
    token_ring.advance(first_piece)
    gate_all = lax.all_gather(after(w_gate, pieces), "fsdp", axis=1, tiled=True)
    w_all = lax.all_gather(pieces, "fsdp", axis=1, tiled=True).reshape(width, -1)
    up_all = lax.all_gather(w_up, "fsdp", axis=1, tiled=True)
    for _ in range(2, half):
        token_ring.advance()
    w_t = w_all[:, : 3 * columns].T
    all_gains = w_all[:, 3 * columns : 3 * columns + 4].astype(jnp.float32).T
    gain_attn, gain_ffn = all_gains[0], all_gains[3]
    gain_query = lax.dynamic_slice_in_dim(all_gains[1], me * columns, columns)[:, None]
    gain_key = lax.dynamic_slice_in_dim(all_gains[2], me * columns, columns)[:, None]

    owners = owner(jnp.arange(contexts, dtype=jnp.int32))
    routing = pieces[:, :, 3 * columns + 4 : 3 * columns + 4 + routing_columns]
    routing = routing.reshape(contexts, 4, local_experts, 1, rows)[owners].astype(jnp.float32)
    all_ranks = (16.0 * routing[:, 0] + routing[:, 1]).astype(jnp.int32)
    all_gates = routing[:, 2] + routing[:, 3]

    lengths_in = cont_lengths[0]
    token_index = jnp.arange(total, dtype=jnp.int32)
    _, position = places(token_index, lengths_in, prompt_rows)
    starts = prompt_rows + jnp.cumsum(lengths_in) - lengths_in
    frequency = ROPE_BASE ** (-jnp.arange(HEAD // 2).astype(jnp.float32) / (HEAD // 2))
    angles = frequency[:, None] * position.astype(jnp.float32)[None, :]
    cosine, sine = jnp.cos(angles), jnp.sin(angles)

    def project_all(offsets, made):
        blocks = [token_ring.blocks[offset] for offset in offsets]
        places_of = owner(jnp.asarray(offsets, jnp.int32))
        return project(places_of, blocks, rows, w_t, gain_attn[None], made, total)

    made = project_all([0] + others[: 2 * (half - 2)], None)
    token_ring.advance(made[-1], up_all, gate_all)
    made = project_all(others[2 * (half - 2) : -1], made)
    token_ring.blocks[half] = after(token_ring.blocks[half], made[-1])
    made = project_all(others[-1:], made)
    hidden_all, query_pre, key_pre, value_t, squares = made
    w_out_rows = place_rows(
        owners, [token_ring.blocks[k if k <= half else k - contexts] for k in range(contexts)], rows, own_rows
    )
    out_all = lax.all_gather(w_out_rows, "fsdp", axis=1, tiled=True).reshape(width, width)
    down_all = lax.all_gather(w_down, "fsdp", axis=1, tiled=True)

    squares = sum_over_ctx(squares, contexts)
    inverse = lax.rsqrt(squares / width + EPSILON)
    query_inv, key_inv = inverse[0:1], inverse[1:2]
    grad_ring = RingGather(cotangent[0], ring)
    grad_ring.advance(squares)

    attended, query, key, key_t, log_rows = attend_forward(
        starts, query_pre, key_pre, value_t, query_inv, key_inv, gain_query, gain_key, cosine, sine, size, prompt_rows, score_scale
    )
    sent = after(attended, grad_ring.from_before, grad_ring.from_after)
    back = lax.all_to_all(
        sent.reshape(contexts, rows, columns), "ctx", split_axis=0, concat_axis=0, tiled=True
    )
    grad_ring.advance(attended)
    own_attended = jnp.transpose(back, (1, 0, 2)).reshape(rows, width)
    inputs = tokens[0].astype(jnp.float32)
    mixed = inputs + jnp.dot(own_attended, out_all, preferred_element_type=jnp.float32)
    mixed_inv = lax.rsqrt(jnp.mean(mixed * mixed, axis=-1, keepdims=True) + EPSILON)
    second = (mixed * mixed_inv * gain_ffn).astype(jnp.bfloat16)

    second_ring = RingGather(second, ring)
    weights = (gate_all, up_all, down_all)

    def stage_info(offsets):
        ranks = jnp.stack([all_ranks[k] for k in offsets])
        stage_gates = jnp.stack([all_gates[k] for k in offsets])
        if len(offsets) == 2:
            return ranks, stage_gates, offsets[1] - 1
        return ranks, stage_gates, contexts - (2 if offsets[0] == 0 else 1)

    stages = [(0,)] + [(-step, step) for step in range(1, half)] + [(half,)]
    infos = [stage_info(stage) for stage in stages]
    result_terms, second_terms, slopes = {}, {}, {}
    kept = kept_grads = None

    def forward(step, *earlier):
        nonlocal kept
        ranks, stage_gates, at = infos[step]
        ranks = after(ranks, *earlier) if earlier else ranks
        blocks = [second_ring.blocks[k] for k in stages[step]]
        made = experts_stage(
            True, ranks, stage_gates, blocks, weights, (), kept, at, slots, all_slots
        )
        kept, slopes[step], terms = made[:2], made[2:4], made[4:]
        result_terms.update(zip(stages[step], terms))
        return terms[0]

    def backward(step, *earlier, light=False):
        nonlocal kept_grads
        ranks, stage_gates, at = infos[step]
        ranks = after(ranks, *earlier) if earlier else ranks
        blocks = [grad_ring.blocks[k] for k in stages[step]]
        made = experts_stage(
            False,
            ranks,
            stage_gates,
            blocks,
            weights,
            slopes[step],
            kept_grads,
            at,
            slots,
            all_slots,
            light,
        )
        kept_grads, terms = made[:3], made[3:]
        second_terms.update(zip(stages[step], terms))
        return terms[0]

    def weight_grad(left, right):
        return jnp.einsum("emd,emf->edf", left, right, preferred_element_type=jnp.float32).astype(
            jnp.bfloat16
        )

    second_ring.advance()
    grad_second = (grad_ring.from_before, grad_ring.from_after)
    done = forward(0)
    done = backward(0, done, *grad_second, light=True)
    for step in range(1, half):
        near = [second_ring.blocks[k] for k in stages[step]]
        second_ring.advance(done)
        waits = (done,)
        if step > 1:
            waits += (grad_ring.from_before, grad_ring.from_after)
        if step in (1, half - 1):
            grad_ring.advance(done, *near)
        done = forward(step, *waits)
        if step < half - 2:
            done = backward(step, done, light=True)
    done = forward(half, done)

    second_sum, result_sum = RingScatter(ring), RingScatter(ring)
    result_sum.advance(result_terms)
    backward(half, done)
    sent = second_sum.advance(second_terms, result_sum.to_before, result_sum.to_after)
    backward(half - 1, *sent)
    sent = second_sum.advance(second_terms)
    backward(half - 2, *sent)
    sent = second_sum.advance(second_terms)
    rows_taken, active = kept
    route_grad, gate_grad, up_grad = kept_grads
    gate_product = weight_grad(after(rows_taken, *sent), gate_grad)
    sent = second_sum.advance(second_terms, gate_product[0, :8, :128])
    result_sum.prepare(result_terms, *sent)
    up_product = weight_grad(after(rows_taken, *result_sum.payload), up_grad)
    second_grad = second_sum.finish(after(second_terms[0], up_product[0, :8, :128]))

    def fsdp_sum_low(product):
        return lax.psum_scatter(product, "fsdp", scatter_dimension=1, tiled=True)

    gate_w_grad = fsdp_sum_low(after(gate_product, second_grad))
    up_w_grad = fsdp_sum_low(after(up_product, second_grad))

    upstream = cotangent[0].astype(jnp.float32)
    mixed_normed = mixed * mixed_inv
    ffn_gain_grad = jnp.sum(second_grad * mixed_normed, axis=0)
    scaled = second_grad * gain_ffn
    mixed_grad = upstream + mixed_inv * (
        scaled - mixed_normed * jnp.mean(scaled * mixed_normed, axis=-1, keepdims=True)
    )
    branch = mixed_grad.astype(jnp.bfloat16)
    out_grad = out_grad_of(branch, out_all, contexts)
    w_out_grad = lax.dot_general(
        own_attended, after(branch, out_grad), (((0,), (0,)), ((), ())), preferred_element_type=jnp.float32
    ).astype(jnp.bfloat16)
    down_product = weight_grad(after(active, out_grad), route_grad)
    out_grad = lax.all_to_all(out_grad, "ctx", split_axis=0, concat_axis=0, tiled=True)
    out_grad = out_grad.reshape(total, columns)
    w_out_grad = fsdp_sum_low(
        after(w_out_grad, out_grad).reshape(contexts, splits * own_rows, width)
    )
    down_w_grad = fsdp_sum_low(after(down_product, out_grad))

    log_rows = log_rows.reshape(columns // HEAD, 1, total)
    held, dots, waits = None, 0.0, (out_grad, down_product[0, :8, :128])
    for head in range(columns // HEAD):
        if head == 1:
            result_sum.prepare(result_terms, dots)
            waits = result_sum.payload + (gate_w_grad,)
        if head < 2:
            result_sum.send(out_grad)
        *held, part = attend_backward(
            after(starts, *waits), head, held, query, key, key_t, value_t, out_grad, attended, log_rows, query_pre, key_pre, query_inv, key_inv, gain_query, gain_key, cosine, sine, size, prompt_rows, score_scale
        )
        dots = dots + part
    query_scaled, key_scaled, value_grad, query_gain_grad, key_gain_grad = held
    dots = after(dots, up_w_grad, result_sum.to_before, result_sum.to_after)
    result_sum.prepare(result_terms, dots)
    dots = sum_over_ctx(dots, contexts) / width
    dots = after(dots, *result_sum.payload)
    heads_grad = heads_grad_of(
        query_scaled, key_scaled, value_grad, query_pre, key_pre, inverse, dots
    )

    def own_columns(grad):
        return lax.dynamic_update_slice_in_dim(
            jnp.zeros((width, 1), jnp.float32), grad, me * columns, 0
        )

    other_grads = jnp.concatenate(
        [
            ffn_gain_grad[:, None],
            own_columns(query_gain_grad),
            own_columns(key_gain_grad),
            jnp.zeros((width, 125), jnp.float32),
        ],
        axis=1,
    )
    def term(offset, *earlier, **got):
        at = after(owner(offset)[None], *earlier)
        return hidden_term(at, heads_grad, w_t, w_out_grad, rows, **got)

    result_sum.send(dots)
    hidden_sum = RingScatter(ring)
    hidden_sum.payload = far = term(half)
    hidden_sum.send()
    heads_product = heads_product_of(
        heads_grad, hidden_all, after(other_grads, *far), contexts
    )
    heads_w_grad = fsdp_sum_low(after(heads_product, hidden_sum.to_before, hidden_sum.to_after))
    done = (result_sum.to_before, result_sum.to_after)
    for step in range(half - 1, 0, -1):
        start = far[0].shape[0] if step == half - 1 else 0
        if step == half - 2:
            done = (heads_product,)
        if step == 1:
            done = (down_w_grad,)
        hidden_sum.payload = (
            term(-step, *done, got=hidden_sum.to_before),
            term(step, *done, got=hidden_sum.to_after, start=start),
        )
        hidden_sum.send()
        done = ()
    hidden_grad, w_out_grad = own_term(
        owner(0)[None], heads_grad, w_t, w_out_grad, rows, hidden_sum.to_before, hidden_sum.to_after
    )
    routed = result_sum.finish(result_terms[0])
    output = (mixed + routed)[None]

    heads_w_grad = lax.all_to_all(
        heads_w_grad, "ctx", split_axis=0, concat_axis=0, tiled=True
    ).astype(jnp.float32)
    other_grads = jnp.sum(heads_w_grad[:, :, 3 * columns : 3 * columns + 3], axis=0)
    heads_w_grad = jnp.transpose(
        heads_w_grad[:, :, : 3 * columns].reshape(contexts, own_rows, 3, columns), (2, 1, 0, 3)
    ).reshape(3, own_rows, width)

    attn_gain_grad = jnp.sum(
        w_query.astype(jnp.float32) * heads_w_grad[0]
        + w_key.astype(jnp.float32) * heads_w_grad[1]
        + w_value.astype(jnp.float32) * heads_w_grad[2],
        axis=1,
    ) / attn_gain.astype(jnp.float32)

    attn_inv = lax.rsqrt(jnp.mean(inputs * inputs, axis=-1, keepdims=True) + EPSILON)
    normed = inputs * attn_inv
    scaled = hidden_grad * gain_attn
    input_grad = mixed_grad + attn_inv * (
        scaled - normed * jnp.mean(scaled * normed, axis=-1, keepdims=True)
    )
    return (
        output,
        input_grad[None],
        attn_gain_grad,
        other_grads[:, 1],
        other_grads[:, 2],
        other_grads[:, 0],
        heads_w_grad[0],
        heads_w_grad[1],
        heads_w_grad[2],
        w_out_grad,
        gate_w_grad.astype(jnp.float32),
        up_w_grad.astype(jnp.float32),
        down_w_grad.astype(jnp.float32),
    )


def solution(mesh):
    contexts = mesh.shape["ctx"]
    fits = contexts == 8
    placed = (
        P("fsdp", "ctx", None),
        P("fsdp", "ctx", None),
        P("fsdp", None),
        P("fsdp", "ctx", None),
        P("fsdp", "ctx", None),
        P(("ctx", "fsdp")),
        P(("ctx", "fsdp")),
        P(("ctx", "fsdp")),
        P(("ctx", "fsdp")),
        P(("ctx", "fsdp"), None),
        P(("ctx", "fsdp"), None),
        P(("ctx", "fsdp"), None),
        P(("ctx", "fsdp"), None),
        P("ctx", "fsdp", None),
        P("ctx", "fsdp", None),
        P("ctx", "fsdp", None),
    )
    return jax.shard_map(
        shards_by_heads if fits else shards_wide,
        mesh=mesh,
        in_specs=placed,
        out_specs=(
            P("fsdp", "ctx", None),
            P("fsdp", "ctx", None),
            P(("ctx", "fsdp")),
            P(("ctx", "fsdp")),
            P(("ctx", "fsdp")),
            P(("ctx", "fsdp")),
            P(("ctx", "fsdp"), None),
            P(("ctx", "fsdp"), None),
            P(("ctx", "fsdp"), None),
            P(("ctx", "fsdp"), None),
            P("ctx", "fsdp", None),
            P("ctx", "fsdp", None),
            P("ctx", "fsdp", None),
        ),
        check_vma=False,
    )
```

```python
from functools import partial

import jax
import jax.numpy as jnp
from jax import lax
from jax.experimental import pallas as pl
from jax.experimental.pallas import tpu as pltpu
from jax.sharding import PartitionSpec as P

HEAD = 128


EPSILON = 1e-05
ROPE_BASE = 10000.0
MASKED = -1e30


def norm_rows(values_in, gain_in):
    return (
        values_in
        * lax.rsqrt(jnp.mean(values_in * values_in, axis=-1, keepdims=True) + EPSILON)
        * gain_in
    )


def places(token_index, lengths_in, prompt_rows):
    ends = prompt_rows + jnp.cumsum(lengths_in)
    passed = (token_index[:, None] >= ends[None, :]).astype(jnp.int32)
    before = jnp.sum(passed * lengths_in[None, :], axis=1)
    inside = token_index >= prompt_rows
    segment = jnp.where(inside, 1 + jnp.sum(passed, axis=1), 0)
    position = jnp.where(inside, token_index - before, token_index)
    return (segment, position)


def rotate(values_in, positions):
    full_shape = values_in.shape
    per_head = values_in.reshape(full_shape[:-1] + (full_shape[-1] // HEAD, HEAD))
    half_dim = HEAD // 2
    frequency = ROPE_BASE ** (-jnp.arange(half_dim).astype(values_in.dtype) / half_dim)
    angles = positions.astype(values_in.dtype)[..., None] * frequency
    cosine = jnp.cos(angles)[..., None, :]
    sine = jnp.sin(angles)[..., None, :]
    former = per_head[..., :half_dim]
    latter = per_head[..., half_dim:]
    turned = jnp.concatenate(
        [former * cosine - latter * sine, latter * cosine + former * sine], axis=-1
    )
    return turned.reshape(full_shape)


def allowed_pairs(query_index, query_seg, key_index, key_seg):
    return (key_index[None, :] <= query_index[:, None]) & (
        (key_seg[None, :] == 0) | (key_seg[None, :] == query_seg[:, None])
    )


def attend_fold(
    state_in,
    shard_piece,
    first_row,
    query_heads,
    own_index,
    own_seg,
    lengths_in,
    prompt_rows,
    score_scale,
):
    highest, denominator, weighted = state_in
    key_rows, value_rows = shard_piece
    piece_count = key_rows.shape[0]
    key_index = jnp.arange(piece_count, dtype=jnp.int32)
    key_seg, _ = places(key_index, lengths_in, prompt_rows)
    key_heads = key_rows.reshape(piece_count, -1, HEAD)
    value_heads = value_rows.reshape(piece_count, -1, HEAD)
    scores = (
        jnp.einsum("qhd,khd->hqk", query_heads, key_heads, preferred_element_type=jnp.float32)
        * score_scale
    )
    allowed = allowed_pairs(own_index, own_seg, key_index, key_seg)
    masked = jnp.where(allowed[None], scores, MASKED)
    new_high = jnp.maximum(highest, jnp.max(masked, axis=-1))
    shrink = jnp.exp(highest - new_high)
    unnormed = jnp.where(allowed[None], jnp.exp(masked - new_high[..., None]), 0.0)
    denominator = jnp.sum(unnormed, axis=-1)
    weighted = jnp.einsum(
        "hqk,khd->hqd",
        unnormed.astype(jnp.bfloat16),
        value_heads,
        preferred_element_type=jnp.float32,
    )
    return (new_high, denominator, weighted)


def pair_terms(
    query_heads,
    grad_heads,
    log_rows,
    dot_rows,
    query_index,
    query_seg,
    key_heads,
    value_heads,
    key_index,
    key_seg,
    score_scale,
):
    scores = (
        jnp.einsum("qhd,khd->hqk", query_heads, key_heads, preferred_element_type=jnp.float32)
        * score_scale
    )
    allowed = allowed_pairs(query_index, query_seg, key_index, key_seg)
    prob = jnp.where(
        allowed[None], jnp.exp(jnp.where(allowed[None], scores, MASKED) - log_rows[..., None]), 0.0
    )
    prob_grad = jnp.einsum(
        "qhd,khd->hqk", grad_heads, value_heads, preferred_element_type=jnp.float32
    )
    score_grad = (prob * (prob_grad - dot_rows[..., None])).astype(jnp.bfloat16)
    return (prob, score_grad)


def slot_targets(route_list, expert_total, capacity):
    onehot = (route_list[:, None] == jnp.arange(expert_total, dtype=jnp.int32)[None, :]).astype(
        jnp.int32
    )
    slot_rank = jnp.sum((jnp.cumsum(onehot, axis=0) - 1) * onehot, axis=1)
    return route_list * capacity + slot_rank


def shards_wide(
    tokens,
    cotangent,
    cont_lengths,
    routes,
    gates,
    attn_gain,
    query_gain,
    key_gain,
    ffn_gain,
    w_query,
    w_key,
    w_value,
    w_out,
    w_gate,
    w_up,
    w_down,
):
    row_count = tokens.shape[1]
    model_width = tokens.shape[2]
    route_count = routes.shape[2]
    context_size = lax.axis_size("ctx")
    all_rows = row_count * context_size
    prompt_rows = all_rows // 2
    local_experts = w_gate.shape[0]
    expert_total = local_experts * context_size
    capacity = max(2, row_count * route_count * 5 // (4 * expert_total))
    head_count = model_width // HEAD
    score_scale = HEAD ** (-0.5)
    lengths_in = cont_lengths[0]
    own_index = lax.axis_index("ctx") * row_count + jnp.arange(row_count, dtype=jnp.int32)
    own_seg, own_pos = places(own_index, lengths_in, prompt_rows)
    attention_set = (
        lax.all_gather(w_query, ("ctx", "fsdp"), axis=0, tiled=True),
        lax.all_gather(w_key, ("ctx", "fsdp"), axis=0, tiled=True),
        lax.all_gather(w_value, ("ctx", "fsdp"), axis=0, tiled=True),
        lax.all_gather(w_out, ("ctx", "fsdp"), axis=0, tiled=True),
        lax.all_gather(attn_gain, ("ctx", "fsdp"), axis=0, tiled=True),
        lax.all_gather(query_gain, ("ctx", "fsdp"), axis=0, tiled=True),
        lax.all_gather(key_gain, ("ctx", "fsdp"), axis=0, tiled=True),
        lax.all_gather(ffn_gain, ("ctx", "fsdp"), axis=0, tiled=True),
    )
    query_all, key_all, value_all, out_all = (
        attention_set[0],
        attention_set[1],
        attention_set[2],
        attention_set[3],
    )
    gain_attn = attention_set[4].astype(jnp.float32)
    gain_query = attention_set[5].astype(jnp.float32)
    gain_key = attention_set[6].astype(jnp.float32)
    gain_ffn = attention_set[7].astype(jnp.float32)
    expert_set = (
        lax.all_gather(w_gate, "fsdp", axis=1, tiled=True),
        lax.all_gather(w_up, "fsdp", axis=1, tiled=True),
        lax.all_gather(w_down, "fsdp", axis=1, tiled=True),
    )
    gate_all, up_all, down_all = expert_set
    inputs = tokens[0].astype(jnp.float32)
    normed, attn_pull = jax.vjp(norm_rows, inputs, gain_attn)
    hidden = normed.astype(jnp.bfloat16)
    query_pre = jnp.dot(hidden, query_all, preferred_element_type=jnp.float32)
    key_pre = jnp.dot(hidden, key_all, preferred_element_type=jnp.float32)
    values = jnp.dot(hidden, value_all, preferred_element_type=jnp.float32).astype(jnp.bfloat16)
    query_rot, query_pull = jax.vjp(
        lambda pre_in, gain_in: rotate(norm_rows(pre_in, gain_in), own_pos), query_pre, gain_query
    )
    key_rot, key_pull = jax.vjp(
        lambda pre_in, gain_in: rotate(norm_rows(pre_in, gain_in), own_pos), key_pre, gain_key
    )
    query_low = query_rot.astype(jnp.bfloat16)
    key_low = key_rot.astype(jnp.bfloat16)
    query_heads = query_low.reshape(row_count, head_count, HEAD)
    folder = partial(
        attend_fold,
        query_heads=query_heads,
        own_index=own_index,
        own_seg=own_seg,
        lengths_in=lengths_in,
        prompt_rows=prompt_rows,
        score_scale=score_scale,
    )
    start_state = (
        jnp.full((head_count, row_count), MASKED, jnp.float32),
        jnp.zeros((head_count, row_count), jnp.float32),
        jnp.zeros((head_count, row_count, HEAD), jnp.float32),
    )
    final_state = folder(
        start_state,
        (
            lax.all_gather(key_low, "ctx", axis=0, tiled=True),
            lax.all_gather(values, "ctx", axis=0, tiled=True),
        ),
        jnp.int32(0),
    )
    highest, denominator, weighted = final_state
    log_total = highest + jnp.log(denominator)
    attn_heads = jnp.transpose(weighted / denominator[..., None], (1, 0, 2))
    attended = attn_heads.reshape(row_count, model_width).astype(jnp.bfloat16)
    mixed = inputs + jnp.dot(attended, out_all, preferred_element_type=jnp.float32)
    normed_second, ffn_pull = jax.vjp(norm_rows, mixed, gain_ffn)
    second = normed_second.astype(jnp.bfloat16)
    route_list = routes[0].reshape(-1)
    targets = slot_targets(route_list, expert_total, capacity)

    def dispatch_rows(route_rows):
        buffer = (
            jnp.zeros((expert_total * capacity, model_width), jnp.bfloat16)
            .at[targets]
            .set(route_rows)
        )
        return buffer.reshape(context_size, local_experts * capacity, model_width)

    sent_rows = dispatch_rows(jnp.repeat(second, route_count, axis=0))
    arrived = lax.all_to_all(sent_rows, "ctx", split_axis=0, concat_axis=0, tiled=True).reshape(
        context_size, local_experts, capacity, model_width
    )
    gate_pre = jnp.einsum("sekd,edf->sekf", arrived, gate_all, preferred_element_type=jnp.float32)
    up_pre = jnp.einsum("sekd,edf->sekf", arrived, up_all, preferred_element_type=jnp.float32)
    active = (jax.nn.silu(gate_pre) * up_pre).astype(jnp.bfloat16)
    expert_out = jnp.einsum(
        "sekf,efd->sekd", active, down_all, preferred_element_type=jnp.float32
    ).astype(jnp.bfloat16)
    returned = lax.all_to_all(
        expert_out.reshape(context_size, local_experts * capacity, model_width),
        "ctx",
        split_axis=0,
        concat_axis=0,
        tiled=True,
    )
    per_route = (
        returned.reshape(expert_total * capacity, model_width)[targets]
        .astype(jnp.float32)
        .reshape(row_count, route_count, model_width)
    )
    gate_values = gates[0]
    result = mixed + jnp.sum(gate_values[..., None] * per_route, axis=1)
    output = result[None]
    upstream = cotangent[0].astype(jnp.float32)
    route_grad = (
        (gate_values[..., None] * upstream[:, None, :])
        .astype(jnp.bfloat16)
        .reshape(row_count * route_count, model_width)
    )
    grad_arrived = lax.all_to_all(
        dispatch_rows(route_grad), "ctx", split_axis=0, concat_axis=0, tiled=True
    ).reshape(context_size, local_experts, capacity, model_width)
    active_grad = jnp.einsum(
        "sekd,efd->sekf", grad_arrived, down_all, preferred_element_type=jnp.float32
    )
    down_w_grad = jnp.einsum(
        "sekf,sekd->efd", active, grad_arrived, preferred_element_type=jnp.float32
    )
    sigmoid_gate = jax.nn.sigmoid(gate_pre)
    gate_grad = (
        active_grad * up_pre * sigmoid_gate * (1.0 + gate_pre * (1.0 - sigmoid_gate))
    ).astype(jnp.bfloat16)
    up_grad = (active_grad * gate_pre * sigmoid_gate).astype(jnp.bfloat16)
    gate_w_grad = jnp.einsum(
        "sekd,sekf->edf", arrived, gate_grad, preferred_element_type=jnp.float32
    )
    up_w_grad = jnp.einsum("sekd,sekf->edf", arrived, up_grad, preferred_element_type=jnp.float32)
    arrived_grad = jnp.einsum(
        "sekf,edf->sekd", gate_grad, gate_all, preferred_element_type=jnp.float32
    )
    arrived_grad = (
        arrived_grad
        + jnp.einsum("sekf,edf->sekd", up_grad, up_all, preferred_element_type=jnp.float32)
    ).astype(jnp.bfloat16)
    grad_back = lax.all_to_all(
        arrived_grad.reshape(context_size, local_experts * capacity, model_width),
        "ctx",
        split_axis=0,
        concat_axis=0,
        tiled=True,
    )
    second_grad = jnp.sum(
        grad_back.reshape(expert_total * capacity, model_width)[targets]
        .astype(jnp.float32)
        .reshape(row_count, route_count, model_width),
        axis=1,
    )
    expert_grads = (
        lax.psum_scatter(
            gate_w_grad.astype(jnp.bfloat16), "fsdp", scatter_dimension=1, tiled=True
        ).astype(jnp.float32),
        lax.psum_scatter(
            up_w_grad.astype(jnp.bfloat16), "fsdp", scatter_dimension=1, tiled=True
        ).astype(jnp.float32),
        lax.psum_scatter(
            down_w_grad.astype(jnp.bfloat16), "fsdp", scatter_dimension=1, tiled=True
        ).astype(jnp.float32),
    )
    mixed_norm_grad, ffn_gain_grad = ffn_pull(second_grad)
    mixed_grad = upstream + mixed_norm_grad
    branch_grad = mixed_grad.astype(jnp.bfloat16)
    out_w_grad = jnp.dot(attended.T, branch_grad, preferred_element_type=jnp.float32)
    attended_grad = jnp.dot(branch_grad, out_all.T, preferred_element_type=jnp.float32).astype(
        jnp.bfloat16
    )
    grad_heads = attended_grad.reshape(row_count, head_count, HEAD)
    row_dot = jnp.transpose(jnp.sum(grad_heads.astype(jnp.float32) * attn_heads, axis=-1))
    keys_whole, values_whole = (
        lax.all_gather(key_low, "ctx", axis=0, tiled=True),
        lax.all_gather(values, "ctx", axis=0, tiled=True),
    )
    block_rows = min(1024, all_rows)
    block_count = all_rows // block_rows
    block_index = jnp.arange(all_rows, dtype=jnp.int32).reshape(block_count, block_rows)
    key_blocks = keys_whole.reshape(block_count, block_rows, model_width)
    value_blocks = values_whole.reshape(block_count, block_rows, model_width)

    def query_side(key_rows, value_rows, key_index):
        key_seg, _ = places(key_index, lengths_in, prompt_rows)
        key_heads = key_rows.reshape(block_rows, head_count, HEAD)
        value_heads = value_rows.reshape(block_rows, head_count, HEAD)
        prob, score_grad = pair_terms(
            query_heads,
            grad_heads,
            log_total,
            row_dot,
            own_index,
            own_seg,
            key_heads,
            value_heads,
            key_index,
            key_seg,
            score_scale,
        )
        query_term = (
            jnp.einsum("hqk,khd->qhd", score_grad, key_heads, preferred_element_type=jnp.float32)
            * score_scale
        )
        return (prob, score_grad, query_term)

    def back_block(query_grad, block_args):
        key_rows, value_rows, key_index = block_args
        prob, score_grad, query_term = query_side(key_rows, value_rows, key_index)
        key_term = (
            jnp.einsum("hqk,qhd->khd", score_grad, query_heads, preferred_element_type=jnp.float32)
            * score_scale
        )
        value_term = jnp.einsum(
            "hqk,qhd->khd",
            prob.astype(jnp.bfloat16),
            grad_heads,
            preferred_element_type=jnp.float32,
        )
        return (
            query_grad + query_term,
            (
                key_term.reshape(block_rows, model_width),
                value_term.reshape(block_rows, model_width),
            ),
        )

    query_grad, (key_terms, value_terms) = lax.scan(
        back_block,
        jnp.zeros((row_count, head_count, HEAD), jnp.float32),
        (key_blocks, value_blocks, block_index),
    )
    key_grad, value_grad = (
        lax.psum_scatter(
            key_terms.reshape(all_rows, model_width).astype(jnp.bfloat16),
            "ctx",
            scatter_dimension=0,
            tiled=True,
        ).astype(jnp.float32),
        lax.psum_scatter(
            value_terms.reshape(all_rows, model_width).astype(jnp.bfloat16),
            "ctx",
            scatter_dimension=0,
            tiled=True,
        ).astype(jnp.float32),
    )
    query_pre_grad, query_gain_grad = query_pull(query_grad.reshape(row_count, model_width))
    key_pre_grad, key_gain_grad = key_pull(key_grad)
    query_low_grad = query_pre_grad.astype(jnp.bfloat16)
    key_low_grad = key_pre_grad.astype(jnp.bfloat16)
    value_low_grad = value_grad.astype(jnp.bfloat16)
    query_w_grad = jnp.dot(hidden.T, query_low_grad, preferred_element_type=jnp.float32)
    key_w_grad = jnp.dot(hidden.T, key_low_grad, preferred_element_type=jnp.float32)
    value_w_grad = jnp.dot(hidden.T, value_low_grad, preferred_element_type=jnp.float32)
    hidden_grad = jnp.dot(query_low_grad, query_all.T, preferred_element_type=jnp.float32)
    hidden_grad = hidden_grad + jnp.dot(key_low_grad, key_all.T, preferred_element_type=jnp.float32)
    hidden_grad = hidden_grad + jnp.dot(
        value_low_grad, value_all.T, preferred_element_type=jnp.float32
    )
    input_norm_grad, attn_gain_grad = attn_pull(hidden_grad)
    input_grad = (mixed_grad + input_norm_grad)[None]
    summed_grads = (
        lax.psum_scatter(query_w_grad, ("ctx", "fsdp"), scatter_dimension=0, tiled=True),
        lax.psum_scatter(key_w_grad, ("ctx", "fsdp"), scatter_dimension=0, tiled=True),
        lax.psum_scatter(value_w_grad, ("ctx", "fsdp"), scatter_dimension=0, tiled=True),
        lax.psum_scatter(out_w_grad, ("ctx", "fsdp"), scatter_dimension=0, tiled=True),
        lax.psum_scatter(attn_gain_grad, ("ctx", "fsdp"), scatter_dimension=0, tiled=True),
        lax.psum_scatter(query_gain_grad, ("ctx", "fsdp"), scatter_dimension=0, tiled=True),
        lax.psum_scatter(key_gain_grad, ("ctx", "fsdp"), scatter_dimension=0, tiled=True),
        lax.psum_scatter(ffn_gain_grad, ("ctx", "fsdp"), scatter_dimension=0, tiled=True),
    )
    return (
        output,
        input_grad,
        summed_grads[4],
        summed_grads[5],
        summed_grads[6],
        summed_grads[7],
        summed_grads[0],
        summed_grads[1],
        summed_grads[2],
        summed_grads[3],
        expert_grads[0],
        expert_grads[1],
        expert_grads[2],
    )


HEADS = 16
LOG2E = 1.4426950408889634
VMEM_BYTES = 60 * 2**20


def dot_nn(left, right):
    return lax.dot_general(
        left, right, (((1,), (0,)), ((), ())), preferred_element_type=jnp.float32
    )


def dot_nt(left, right):
    return lax.dot_general(
        left, right, (((1,), (1,)), ((), ())), preferred_element_type=jnp.float32
    )


def dot_tn(left, right):
    return lax.dot_general(
        left, right, (((0,), (0,)), ((), ())), preferred_element_type=jnp.float32
    )


def segment_start(starts, index):
    first = starts[0]
    for c in range(1, starts.shape[0]):
        first = jnp.where(index >= starts[c], starts[c], first)
    return first


def segment_end(starts, index, total):
    last = jnp.int32(total)
    for c in range(starts.shape[0] - 1, 0, -1):
        last = jnp.where(index < starts[c], starts[c], last)
    return last


def allowed_tile(starts, key_first, query_first, size, prompt_rows):
    key_index = key_first + lax.broadcasted_iota(jnp.int32, (size, size), 0)
    query_index = query_first + lax.broadcasted_iota(jnp.int32, (1, size), 1)
    own_start = jnp.full((1, size), prompt_rows, jnp.int32)
    for c in range(1, starts.shape[0]):
        own_start = jnp.where(query_index >= starts[c], starts[c], own_start)
    return (key_index <= query_index) & ((key_index < prompt_rows) | (key_index >= own_start))


def attend_forward_kernel(
    starts,
    query_pre,
    key_pre,
    value_t,
    query_inv,
    key_inv,
    query_gain,
    key_gain,
    cosine,
    sine,
    out,
    query,
    key,
    key_t,
    log_rows,
    *,
    size,
    prompt_rows,
    score_scale,
):
    i = pl.program_id(0)
    half = HEAD // 2
    total, columns = key.shape
    spans = [slice(h * HEAD, (h + 1) * HEAD) for h in range(columns // HEAD)]
    prompt_blocks = prompt_rows // size

    @pl.when(i == 0)
    def _():
        @pl.loop(0, total // size)
        def _(b):
            at = pl.ds(pl.multiple_of(b * size, size), size)
            cos, sin = cosine[:, at], sine[:, at]
            for span in spans:
                for pre, inv, gain, is_key in (
                    (query_pre, query_inv, query_gain, False),
                    (key_pre, key_inv, key_gain, True),
                ):
                    normed = pre[span, at] * inv[:, at] * gain[span, :]
                    former, latter = normed[:half], normed[half:]
                    turned = jnp.concatenate(
                        [former * cos - latter * sin, latter * cos + former * sin], axis=0
                    )
                    if is_key:
                        key_t[span, at] = turned.astype(jnp.bfloat16)
                        key[at, span] = turned.T.astype(jnp.bfloat16)
                    else:
                        turned = turned * (score_scale * LOG2E)
                        query[at, span] = turned.T.astype(jnp.bfloat16)

    query_first = i * size
    here = pl.ds(pl.multiple_of(query_first, size), size)
    chunk = size // 2
    parts = [slice(c * chunk, (c + 1) * chunk) for c in range(2)]
    work = [(span, part) for span in spans for part in parts]
    query_all = [query[here, span] for span in spans]
    query_rows = [rows[part] for rows in query_all for part in parts]

    def fold(j, states, masked):
        at = pl.ds(pl.multiple_of(j * size, size), size)
        scores = [dot_nt(key[at, span], rows) for (span, _), rows in zip(work, query_rows)]
        if masked:
            allowed = allowed_tile(starts, j * size, query_first, size, prompt_rows)
        made = []
        for (span, part), score, (highest, denominator, weighted) in zip(work, scores, states):
            if masked:
                score = jnp.where(allowed[:, part], score, MASKED)
            new_high = jnp.maximum(highest, jnp.max(score, axis=0, keepdims=True))
            shrink = jnp.exp2(highest - new_high)
            unnormed = jnp.exp2(score - new_high)
            denominator = denominator * shrink + jnp.sum(unnormed, axis=0, keepdims=True)
            weighted = weighted * shrink + dot_nn(value_t[span, at], unnormed.astype(jnp.bfloat16))
            made.append((new_high, denominator, weighted))
        return tuple(made)

    states = tuple(
        (
            jnp.full((1, chunk), MASKED, jnp.float32),
            jnp.zeros((1, chunk), jnp.float32),
            jnp.zeros((HEAD, chunk), jnp.float32),
        )
        for _ in work
    )
    in_prompt = i < prompt_blocks
    whole = jnp.where(in_prompt, i, prompt_blocks)
    states = lax.fori_loop(0, whole, lambda j, s: fold(j, s, False), states)
    own_first = jnp.where(in_prompt, i, segment_start(starts, query_first) // size)
    states = lax.fori_loop(own_first, i + 1, lambda j, s: fold(j, s, True), states)
    for k, ((span, part), (highest, denominator, weighted)) in enumerate(zip(work, states)):
        out[part, span] = (weighted / denominator).T.astype(jnp.bfloat16)
        log_rows[k // 2 : k // 2 + 1, part] = highest + jnp.log2(denominator)


def attend_forward(starts, query_pre, key_pre, value_t, query_inv, key_inv, query_gain, key_gain, cosine, sine, size, prompt_rows, score_scale):
    columns, total = query_pre.shape
    heads = columns // HEAD
    pairs = total * total // 2

    def once(shape):
        return pl.BlockSpec(shape, lambda i, s: (0, 0), pipeline_mode=pl.Buffered(1))

    wide, tall, row = (columns, total), (total, columns), (1, total)
    gain, table = (columns, 1), (HEAD // 2, total)
    return pl.pallas_call(
        partial(attend_forward_kernel, size=size, prompt_rows=prompt_rows, score_scale=score_scale),
        grid_spec=pltpu.PrefetchScalarGridSpec(
            num_scalar_prefetch=1,
            grid=(total // size,),
            in_specs=[once(k) for k in (wide, wide, wide, row, row, gain, gain, table, table)],
            out_specs=[
                pl.BlockSpec((size, columns), lambda i, s: (i, 0)),
                pl.BlockSpec(tall, lambda i, s: (0, 0)),
                pl.BlockSpec(tall, lambda i, s: (0, 0)),
                pl.BlockSpec(wide, lambda i, s: (0, 0)),
                pl.BlockSpec((heads, size), lambda i, s: (0, i)),
            ],
        ),
        out_shape=[
            jax.ShapeDtypeStruct(tall, jnp.bfloat16),
            jax.ShapeDtypeStruct(tall, jnp.bfloat16),
            jax.ShapeDtypeStruct(tall, jnp.bfloat16),
            jax.ShapeDtypeStruct(wide, jnp.bfloat16),
            jax.ShapeDtypeStruct((heads, total), jnp.float32),
        ],
        compiler_params=pltpu.CompilerParams(vmem_limit_bytes=VMEM_BYTES),
        cost_estimate=pl.CostEstimate(
            flops=12 * pairs * columns, bytes_accessed=20 * total * columns, transcendentals=pairs * heads
        ),
        name="attend_forward",
    )(starts, query_pre, key_pre, value_t, query_inv, key_inv, query_gain, key_gain, cosine, sine)


def attend_backward_kernel(
    starts,
    query,
    key,
    key_t,
    value_t,
    out_grad,
    out,
    log_rows,
    query_pre,
    key_pre,
    query_inv,
    key_inv,
    query_gain,
    key_gain,
    cosine,
    sine,
    *refs,
    size,
    prompt_rows,
    score_scale,
):
    query_scaled, key_scaled, value_grad, query_gain_grad, key_gain_grad, dots = refs[-9:-3]
    query_sum, key_sum, row_dot = refs[-3:]
    j = pl.program_id(0)
    half = HEAD // 2
    total, columns = key.shape
    spans = [slice(h * HEAD, (h + 1) * HEAD) for h in range(columns // HEAD)]
    blocks = total // size
    prompt_blocks = prompt_rows // size

    @pl.when(j == 0)
    def _():
        query_sum[...] = jnp.zeros_like(query_sum)

        @pl.loop(0, blocks)
        def _(b):
            at = pl.ds(pl.multiple_of(b * size, size), size)
            for h, span in enumerate(spans):
                product = out_grad[at, span].astype(jnp.float32) * out[at, span].astype(jnp.float32)
                row_dot[h : h + 1, at] = jnp.sum(product.T, axis=0, keepdims=True)

    chunk = size // 2
    here = pl.ds(pl.multiple_of(j * size, size), size)
    key_rows = [key[here, span] for span in spans]
    key_cols = [key_t[span, here] for span in spans]
    value_rows = [value_t[span, here].T for span in spans]

    def fold(i, states, masked):
        if masked:
            allowed = allowed_tile(starts, j * size, i * size, size, prompt_rows)
        made = list(states)
        for c in range(2):
            at = pl.ds(pl.multiple_of(i * size + c * chunk, chunk), chunk)
            query_rows = [query[at, span] for span in spans]
            grad_rows = [out_grad[at, span] for span in spans]
            scores = [dot_nt(k, q) for k, q in zip(key_rows, query_rows)]
            prob_grads = [dot_nt(v, g) for v, g in zip(value_rows, grad_rows)]
            for h, span in enumerate(spans):
                key_part, value_part = made[h]
                prob = jnp.exp2(scores[h] - log_rows[h, :, at])
                if masked:
                    prob = jnp.where(allowed[:, c * chunk : (c + 1) * chunk], prob, 0.0)
                score_grad = (prob * (prob_grads[h] - row_dot[h : h + 1, at])).astype(jnp.bfloat16)
                value_part = value_part + dot_nn(prob.astype(jnp.bfloat16), grad_rows[h])
                key_part = key_part + dot_nn(score_grad, query_rows[h])
                query_sum[span, at] += dot_nn(key_cols[h], score_grad)
                made[h] = (key_part, value_part)
        return tuple(made)

    states = tuple(
        (jnp.zeros((size, HEAD), jnp.float32), jnp.zeros((size, HEAD), jnp.float32)) for _ in spans
    )
    in_prompt = j < prompt_blocks
    last_own = (segment_end(starts, (j + 1) * size - 1, total) - 1) // size + 1
    masked_end = jnp.where(in_prompt, j + 1, last_own)
    states = lax.fori_loop(j, masked_end, lambda i, s: fold(i, s, True), states)
    whole_end = jnp.where(in_prompt, blocks, masked_end)
    states = lax.fori_loop(masked_end, whole_end, lambda i, s: fold(i, s, False), states)
    for span, (key_part, value_part) in zip(spans, states):
        key_sum[span, here] = key_part.T
        value_grad[span, here] = value_part.T.astype(jnp.bfloat16)

    @pl.when(j == blocks - 1)
    def _():
        query_gain_grad[...] = jnp.zeros_like(query_gain_grad)
        key_gain_grad[...] = jnp.zeros_like(key_gain_grad)

        @pl.loop(0, blocks)
        def _(b):
            at = pl.ds(pl.multiple_of(b * size, size), size)
            cos, sin = cosine[:, at], sine[:, at]
            for place, (grad, factor, pre, inv, gain, scaled, gain_grad) in enumerate(
                (
                    (query_sum, score_scale, query_pre, query_inv, query_gain, query_scaled, query_gain_grad),
                    (key_sum, 1.0 / LOG2E, key_pre, key_inv, key_gain, key_scaled, key_gain_grad),
                )
            ):
                summed = None
                for span in spans:
                    turned = grad[span, at] * factor
                    former, latter = turned[:half], turned[half:]
                    back = jnp.concatenate(
                        [former * cos + latter * sin, latter * cos - former * sin], axis=0
                    )
                    before = pre[span, at]
                    gain_grad[span, :] += jnp.sum(
                        back * (before * inv[:, at]), axis=1, keepdims=True
                    )
                    back = back * gain[span, :]
                    scaled[span, at] = back
                    dot = jnp.sum(back * before, axis=0, keepdims=True)
                    summed = dot if summed is None else summed + dot
                dots[place : place + 1, at] = summed


def attend_backward(starts, head, held, query, key, key_t, value_t, out_grad, out, log_rows, query_pre, key_pre, query_inv, key_inv, query_gain, key_gain, cosine, sine, size, prompt_rows, score_scale):
    columns, total = query_pre.shape
    pairs = total * total // 2
    held = () if held is None else tuple(held)

    def once(shape, index):
        return pl.BlockSpec(shape, lambda j, s: index, pipeline_mode=pl.Buffered(1))

    wide, tall = once((HEAD, total), (head, 0)), once((total, HEAD), (0, head))
    row, table = once((1, total), (0, 0)), once((HEAD // 2, total), (0, 0))
    gain, per_head = once((HEAD, 1), (head, 0)), once((1, 1, total), (head, 0, 0))
    return pl.pallas_call(
        partial(attend_backward_kernel, size=size, prompt_rows=prompt_rows, score_scale=score_scale),
        grid_spec=pltpu.PrefetchScalarGridSpec(
            num_scalar_prefetch=1,
            grid=(total // size,),
            in_specs=[tall, tall, wide, wide, tall, tall, per_head, wide, wide, row, row, gain, gain, table, table]
            + [pl.BlockSpec(memory_space=pl.ANY)] * len(held),
            out_specs=[wide, wide, wide, gain, gain, once((2, total), (0, 0))],
            scratch_shapes=[
                pltpu.VMEM((HEAD, total), jnp.float32),
                pltpu.VMEM((HEAD, total), jnp.float32),
                pltpu.VMEM((1, total), jnp.float32),
            ],
        ),
        out_shape=[
            jax.ShapeDtypeStruct((columns, total), jnp.float32),
            jax.ShapeDtypeStruct((columns, total), jnp.float32),
            jax.ShapeDtypeStruct((columns, total), jnp.bfloat16),
            jax.ShapeDtypeStruct((columns, 1), jnp.float32),
            jax.ShapeDtypeStruct((columns, 1), jnp.float32),
            jax.ShapeDtypeStruct((2, total), jnp.float32),
        ],
        input_output_aliases={16 + k: k for k in range(len(held))},
        compiler_params=pltpu.CompilerParams(vmem_limit_bytes=VMEM_BYTES),
        cost_estimate=pl.CostEstimate(
            flops=24 * pairs * HEAD, bytes_accessed=40 * total * HEAD, transcendentals=pairs
        ),
        name="attend_backward",
    )(starts, query, key, key_t, value_t, out_grad, out, log_rows, query_pre, key_pre, query_inv, key_inv, query_gain, key_gain, cosine, sine, *held)


def project_kernel(places, *refs, count):
    blocks = refs[:count]
    w_t, gain = refs[count : count + 2]
    hidden, query_pre, key_pre, value_t, squares = refs[-5:]
    columns = query_pre.shape[0]
    for b, block in enumerate(blocks):

        @pl.when(pl.program_id(0) // 2 == b)
        def _(block=block):
            rows = block[...].astype(jnp.float32)
            inverse = lax.rsqrt(jnp.mean(rows * rows, axis=-1, keepdims=True) + EPSILON)
            hidden[...] = (rows * inverse * gain[...]).astype(jnp.bfloat16)

    for k, out in enumerate((query_pre, key_pre)):
        made = dot_nt(w_t[k * columns : (k + 1) * columns, :], hidden[...])
        out[...] = made
        squares[k : k + 1, :] = jnp.sum(made * made, axis=0, keepdims=True)
    value_t[...] = dot_nt(w_t[2 * columns :, :], hidden[...]).astype(jnp.bfloat16)


def project(places, blocks, rows, w_t, gain, held, total):
    count, width = len(blocks), blocks[0].shape[1]
    columns = w_t.shape[0] // 3
    tile = rows // 2
    held = () if held is None else tuple(held)

    def block_spec(b):
        return pl.BlockSpec((tile, width), lambda i, p: (jnp.clip(i - 2 * b, 0, 1), 0))

    def there(shape, along):
        if along == 0:
            return pl.BlockSpec(shape, lambda i, p: (2 * p[i // 2] + i % 2, 0))
        return pl.BlockSpec(shape, lambda i, p: (0, 2 * p[i // 2] + i % 2))

    return pl.pallas_call(
        partial(project_kernel, count=count),
        grid_spec=pltpu.PrefetchScalarGridSpec(
            num_scalar_prefetch=1,
            grid=(2 * count,),
            in_specs=[block_spec(b) for b in range(count)]
            + [
                pl.BlockSpec(w_t.shape, lambda i, p: (0, 0)),
                pl.BlockSpec((1, width), lambda i, p: (0, 0)),
            ]
            + [pl.BlockSpec(memory_space=pl.ANY)] * len(held),
            out_specs=[
                there((tile, width), 0),
                there((columns, tile), 1),
                there((columns, tile), 1),
                there((columns, tile), 1),
                there((2, tile), 1),
            ],
        ),
        out_shape=[
            jax.ShapeDtypeStruct((total, width), jnp.bfloat16),
            jax.ShapeDtypeStruct((columns, total), jnp.float32),
            jax.ShapeDtypeStruct((columns, total), jnp.float32),
            jax.ShapeDtypeStruct((columns, total), jnp.bfloat16),
            jax.ShapeDtypeStruct((2, total), jnp.float32),
        ],
        input_output_aliases={3 + count + k: k for k in range(len(held))},
        compiler_params=pltpu.CompilerParams(vmem_limit_bytes=VMEM_BYTES),
        cost_estimate=pl.CostEstimate(
            flops=6 * count * rows * width * columns,
            bytes_accessed=count * (4 * rows * width + 10 * rows * columns) + 6 * width * columns,
            transcendentals=count * rows,
        ),
        name="project",
    )(places, *blocks, w_t, gain, *held)


def place_rows_kernel(places, *refs):
    *pieces, out = refs
    for k, piece in enumerate(pieces):
        out[places[k]] = piece[...]


def place_rows(places, blocks, first, rows):
    width = blocks[0].shape[1]
    return pl.pallas_call(
        place_rows_kernel,
        grid_spec=pltpu.PrefetchScalarGridSpec(
            num_scalar_prefetch=1,
            grid=(1,),
            in_specs=[pl.BlockSpec((rows, width), lambda i, p: (first // rows, 0))] * len(blocks),
            out_specs=pl.BlockSpec((len(blocks), rows, width), lambda i, p: (0, 0, 0)),
        ),
        out_shape=jax.ShapeDtypeStruct((len(blocks), rows, width), blocks[0].dtype),
        compiler_params=pltpu.CompilerParams(vmem_limit_bytes=VMEM_BYTES),
        name="place_rows",
    )(places, *blocks)


def hidden_term_kernel(place, heads_grad, w_t, out_rows, *refs, start, halves):
    outs = refs[-2:] if halves else refs[-1:]
    rows = heads_grad.shape[1]
    term = dot_tn(heads_grad[...], w_t[...])
    below = out_rows[0]
    if halves:
        cut = outs[0].shape[0]
        outs[0][...] = term[:cut].astype(jnp.bfloat16)
        outs[1][: rows - cut, :] = term[cut:].astype(jnp.bfloat16)
        outs[1][rows - cut :, :] = below
        return
    (out,) = outs
    got = refs[0]
    stop = start + got.shape[0]
    upper = min(stop, rows)
    if start:
        out[:start, :] = term[:start].astype(jnp.bfloat16)
    if upper < rows:
        out[upper:rows, :] = term[upper:].astype(jnp.bfloat16)
    out[start:upper, :] = (
        term[start:upper] + got[: upper - start, :].astype(jnp.float32)
    ).astype(jnp.bfloat16)
    if stop > rows:
        below = below.astype(jnp.float32) + got[rows - start :, :].astype(jnp.float32)
    out[rows:, :] = below.astype(jnp.bfloat16)


def hidden_term(place, heads_grad, w_t, out_rows, rows, got=None, start=0):
    columns, width = w_t.shape
    whole = rows + out_rows.shape[1]
    tile = min(512, width)
    halves = got is None
    gots, outs = ([], [whole // 2] * 2) if halves else ([got], [whole])
    made = pl.pallas_call(
        partial(hidden_term_kernel, start=start, halves=halves),
        grid_spec=pltpu.PrefetchScalarGridSpec(
            num_scalar_prefetch=1,
            grid=(width // tile,),
            in_specs=[
                pl.BlockSpec((columns, rows), lambda i, p: (0, p[0])),
                pl.BlockSpec((columns, tile), lambda i, p: (0, i)),
                pl.BlockSpec((1, whole - rows, tile), lambda i, p: (p[0], 0, i)),
            ]
            + [pl.BlockSpec((g.shape[0], tile), lambda i, p: (0, i)) for g in gots],
            out_specs=[pl.BlockSpec((count, tile), lambda i, p: (0, i)) for count in outs],
        ),
        out_shape=[jax.ShapeDtypeStruct((count, width), jnp.bfloat16) for count in outs],
        compiler_params=pltpu.CompilerParams(vmem_limit_bytes=VMEM_BYTES),
        cost_estimate=pl.CostEstimate(
            flops=0, bytes_accessed=0, transcendentals=0
        ),
        name="hidden_term",
    )(place, heads_grad, w_t, out_rows, *gots)
    return made if halves else made[0]


def input_grad_kernel(place, heads_grad, w_t, before, past, tokens, gain, mixed_grad, out):
    got = before[...].astype(jnp.float32) + past[...].astype(jnp.float32)
    scaled = (dot_tn(heads_grad[...], w_t[...]) + got) * gain[...]
    inputs = tokens[...].astype(jnp.float32)
    inverse = lax.rsqrt(jnp.mean(inputs * inputs, axis=-1, keepdims=True) + EPSILON)
    normed = inputs * inverse
    along = jnp.mean(scaled * normed, axis=-1, keepdims=True)
    out[...] = mixed_grad[...] + inverse * (scaled - normed * along)


def input_grad_of(place, heads_grad, w_t, before, past, tokens, gain, mixed_grad):
    columns, width = w_t.shape
    rows = tokens.shape[0]
    tile = rows // 4
    block = pl.BlockSpec((tile, width), lambda i, p: (i, 0))
    return pl.pallas_call(
        input_grad_kernel,
        grid_spec=pltpu.PrefetchScalarGridSpec(
            num_scalar_prefetch=1,
            grid=(4,),
            in_specs=[
                pl.BlockSpec((columns, tile), lambda i, p: (0, 4 * p[0] + i)),
                pl.BlockSpec((columns, width), lambda i, p: (0, 0)),
                block,
                block,
                block,
                pl.BlockSpec((1, width), lambda i, p: (0, 0)),
                block,
            ],
            out_specs=block,
        ),
        out_shape=jax.ShapeDtypeStruct((rows, width), jnp.float32),
        compiler_params=pltpu.CompilerParams(vmem_limit_bytes=VMEM_BYTES),
        cost_estimate=pl.CostEstimate(
            flops=2 * rows * width * columns,
            bytes_accessed=2 * columns * (rows + width) + 14 * rows * width,
            transcendentals=rows,
        ),
        name="input_grad",
    )(place, heads_grad, w_t, before, past, tokens, gain, mixed_grad)


def out_grad_kernel(branch, w_out, out):
    made = dot_nt(branch[...], w_out[...]).astype(jnp.bfloat16)
    columns = out.shape[2]
    for k in range(out.shape[0]):
        out[k] = made[:, k * columns : (k + 1) * columns]


def out_grad_of(branch, w_out, contexts):
    rows, width = branch.shape
    columns = w_out.shape[0] // contexts
    return pl.pallas_call(
        out_grad_kernel,
        grid=(contexts // 2,),
        in_specs=[
            pl.BlockSpec((rows, width), lambda i: (0, 0)),
            pl.BlockSpec((2 * columns, width), lambda i: (i, 0)),
        ],
        out_specs=pl.BlockSpec((2, rows, columns), lambda i: (i, 0, 0)),
        out_shape=jax.ShapeDtypeStruct((contexts, rows, columns), jnp.bfloat16),
        compiler_params=pltpu.CompilerParams(vmem_limit_bytes=VMEM_BYTES),
        cost_estimate=pl.CostEstimate(
            flops=2 * rows * width * width, bytes_accessed=2 * width * width, transcendentals=0
        ),
        name="out_grad",
    )(branch, w_out)


def heads_grad_kernel(query_scaled, key_scaled, value_grad, query_pre, key_pre, inverse, dots, out):
    columns = query_scaled.shape[0]
    for k, (scaled, pre) in enumerate(((query_scaled, query_pre), (key_scaled, key_pre))):
        inv = inverse[k : k + 1, :]
        factor = inv * inv * dots[k : k + 1, :]
        out[k * columns : (k + 1) * columns, :] = (inv * (scaled[...] - pre[...] * factor)).astype(
            jnp.bfloat16
        )
    out[2 * columns :, :] = value_grad[...]


def heads_grad_of(query_scaled, key_scaled, value_grad, query_pre, key_pre, inverse, dots):
    columns, total = query_scaled.shape
    tile = total // 4
    wide = pl.BlockSpec((columns, tile), lambda i: (0, i))
    row = pl.BlockSpec((2, tile), lambda i: (0, i))
    return pl.pallas_call(
        heads_grad_kernel,
        grid=(4,),
        in_specs=[wide] * 5 + [row] * 2,
        out_specs=pl.BlockSpec((3 * columns, tile), lambda i: (0, i)),
        out_shape=jax.ShapeDtypeStruct((3 * columns, total), jnp.bfloat16),
        compiler_params=pltpu.CompilerParams(vmem_limit_bytes=VMEM_BYTES),
        cost_estimate=pl.CostEstimate(
            flops=8 * columns * total, bytes_accessed=24 * columns * total, transcendentals=0
        ),
        name="heads_grad",
    )(query_scaled, key_scaled, value_grad, query_pre, key_pre, inverse, dots)


def heads_product_kernel(heads_grad, hidden, others, out):
    columns = heads_grad.shape[0]
    out[0, :, :columns] = dot_nn(heads_grad[...], hidden[...]).T.astype(jnp.bfloat16)
    out[0, :, columns:] = others[...].astype(jnp.bfloat16)


def heads_product_of(heads_grad, hidden_all, others, contexts):
    columns, total = heads_grad.shape
    width = hidden_all.shape[1]
    tile, extra = width // contexts, others.shape[1]
    return pl.pallas_call(
        heads_product_kernel,
        grid=(contexts,),
        in_specs=[
            pl.BlockSpec((columns, total), lambda i: (0, 0), pipeline_mode=pl.Buffered(1)),
            pl.BlockSpec((total, tile), lambda i: (0, i)),
            pl.BlockSpec((tile, extra), lambda i: (i, 0)),
        ],
        out_specs=pl.BlockSpec((1, tile, columns + extra), lambda i: (i, 0, 0)),
        out_shape=jax.ShapeDtypeStruct((contexts, tile, columns + extra), jnp.bfloat16),
        compiler_params=pltpu.CompilerParams(vmem_limit_bytes=VMEM_BYTES),
        cost_estimate=pl.CostEstimate(
            flops=2 * columns * total * width,
            bytes_accessed=2 * total * (columns + width),
            transcendentals=0,
        ),
        name="heads_product",
    )(heads_grad, hidden_all, others)


def gather_pieces_kernel(me, *refs):
    *pieces, out = refs
    for step, piece in enumerate(pieces):
        out[lax.rem(me[0] + step, len(pieces))] = piece[...]


def gather_pieces(me, pieces):
    return pl.pallas_call(
        gather_pieces_kernel,
        grid_spec=pltpu.PrefetchScalarGridSpec(
            num_scalar_prefetch=1,
            grid=(1,),
            in_specs=[pl.BlockSpec(piece.shape, lambda i, m: (0, 0)) for piece in pieces],
            out_specs=pl.BlockSpec((len(pieces),) + pieces[0].shape, lambda i, m: (0, 0, 0)),
        ),
        out_shape=jax.ShapeDtypeStruct((len(pieces),) + pieces[0].shape, pieces[0].dtype),
        compiler_params=pltpu.CompilerParams(vmem_limit_bytes=VMEM_BYTES),
        name="gather_pieces",
    )(me[None], *pieces)


def slot_match(rank_row, slots):
    return lax.broadcasted_iota(jnp.int32, (slots, rank_row.shape[1]), 0) == rank_row


def slot_gates(match, gate_row):
    return jnp.sum(jnp.where(match, gate_row, 0.0), axis=1, keepdims=True)


def experts_forward_kernel(*refs, count, slots, aliased, tiles):
    ranks, gates = refs[:2]
    blocks = refs[2 : 2 + count]
    w_gate, w_up, w_down = refs[2 + count : 5 + count]
    refs = refs[5 + count + aliased :]
    taken, active, gate_slope, up_slope = refs[:4]
    outs = refs[4 : 4 + count]
    made, weights = refs[4 + count :]
    e, f = pl.program_id(0), pl.program_id(1)
    tile, wide_tile = w_gate.shape[2], w_down.shape[2]

    @pl.when(f == 0)
    def _():
        for b in range(count):
            here = slice(b * slots, (b + 1) * slots)
            match = slot_match(ranks[b, e], slots)
            weights[here, :] = slot_gates(match, gates[b, e])
            taken[0, here, :] = dot_nn(match.astype(jnp.bfloat16), blocks[b][...]).astype(
                jnp.bfloat16
            )

    @pl.when(f < tiles)
    def _():
        at = pl.ds(pl.multiple_of(f * tile, tile), tile)
        rows = taken[0]
        gate_pre = dot_nn(rows, w_gate[0])
        up_pre = dot_nn(rows, w_up[0])
        sigmoid_gate = 1.0 / (1.0 + jnp.exp(-gate_pre))
        silu = gate_pre * sigmoid_gate
        active[0, :, at] = (silu * up_pre).astype(jnp.bfloat16)
        up_slope[0, :, at] = silu.astype(jnp.bfloat16)
        gate_slope[0, :, at] = (up_pre * (sigmoid_gate + silu * (1.0 - sigmoid_gate))).astype(
            jnp.bfloat16
        )

    @pl.when(f >= tiles)
    def _():
        at = pl.ds(pl.multiple_of((f - tiles) * wide_tile, wide_tile), wide_tile)
        made[e, :, at] = (dot_nn(active[0], w_down[0]) * weights[...]).astype(jnp.bfloat16)

    @pl.when((f == pl.num_programs(1) - 1) & (e == pl.num_programs(0) - 1))
    def _():
        combine(ranks, made, outs, count, slots)


def combine(ranks, made, outs, count, slots):
    for b in range(count):
        summed = None
        for k in range(made.shape[0]):
            match = slot_match(ranks[b, k], slots).astype(jnp.float32).astype(jnp.bfloat16)
            term = dot_tn(match, made[k, b * slots : (b + 1) * slots, :])
            summed = term if summed is None else summed + term
        outs[b][...] = summed.astype(jnp.bfloat16)


def experts_backward_kernel(*refs, count, slots, aliased, tiles):
    ranks, gates = refs[:2]
    blocks = refs[2 : 2 + count]
    w_gate, w_up, w_down, gate_slope, up_slope = refs[2 + count : 7 + count]
    refs = refs[7 + count + aliased :]
    taken, gate_grad, up_grad = refs[:3]
    outs = refs[3 : 3 + count]
    (made,) = refs[3 + count :]
    e, f = pl.program_id(0), pl.program_id(1)
    tile, wide_tile = w_down.shape[1], w_gate.shape[1]

    @pl.when(f == 0)
    def _():
        for b in range(count):
            match = slot_match(ranks[b, e], slots)
            weight = slot_gates(match, gates[b, e])
            taken[0, b * slots : (b + 1) * slots, :] = (
                dot_nn(match.astype(jnp.bfloat16), blocks[b][...]) * weight
            ).astype(jnp.bfloat16)

    @pl.when(f < tiles)
    def _():
        at = pl.ds(pl.multiple_of(f * tile, tile), tile)
        active_grad = dot_nt(taken[0], w_down[0])
        gate_grad[0, :, at] = (active_grad * gate_slope[0].astype(jnp.float32)).astype(jnp.bfloat16)
        up_grad[0, :, at] = (active_grad * up_slope[0].astype(jnp.float32)).astype(jnp.bfloat16)

    @pl.when(f >= tiles)
    def _():
        at = pl.ds(pl.multiple_of((f - tiles) * wide_tile, wide_tile), wide_tile)
        made[e, :, at] = (dot_nt(gate_grad[0], w_gate[0]) + dot_nt(up_grad[0], w_up[0])).astype(
            jnp.bfloat16
        )

    @pl.when((f == pl.num_programs(1) - 1) & (e == pl.num_programs(0) - 1))
    def _():
        combine(ranks, made, outs, count, slots)


def experts_stage(
    forward, ranks, gates, blocks, weights, slopes, held, place, slots, all_slots, light=False
):
    count = len(blocks)
    rows, width = blocks[0].shape
    experts, _, hidden_units = weights[0].shape
    tile, wide_tile = min(512, hidden_units), min(1024, width)
    tiles, wide_tiles = hidden_units // tile, width // wide_tile
    part = count * slots

    def first(f):
        return jnp.minimum(f, tiles - 1)

    def later(f):
        return jnp.maximum(f - tiles, 0)

    info = pl.BlockSpec((count, experts, 1, rows), lambda e, f: (0, 0, 0, 0))
    block = pl.BlockSpec((rows, width), lambda e, f: (0, 0))
    wide = pl.BlockSpec((1, part, width), lambda e, f: (e, place, 0))
    narrow = pl.BlockSpec((1, part, hidden_units), lambda e, f: (e, place, 0))
    slope = pl.BlockSpec((1, part, tile), lambda e, f: (e, 0, first(f)))
    own = pl.BlockSpec((1, part, hidden_units), lambda e, f: (e, 0, 0))
    if forward:
        kernel, name = experts_forward_kernel, "experts_forward"
        into = pl.BlockSpec((1, width, tile), lambda e, f: (e, 0, first(f)))
        back = pl.BlockSpec((1, hidden_units, wide_tile), lambda e, f: (e, 0, later(f)))
        narrow_outs, own_outs, scratch = 1, 2, [pltpu.VMEM((part, 1), jnp.float32)]
    else:
        kernel, name = experts_backward_kernel, "experts_backward"
        into = pl.BlockSpec((1, wide_tile, hidden_units), lambda e, f: (e, later(f), 0))
        back = pl.BlockSpec((1, tile, width), lambda e, f: (e, first(f), 0))
        narrow_outs, own_outs, scratch = 2, 0, []
    held = () if held is None else tuple(held)
    before = 2 + count + 3 + len(slopes)
    scale = 0 if light else 1
    flops = 2 * experts * part * width * (3 * hidden_units + 2 * rows)
    return pl.pallas_call(
        partial(kernel, count=count, slots=slots, aliased=len(held), tiles=tiles),
        grid=(experts, tiles + wide_tiles),
        in_specs=[info, info]
        + [block] * count
        + [into, into, back]
        + [slope] * len(slopes)
        + [pl.BlockSpec(memory_space=pl.ANY)] * len(held),
        out_specs=[wide] + [narrow] * narrow_outs + [own] * own_outs + [block] * count,
        out_shape=[jax.ShapeDtypeStruct((experts, all_slots, width), jnp.bfloat16)]
        + [jax.ShapeDtypeStruct((experts, all_slots, hidden_units), jnp.bfloat16)] * narrow_outs
        + [jax.ShapeDtypeStruct((experts, part, hidden_units), jnp.bfloat16)] * own_outs
        + [jax.ShapeDtypeStruct((rows, width), jnp.bfloat16)] * count,
        scratch_shapes=[pltpu.VMEM((experts, part, width), jnp.bfloat16)] + scratch,
        input_output_aliases={before + k: k for k in range(len(held))},
        compiler_params=pltpu.CompilerParams(vmem_limit_bytes=VMEM_BYTES),
        cost_estimate=pl.CostEstimate(
            flops=scale * flops,
            bytes_accessed=scale
            * 2
            * (3 * experts * width * hidden_units + 4 * count * rows * width),
            transcendentals=scale * experts * part * hidden_units,
        ),
        name=name,
    )(ranks, gates, *blocks, *weights, *slopes, *held)


def ring_of(contexts):
    order = list(range(0, contexts, 2)) + list(range(contexts - 1, 0, -2))
    place_of = [order.index(c) for c in range(contexts)]
    up = [(order[p], order[(p + 1) % contexts]) for p in range(contexts)]
    down = [(b, a) for a, b in up]
    return order, place_of, up, down


class RingGather:
    def __init__(self, own, ring):
        _, _, self.up, self.down = ring
        self.half = len(self.up) // 2
        self.step = 0
        self.blocks = {0: own}
        self.from_before = self.from_after = own

    def advance(self, *earlier):
        self.step += 1
        before, past = self.from_before, self.from_after
        if earlier:
            before, past = lax.optimization_barrier((before, past) + earlier)[:2]
        if self.step < self.half:
            self.from_before = lax.ppermute(before, "ctx", self.up)
            self.from_after = lax.ppermute(past, "ctx", self.down)
            self.blocks[-self.step] = self.from_before
            self.blocks[self.step] = self.from_after
            return (-self.step, self.step)
        cut = before.shape[0] // 2
        first = lax.ppermute(before[:cut], "ctx", self.up)
        second = lax.ppermute(past[cut:], "ctx", self.down)
        self.blocks[self.half] = jnp.concatenate([first, second], axis=0)
        return (self.half,)


def add_low(left, right):
    return (left.astype(jnp.float32) + right.astype(jnp.float32)).astype(jnp.bfloat16)


class RingScatter:
    def __init__(self, ring):
        _, _, self.up, self.down = ring
        self.half = len(self.up) // 2
        self.step = self.half

    def prepare(self, terms, *earlier):
        if self.step == self.half:
            far = after(terms[self.half], *earlier)
            cut = far.shape[0] // 2
            before, past = far[:cut], far[cut:]
        else:
            before, past = terms[-self.step], terms[self.step]
            got_before, got_past = self.to_before, self.to_after
            if earlier:
                before, past = lax.optimization_barrier((before, past) + earlier)[:2]
            cut = got_before.shape[0]
            if cut < before.shape[0]:
                before = jnp.concatenate([add_low(got_before, before[:cut]), before[cut:]], axis=0)
                past = jnp.concatenate([past[:cut], add_low(got_past, past[cut:])], axis=0)
            else:
                before, past = add_low(got_before, before), add_low(got_past, past)
        self.payload = (before, past)
        return self.payload

    def send(self, *earlier):
        before, past = self.payload
        if earlier:
            before, past = lax.optimization_barrier((before, past) + earlier)[:2]
        self.to_before = lax.ppermute(before, "ctx", self.down)
        self.to_after = lax.ppermute(past, "ctx", self.up)
        self.step -= 1
        return self.payload

    def advance(self, terms, *earlier):
        self.prepare(terms, *earlier)
        return self.send()

    def finish(self, own):
        return (
            own.astype(jnp.float32)
            + self.to_before.astype(jnp.float32)
            + self.to_after.astype(jnp.float32)
        )


def sum_over_ctx(values, contexts):
    bit = 1
    while bit < contexts:
        values = values + lax.ppermute(values, "ctx", [(c, c ^ bit) for c in range(contexts)])
        bit *= 2
    return values


def after(value, *earlier):
    return lax.optimization_barrier((value,) + earlier)[0]


def shards_by_heads(
    tokens,
    cotangent,
    cont_lengths,
    routes,
    gates,
    attn_gain,
    query_gain,
    key_gain,
    ffn_gain,
    w_query,
    w_key,
    w_value,
    w_out,
    w_gate,
    w_up,
    w_down,
):
    both = ("ctx", "fsdp")
    contexts, splits = lax.axis_size("ctx"), lax.axis_size("fsdp")
    rows, width = tokens.shape[1:]
    route_count = routes.shape[2]
    total = rows * contexts
    prompt_rows = total // 2
    columns = width // contexts
    size = min(512, prompt_rows)
    local_experts = w_gate.shape[0]
    expert_total = local_experts * contexts
    slots = max(2, rows * route_count * 5 // (4 * expert_total))
    all_slots = contexts * slots
    score_scale = HEAD ** (-0.5)
    me = lax.axis_index("ctx")
    ring = ring_of(contexts)
    half = contexts // 2
    place = jnp.where(me % 2 == 0, me // 2, contexts - 1 - me // 2)

    def owner(offset):
        at = (place + offset) % contexts
        return jnp.where(at < half, 2 * at, 2 * (contexts - 1 - at) + 1)

    others = [k for step in range(1, half) for k in (-step, step)] + [half]

    own_rows = w_out.shape[0]
    token_ring = RingGather(jnp.concatenate([tokens[0], w_out], axis=0), ring)

    chosen = routes[0].T[None] == jnp.arange(expert_total, dtype=jnp.int32)[:, None, None]
    member = jnp.any(chosen, axis=1)
    gate_rows = jnp.sum(jnp.where(chosen, gates[0].T[None], 0.0), axis=1)
    earlier = jnp.tril(jnp.ones((rows, rows), jnp.bfloat16), -1)
    rank = jnp.einsum(
        "et,ut->eu", member.astype(jnp.bfloat16), earlier, preferred_element_type=jnp.float32
    )
    rank = jnp.where(member, rank, -1.0)
    rank_high = jnp.floor(rank / 16.0)
    gate_high = gate_rows.astype(jnp.bfloat16).astype(jnp.float32)
    routing = jnp.stack([rank_high, rank - 16.0 * rank_high, gate_high, gate_rows - gate_high])
    routing = routing.astype(jnp.bfloat16).reshape(4, contexts, local_experts * rows)
    routing = jnp.transpose(routing, (1, 0, 2)).reshape(contexts, own_rows, -1)
    routing_columns = routing.shape[2]

    cut = jnp.stack([w_query, w_key, w_value]).reshape(3, own_rows, contexts, columns)
    cut = jnp.transpose(cut, (2, 1, 0, 3)).reshape(contexts, own_rows, 3 * columns)
    own_gains = jnp.stack([attn_gain, query_gain, key_gain, ffn_gain], axis=1)
    cut = jnp.concatenate(
        [cut, jnp.broadcast_to(own_gains, (contexts,) + own_gains.shape), routing], axis=2
    )
    spare = -cut.shape[2] % 128
    cut = jnp.pad(cut, ((0, 0), (0, 0), (0, spare)))
    pieces = []
    for step in range(contexts):
        piece = lax.dynamic_index_in_dim(cut, (me - step) % contexts, 0, keepdims=False)
        if step:
            pairs = [(c, (c - step) % contexts) for c in range(contexts)]
            piece = lax.ppermute(piece, "ctx", pairs)
        pieces.append(piece)
    first_piece = pieces[1]
    pieces = gather_pieces(me, pieces)
    token_ring.advance(first_piece)
    gate_all = lax.all_gather(after(w_gate, pieces), "fsdp", axis=1, tiled=True)
    w_all = lax.all_gather(pieces, "fsdp", axis=1, tiled=True).reshape(width, -1)
    up_all = lax.all_gather(w_up, "fsdp", axis=1, tiled=True)
    for _ in range(2, half):
        token_ring.advance()
    w_t = w_all[:, : 3 * columns].T
    all_gains = w_all[:, 3 * columns : 3 * columns + 4].astype(jnp.float32).T
    gain_attn, gain_ffn = all_gains[0], all_gains[3]
    gain_query = lax.dynamic_slice_in_dim(all_gains[1], me * columns, columns)[:, None]
    gain_key = lax.dynamic_slice_in_dim(all_gains[2], me * columns, columns)[:, None]

    owners = owner(jnp.arange(contexts, dtype=jnp.int32))
    routing = pieces[:, :, 3 * columns + 4 : 3 * columns + 4 + routing_columns]
    routing = routing.reshape(contexts, 4, local_experts, 1, rows)[owners].astype(jnp.float32)
    all_ranks = (16.0 * routing[:, 0] + routing[:, 1]).astype(jnp.int32)
    all_gates = routing[:, 2] + routing[:, 3]

    lengths_in = cont_lengths[0]
    token_index = jnp.arange(total, dtype=jnp.int32)
    _, position = places(token_index, lengths_in, prompt_rows)
    starts = prompt_rows + jnp.cumsum(lengths_in) - lengths_in
    frequency = ROPE_BASE ** (-jnp.arange(HEAD // 2).astype(jnp.float32) / (HEAD // 2))
    angles = frequency[:, None] * position.astype(jnp.float32)[None, :]
    cosine, sine = jnp.cos(angles), jnp.sin(angles)

    def project_all(offsets, made):
        blocks = [token_ring.blocks[offset] for offset in offsets]
        places_of = owner(jnp.asarray(offsets, jnp.int32))
        return project(places_of, blocks, rows, w_t, gain_attn[None], made, total)

    made = project_all([0] + others[: 2 * (half - 2)], None)
    token_ring.advance(made[-1], up_all, gate_all)
    made = project_all(others[2 * (half - 2) : -1], made)
    token_ring.blocks[half] = after(token_ring.blocks[half], made[-1])
    made = project_all(others[-1:], made)
    hidden_all, query_pre, key_pre, value_t, squares = made
    w_out_rows = place_rows(
        after(owners, made[-1]), [token_ring.blocks[k if k <= half else k - contexts] for k in range(contexts)], rows, own_rows
    )
    out_all = lax.all_gather(w_out_rows, "fsdp", axis=1, tiled=True).reshape(width, width)
    down_all = lax.all_gather(w_down, "fsdp", axis=1, tiled=True)

    squares = sum_over_ctx(squares, contexts)
    inverse = lax.rsqrt(squares / width + EPSILON)
    query_inv, key_inv = inverse[0:1], inverse[1:2]
    grad_ring = RingGather(cotangent[0], ring)
    grad_ring.advance(squares)

    attended, query, key, key_t, log_rows = attend_forward(
        starts, query_pre, key_pre, value_t, query_inv, key_inv, gain_query, gain_key, cosine, sine, size, prompt_rows, score_scale
    )
    sent = after(attended, grad_ring.from_before, grad_ring.from_after)
    back = lax.all_to_all(
        sent.reshape(contexts, rows, columns), "ctx", split_axis=0, concat_axis=0, tiled=True
    )
    grad_ring.advance(attended)
    own_attended = jnp.transpose(back, (1, 0, 2)).reshape(rows, width)
    inputs = tokens[0].astype(jnp.float32)
    mixed = inputs + jnp.dot(own_attended, out_all, preferred_element_type=jnp.float32)
    mixed_inv = lax.rsqrt(jnp.mean(mixed * mixed, axis=-1, keepdims=True) + EPSILON)
    second = (mixed * mixed_inv * gain_ffn).astype(jnp.bfloat16)

    second_ring = RingGather(second, ring)
    weights = (gate_all, up_all, down_all)

    def stage_info(offsets):
        ranks = jnp.stack([all_ranks[k] for k in offsets])
        stage_gates = jnp.stack([all_gates[k] for k in offsets])
        if len(offsets) == 2:
            return ranks, stage_gates, offsets[1] - 1
        return ranks, stage_gates, contexts - (2 if offsets[0] == 0 else 1)

    stages = [(0,)] + [(-step, step) for step in range(1, half)] + [(half,)]
    infos = [stage_info(stage) for stage in stages]
    result_terms, second_terms, slopes = {}, {}, {}
    kept = kept_grads = None

    def forward(step, *earlier):
        nonlocal kept
        ranks, stage_gates, at = infos[step]
        ranks = after(ranks, *earlier) if earlier else ranks
        blocks = [second_ring.blocks[k] for k in stages[step]]
        made = experts_stage(
            True, ranks, stage_gates, blocks, weights, (), kept, at, slots, all_slots
        )
        kept, slopes[step], terms = made[:2], made[2:4], made[4:]
        result_terms.update(zip(stages[step], terms))
        return terms[0]

    def backward(step, *earlier, light=False):
        nonlocal kept_grads
        ranks, stage_gates, at = infos[step]
        ranks = after(ranks, *earlier) if earlier else ranks
        blocks = [grad_ring.blocks[k] for k in stages[step]]
        made = experts_stage(
            False,
            ranks,
            stage_gates,
            blocks,
            weights,
            slopes[step],
            kept_grads,
            at,
            slots,
            all_slots,
            light,
        )
        kept_grads, terms = made[:3], made[3:]
        second_terms.update(zip(stages[step], terms))
        return terms[0]

    def weight_grad(left, right):
        return jnp.einsum("emd,emf->edf", left, right, preferred_element_type=jnp.float32).astype(
            jnp.bfloat16
        )

    second_ring.advance()
    grad_second = (grad_ring.from_before, grad_ring.from_after)
    done = forward(0)
    done = backward(0, done, *grad_second, light=True)
    for step in range(1, half):
        near = [second_ring.blocks[k] for k in stages[step]]
        second_ring.advance(done)
        waits = (done,)
        if step > 1:
            waits += (grad_ring.from_before, grad_ring.from_after)
        if step in (1, half - 1):
            grad_ring.advance(done, *near)
        done = forward(step, *waits)
        if step < half - 2:
            done = backward(step, done, light=True)
    done = forward(half, done)

    second_sum, result_sum = RingScatter(ring), RingScatter(ring)
    result_sum.advance(result_terms)
    backward(half, done)
    sent = second_sum.advance(second_terms, result_sum.to_before, result_sum.to_after)
    backward(half - 1, *sent)
    sent = second_sum.advance(second_terms)
    backward(half - 2, *sent)
    sent = second_sum.advance(second_terms)
    rows_taken, active = kept
    route_grad, gate_grad, up_grad = kept_grads
    gate_product = weight_grad(after(rows_taken, *sent), gate_grad)
    sent = second_sum.advance(second_terms, gate_product)
    result_sum.prepare(result_terms, *sent)
    up_product = weight_grad(after(rows_taken, *result_sum.payload), up_grad)
    second_grad = second_sum.finish(after(second_terms[0], up_product))

    def fsdp_sum_low(product):
        return lax.psum_scatter(product, "fsdp", scatter_dimension=1, tiled=True)


    upstream = cotangent[0].astype(jnp.float32)
    mixed_normed = mixed * mixed_inv
    ffn_gain_grad = jnp.sum(second_grad * mixed_normed, axis=0)
    scaled = second_grad * gain_ffn
    mixed_grad = upstream + mixed_inv * (
        scaled - mixed_normed * jnp.mean(scaled * mixed_normed, axis=-1, keepdims=True)
    )
    branch = mixed_grad.astype(jnp.bfloat16)
    out_grad = out_grad_of(branch, out_all, contexts)
    w_out_grad = lax.dot_general(
        own_attended, after(branch, out_grad), (((0,), (0,)), ((), ())), preferred_element_type=jnp.float32
    ).astype(jnp.bfloat16)
    out_grad = lax.all_to_all(out_grad, "ctx", split_axis=0, concat_axis=0, tiled=True)
    out_grad = out_grad.reshape(total, columns)
    w_out_grad = fsdp_sum_low(
        after(w_out_grad, out_grad).reshape(contexts, splits * own_rows, width)
    )
    gate_w_grad = fsdp_sum_low(after(gate_product, out_grad))
    up_w_grad = fsdp_sum_low(after(up_product, out_grad))

    log_rows = log_rows.reshape(columns // HEAD, 1, total)
    held, dots, waits = None, 0.0, (out_grad,)
    for head in range(columns // HEAD):
        if head == 1:
            result_sum.prepare(result_terms, dots)
            waits = result_sum.payload
        if head < 2:
            result_sum.send(out_grad)
        *held, part = attend_backward(
            after(starts, *waits), head, held, query, key, key_t, value_t, out_grad, attended, log_rows, query_pre, key_pre, query_inv, key_inv, gain_query, gain_key, cosine, sine, size, prompt_rows, score_scale
        )
        dots = dots + part
    query_scaled, key_scaled, value_grad, query_gain_grad, key_gain_grad = held
    dots = after(dots, result_sum.to_before, result_sum.to_after)
    result_sum.prepare(result_terms, dots)
    dots = sum_over_ctx(dots, contexts) / width
    dots = after(dots, *result_sum.payload)
    heads_grad = heads_grad_of(
        query_scaled, key_scaled, value_grad, query_pre, key_pre, inverse, dots
    )

    def own_columns(grad):
        return lax.dynamic_update_slice_in_dim(
            jnp.zeros((width, 1), jnp.float32), grad, me * columns, 0
        )

    other_grads = jnp.concatenate(
        [
            ffn_gain_grad[:, None],
            own_columns(query_gain_grad),
            own_columns(key_gain_grad),
            jnp.zeros((width, 125), jnp.float32),
        ],
        axis=1,
    )
    def term(offset, *earlier, **got):
        at = after(owner(offset)[None], *earlier)
        return hidden_term(at, heads_grad, w_t, w_out_grad, rows, **got)

    result_sum.send(dots)
    hidden_sum = RingScatter(ring)
    hidden_sum.payload = far = term(half)
    hidden_sum.send()
    heads_product = heads_product_of(
        heads_grad, hidden_all, after(other_grads, *far), contexts
    )
    heads_w_grad = fsdp_sum_low(after(heads_product, hidden_sum.to_before, hidden_sum.to_after))
    done = (result_sum.to_before, result_sum.to_after)
    for step in range(half - 1, 0, -1):
        start = far[0].shape[0] if step == half - 1 else 0
        if step == half - 2:
            done = (heads_product, down_product, gate_w_grad)
        if step == 1:
            done = (heads_w_grad, up_w_grad)
        hidden_sum.payload = sent = (
            term(-step, *done, got=hidden_sum.to_before),
            term(step, *done, got=hidden_sum.to_after, start=start),
        )
        hidden_sum.send()
        if step == half - 1:
            down_product = weight_grad(after(active, *sent), route_grad)
            down_w_grad = fsdp_sum_low(down_product)
            heads_w_grad = lax.all_to_all(
                heads_w_grad, "ctx", split_axis=0, concat_axis=0, tiled=True
            )
        done = ()
    input_grad = input_grad_of(
        owner(0)[None],
        heads_grad,
        w_t,
        hidden_sum.to_before,
        hidden_sum.to_after,
        tokens[0],
        gain_attn[None],
        mixed_grad,
    )
    w_out_grad = (
        lax.dynamic_index_in_dim(w_out_grad, me, 0, keepdims=False).astype(jnp.float32)
        + hidden_sum.to_before[rows:].astype(jnp.float32)
        + hidden_sum.to_after[rows:].astype(jnp.float32)
    )
    routed = result_sum.finish(result_terms[0])
    output = (mixed + routed)[None]

    heads_w_grad = heads_w_grad.astype(jnp.float32)
    other_grads = jnp.sum(heads_w_grad[:, :, 3 * columns : 3 * columns + 3], axis=0)
    heads_w_grad = jnp.transpose(
        heads_w_grad[:, :, : 3 * columns].reshape(contexts, own_rows, 3, columns), (2, 1, 0, 3)
    ).reshape(3, own_rows, width)

    attn_gain_grad = jnp.sum(
        w_query.astype(jnp.float32) * heads_w_grad[0]
        + w_key.astype(jnp.float32) * heads_w_grad[1]
        + w_value.astype(jnp.float32) * heads_w_grad[2],
        axis=1,
    ) / attn_gain.astype(jnp.float32)

    return (
        output,
        input_grad[None],
        attn_gain_grad,
        other_grads[:, 1],
        other_grads[:, 2],
        other_grads[:, 0],
        heads_w_grad[0],
        heads_w_grad[1],
        heads_w_grad[2],
        w_out_grad,
        gate_w_grad.astype(jnp.float32),
        up_w_grad.astype(jnp.float32),
        down_w_grad.astype(jnp.float32),
    )


def solution(mesh):
    contexts = mesh.shape["ctx"]
    fits = contexts == 8
    placed = (
        P("fsdp", "ctx", None),
        P("fsdp", "ctx", None),
        P("fsdp", None),
        P("fsdp", "ctx", None),
        P("fsdp", "ctx", None),
        P(("ctx", "fsdp")),
        P(("ctx", "fsdp")),
        P(("ctx", "fsdp")),
        P(("ctx", "fsdp")),
        P(("ctx", "fsdp"), None),
        P(("ctx", "fsdp"), None),
        P(("ctx", "fsdp"), None),
        P(("ctx", "fsdp"), None),
        P("ctx", "fsdp", None),
        P("ctx", "fsdp", None),
        P("ctx", "fsdp", None),
    )
    return jax.shard_map(
        shards_by_heads if fits else shards_wide,
        mesh=mesh,
        in_specs=placed,
        out_specs=(
            P("fsdp", "ctx", None),
            P("fsdp", "ctx", None),
            P(("ctx", "fsdp")),
            P(("ctx", "fsdp")),
            P(("ctx", "fsdp")),
            P(("ctx", "fsdp")),
            P(("ctx", "fsdp"), None),
            P(("ctx", "fsdp"), None),
            P(("ctx", "fsdp"), None),
            P(("ctx", "fsdp"), None),
            P("ctx", "fsdp", None),
            P("ctx", "fsdp", None),
            P("ctx", "fsdp", None),
        ),
        check_vma=False,
    )
```

```python
from functools import partial

import jax
import jax.numpy as jnp
from jax import lax
from jax.experimental import pallas as pl
from jax.experimental.pallas import tpu as pltpu
from jax.sharding import PartitionSpec as P

HEAD = 128


EPSILON = 1e-05
ROPE_BASE = 10000.0
MASKED = -1e30


def norm_rows(values_in, gain_in):
    return (
        values_in
        * lax.rsqrt(jnp.mean(values_in * values_in, axis=-1, keepdims=True) + EPSILON)
        * gain_in
    )


def places(token_index, lengths_in, prompt_rows):
    ends = prompt_rows + jnp.cumsum(lengths_in)
    passed = (token_index[:, None] >= ends[None, :]).astype(jnp.int32)
    before = jnp.sum(passed * lengths_in[None, :], axis=1)
    inside = token_index >= prompt_rows
    segment = jnp.where(inside, 1 + jnp.sum(passed, axis=1), 0)
    position = jnp.where(inside, token_index - before, token_index)
    return (segment, position)


def rotate(values_in, positions):
    full_shape = values_in.shape
    per_head = values_in.reshape(full_shape[:-1] + (full_shape[-1] // HEAD, HEAD))
    half_dim = HEAD // 2
    frequency = ROPE_BASE ** (-jnp.arange(half_dim).astype(values_in.dtype) / half_dim)
    angles = positions.astype(values_in.dtype)[..., None] * frequency
    cosine = jnp.cos(angles)[..., None, :]
    sine = jnp.sin(angles)[..., None, :]
    former = per_head[..., :half_dim]
    latter = per_head[..., half_dim:]
    turned = jnp.concatenate(
        [former * cosine - latter * sine, latter * cosine + former * sine], axis=-1
    )
    return turned.reshape(full_shape)


def allowed_pairs(query_index, query_seg, key_index, key_seg):
    return (key_index[None, :] <= query_index[:, None]) & (
        (key_seg[None, :] == 0) | (key_seg[None, :] == query_seg[:, None])
    )


def attend_fold(
    state_in,
    shard_piece,
    first_row,
    query_heads,
    own_index,
    own_seg,
    lengths_in,
    prompt_rows,
    score_scale,
):
    highest, denominator, weighted = state_in
    key_rows, value_rows = shard_piece
    piece_count = key_rows.shape[0]
    key_index = jnp.arange(piece_count, dtype=jnp.int32)
    key_seg, _ = places(key_index, lengths_in, prompt_rows)
    key_heads = key_rows.reshape(piece_count, -1, HEAD)
    value_heads = value_rows.reshape(piece_count, -1, HEAD)
    scores = (
        jnp.einsum("qhd,khd->hqk", query_heads, key_heads, preferred_element_type=jnp.float32)
        * score_scale
    )
    allowed = allowed_pairs(own_index, own_seg, key_index, key_seg)
    masked = jnp.where(allowed[None], scores, MASKED)
    new_high = jnp.maximum(highest, jnp.max(masked, axis=-1))
    shrink = jnp.exp(highest - new_high)
    unnormed = jnp.where(allowed[None], jnp.exp(masked - new_high[..., None]), 0.0)
    denominator = jnp.sum(unnormed, axis=-1)
    weighted = jnp.einsum(
        "hqk,khd->hqd",
        unnormed.astype(jnp.bfloat16),
        value_heads,
        preferred_element_type=jnp.float32,
    )
    return (new_high, denominator, weighted)


def pair_terms(
    query_heads,
    grad_heads,
    log_rows,
    dot_rows,
    query_index,
    query_seg,
    key_heads,
    value_heads,
    key_index,
    key_seg,
    score_scale,
):
    scores = (
        jnp.einsum("qhd,khd->hqk", query_heads, key_heads, preferred_element_type=jnp.float32)
        * score_scale
    )
    allowed = allowed_pairs(query_index, query_seg, key_index, key_seg)
    prob = jnp.where(
        allowed[None], jnp.exp(jnp.where(allowed[None], scores, MASKED) - log_rows[..., None]), 0.0
    )
    prob_grad = jnp.einsum(
        "qhd,khd->hqk", grad_heads, value_heads, preferred_element_type=jnp.float32
    )
    score_grad = (prob * (prob_grad - dot_rows[..., None])).astype(jnp.bfloat16)
    return (prob, score_grad)


def slot_targets(route_list, expert_total, capacity):
    onehot = (route_list[:, None] == jnp.arange(expert_total, dtype=jnp.int32)[None, :]).astype(
        jnp.int32
    )
    slot_rank = jnp.sum((jnp.cumsum(onehot, axis=0) - 1) * onehot, axis=1)
    return route_list * capacity + slot_rank


def shards_wide(
    tokens,
    cotangent,
    cont_lengths,
    routes,
    gates,
    attn_gain,
    query_gain,
    key_gain,
    ffn_gain,
    w_query,
    w_key,
    w_value,
    w_out,
    w_gate,
    w_up,
    w_down,
):
    row_count = tokens.shape[1]
    model_width = tokens.shape[2]
    route_count = routes.shape[2]
    context_size = lax.axis_size("ctx")
    all_rows = row_count * context_size
    prompt_rows = all_rows // 2
    local_experts = w_gate.shape[0]
    expert_total = local_experts * context_size
    capacity = max(2, row_count * route_count * 5 // (4 * expert_total))
    head_count = model_width // HEAD
    score_scale = HEAD ** (-0.5)
    lengths_in = cont_lengths[0]
    own_index = lax.axis_index("ctx") * row_count + jnp.arange(row_count, dtype=jnp.int32)
    own_seg, own_pos = places(own_index, lengths_in, prompt_rows)
    attention_set = (
        lax.all_gather(w_query, ("ctx", "fsdp"), axis=0, tiled=True),
        lax.all_gather(w_key, ("ctx", "fsdp"), axis=0, tiled=True),
        lax.all_gather(w_value, ("ctx", "fsdp"), axis=0, tiled=True),
        lax.all_gather(w_out, ("ctx", "fsdp"), axis=0, tiled=True),
        lax.all_gather(attn_gain, ("ctx", "fsdp"), axis=0, tiled=True),
        lax.all_gather(query_gain, ("ctx", "fsdp"), axis=0, tiled=True),
        lax.all_gather(key_gain, ("ctx", "fsdp"), axis=0, tiled=True),
        lax.all_gather(ffn_gain, ("ctx", "fsdp"), axis=0, tiled=True),
    )
    query_all, key_all, value_all, out_all = (
        attention_set[0],
        attention_set[1],
        attention_set[2],
        attention_set[3],
    )
    gain_attn = attention_set[4].astype(jnp.float32)
    gain_query = attention_set[5].astype(jnp.float32)
    gain_key = attention_set[6].astype(jnp.float32)
    gain_ffn = attention_set[7].astype(jnp.float32)
    expert_set = (
        lax.all_gather(w_gate, "fsdp", axis=1, tiled=True),
        lax.all_gather(w_up, "fsdp", axis=1, tiled=True),
        lax.all_gather(w_down, "fsdp", axis=1, tiled=True),
    )
    gate_all, up_all, down_all = expert_set
    inputs = tokens[0].astype(jnp.float32)
    normed, attn_pull = jax.vjp(norm_rows, inputs, gain_attn)
    hidden = normed.astype(jnp.bfloat16)
    query_pre = jnp.dot(hidden, query_all, preferred_element_type=jnp.float32)
    key_pre = jnp.dot(hidden, key_all, preferred_element_type=jnp.float32)
    values = jnp.dot(hidden, value_all, preferred_element_type=jnp.float32).astype(jnp.bfloat16)
    query_rot, query_pull = jax.vjp(
        lambda pre_in, gain_in: rotate(norm_rows(pre_in, gain_in), own_pos), query_pre, gain_query
    )
    key_rot, key_pull = jax.vjp(
        lambda pre_in, gain_in: rotate(norm_rows(pre_in, gain_in), own_pos), key_pre, gain_key
    )
    query_low = query_rot.astype(jnp.bfloat16)
    key_low = key_rot.astype(jnp.bfloat16)
    query_heads = query_low.reshape(row_count, head_count, HEAD)
    folder = partial(
        attend_fold,
        query_heads=query_heads,
        own_index=own_index,
        own_seg=own_seg,
        lengths_in=lengths_in,
        prompt_rows=prompt_rows,
        score_scale=score_scale,
    )
    start_state = (
        jnp.full((head_count, row_count), MASKED, jnp.float32),
        jnp.zeros((head_count, row_count), jnp.float32),
        jnp.zeros((head_count, row_count, HEAD), jnp.float32),
    )
    final_state = folder(
        start_state,
        (
            lax.all_gather(key_low, "ctx", axis=0, tiled=True),
            lax.all_gather(values, "ctx", axis=0, tiled=True),
        ),
        jnp.int32(0),
    )
    highest, denominator, weighted = final_state
    log_total = highest + jnp.log(denominator)
    attn_heads = jnp.transpose(weighted / denominator[..., None], (1, 0, 2))
    attended = attn_heads.reshape(row_count, model_width).astype(jnp.bfloat16)
    mixed = inputs + jnp.dot(attended, out_all, preferred_element_type=jnp.float32)
    normed_second, ffn_pull = jax.vjp(norm_rows, mixed, gain_ffn)
    second = normed_second.astype(jnp.bfloat16)
    route_list = routes[0].reshape(-1)
    targets = slot_targets(route_list, expert_total, capacity)

    def dispatch_rows(route_rows):
        buffer = (
            jnp.zeros((expert_total * capacity, model_width), jnp.bfloat16)
            .at[targets]
            .set(route_rows)
        )
        return buffer.reshape(context_size, local_experts * capacity, model_width)

    sent_rows = dispatch_rows(jnp.repeat(second, route_count, axis=0))
    arrived = lax.all_to_all(sent_rows, "ctx", split_axis=0, concat_axis=0, tiled=True).reshape(
        context_size, local_experts, capacity, model_width
    )
    gate_pre = jnp.einsum("sekd,edf->sekf", arrived, gate_all, preferred_element_type=jnp.float32)
    up_pre = jnp.einsum("sekd,edf->sekf", arrived, up_all, preferred_element_type=jnp.float32)
    active = (jax.nn.silu(gate_pre) * up_pre).astype(jnp.bfloat16)
    expert_out = jnp.einsum(
        "sekf,efd->sekd", active, down_all, preferred_element_type=jnp.float32
    ).astype(jnp.bfloat16)
    returned = lax.all_to_all(
        expert_out.reshape(context_size, local_experts * capacity, model_width),
        "ctx",
        split_axis=0,
        concat_axis=0,
        tiled=True,
    )
    per_route = (
        returned.reshape(expert_total * capacity, model_width)[targets]
        .astype(jnp.float32)
        .reshape(row_count, route_count, model_width)
    )
    gate_values = gates[0]
    result = mixed + jnp.sum(gate_values[..., None] * per_route, axis=1)
    output = result[None]
    upstream = cotangent[0].astype(jnp.float32)
    route_grad = (
        (gate_values[..., None] * upstream[:, None, :])
        .astype(jnp.bfloat16)
        .reshape(row_count * route_count, model_width)
    )
    grad_arrived = lax.all_to_all(
        dispatch_rows(route_grad), "ctx", split_axis=0, concat_axis=0, tiled=True
    ).reshape(context_size, local_experts, capacity, model_width)
    active_grad = jnp.einsum(
        "sekd,efd->sekf", grad_arrived, down_all, preferred_element_type=jnp.float32
    )
    down_w_grad = jnp.einsum(
        "sekf,sekd->efd", active, grad_arrived, preferred_element_type=jnp.float32
    )
    sigmoid_gate = jax.nn.sigmoid(gate_pre)
    gate_grad = (
        active_grad * up_pre * sigmoid_gate * (1.0 + gate_pre * (1.0 - sigmoid_gate))
    ).astype(jnp.bfloat16)
    up_grad = (active_grad * gate_pre * sigmoid_gate).astype(jnp.bfloat16)
    gate_w_grad = jnp.einsum(
        "sekd,sekf->edf", arrived, gate_grad, preferred_element_type=jnp.float32
    )
    up_w_grad = jnp.einsum("sekd,sekf->edf", arrived, up_grad, preferred_element_type=jnp.float32)
    arrived_grad = jnp.einsum(
        "sekf,edf->sekd", gate_grad, gate_all, preferred_element_type=jnp.float32
    )
    arrived_grad = (
        arrived_grad
        + jnp.einsum("sekf,edf->sekd", up_grad, up_all, preferred_element_type=jnp.float32)
    ).astype(jnp.bfloat16)
    grad_back = lax.all_to_all(
        arrived_grad.reshape(context_size, local_experts * capacity, model_width),
        "ctx",
        split_axis=0,
        concat_axis=0,
        tiled=True,
    )
    second_grad = jnp.sum(
        grad_back.reshape(expert_total * capacity, model_width)[targets]
        .astype(jnp.float32)
        .reshape(row_count, route_count, model_width),
        axis=1,
    )
    expert_grads = (
        lax.psum_scatter(
            gate_w_grad.astype(jnp.bfloat16), "fsdp", scatter_dimension=1, tiled=True
        ).astype(jnp.float32),
        lax.psum_scatter(
            up_w_grad.astype(jnp.bfloat16), "fsdp", scatter_dimension=1, tiled=True
        ).astype(jnp.float32),
        lax.psum_scatter(
            down_w_grad.astype(jnp.bfloat16), "fsdp", scatter_dimension=1, tiled=True
        ).astype(jnp.float32),
    )
    mixed_norm_grad, ffn_gain_grad = ffn_pull(second_grad)
    mixed_grad = upstream + mixed_norm_grad
    branch_grad = mixed_grad.astype(jnp.bfloat16)
    out_w_grad = jnp.dot(attended.T, branch_grad, preferred_element_type=jnp.float32)
    attended_grad = jnp.dot(branch_grad, out_all.T, preferred_element_type=jnp.float32).astype(
        jnp.bfloat16
    )
    grad_heads = attended_grad.reshape(row_count, head_count, HEAD)
    row_dot = jnp.transpose(jnp.sum(grad_heads.astype(jnp.float32) * attn_heads, axis=-1))
    keys_whole, values_whole = (
        lax.all_gather(key_low, "ctx", axis=0, tiled=True),
        lax.all_gather(values, "ctx", axis=0, tiled=True),
    )
    block_rows = min(1024, all_rows)
    block_count = all_rows // block_rows
    block_index = jnp.arange(all_rows, dtype=jnp.int32).reshape(block_count, block_rows)
    key_blocks = keys_whole.reshape(block_count, block_rows, model_width)
    value_blocks = values_whole.reshape(block_count, block_rows, model_width)

    def query_side(key_rows, value_rows, key_index):
        key_seg, _ = places(key_index, lengths_in, prompt_rows)
        key_heads = key_rows.reshape(block_rows, head_count, HEAD)
        value_heads = value_rows.reshape(block_rows, head_count, HEAD)
        prob, score_grad = pair_terms(
            query_heads,
            grad_heads,
            log_total,
            row_dot,
            own_index,
            own_seg,
            key_heads,
            value_heads,
            key_index,
            key_seg,
            score_scale,
        )
        query_term = (
            jnp.einsum("hqk,khd->qhd", score_grad, key_heads, preferred_element_type=jnp.float32)
            * score_scale
        )
        return (prob, score_grad, query_term)

    def back_block(query_grad, block_args):
        key_rows, value_rows, key_index = block_args
        prob, score_grad, query_term = query_side(key_rows, value_rows, key_index)
        key_term = (
            jnp.einsum("hqk,qhd->khd", score_grad, query_heads, preferred_element_type=jnp.float32)
            * score_scale
        )
        value_term = jnp.einsum(
            "hqk,qhd->khd",
            prob.astype(jnp.bfloat16),
            grad_heads,
            preferred_element_type=jnp.float32,
        )
        return (
            query_grad + query_term,
            (
                key_term.reshape(block_rows, model_width),
                value_term.reshape(block_rows, model_width),
            ),
        )

    query_grad, (key_terms, value_terms) = lax.scan(
        back_block,
        jnp.zeros((row_count, head_count, HEAD), jnp.float32),
        (key_blocks, value_blocks, block_index),
    )
    key_grad, value_grad = (
        lax.psum_scatter(
            key_terms.reshape(all_rows, model_width).astype(jnp.bfloat16),
            "ctx",
            scatter_dimension=0,
            tiled=True,
        ).astype(jnp.float32),
        lax.psum_scatter(
            value_terms.reshape(all_rows, model_width).astype(jnp.bfloat16),
            "ctx",
            scatter_dimension=0,
            tiled=True,
        ).astype(jnp.float32),
    )
    query_pre_grad, query_gain_grad = query_pull(query_grad.reshape(row_count, model_width))
    key_pre_grad, key_gain_grad = key_pull(key_grad)
    query_low_grad = query_pre_grad.astype(jnp.bfloat16)
    key_low_grad = key_pre_grad.astype(jnp.bfloat16)
    value_low_grad = value_grad.astype(jnp.bfloat16)
    query_w_grad = jnp.dot(hidden.T, query_low_grad, preferred_element_type=jnp.float32)
    key_w_grad = jnp.dot(hidden.T, key_low_grad, preferred_element_type=jnp.float32)
    value_w_grad = jnp.dot(hidden.T, value_low_grad, preferred_element_type=jnp.float32)
    hidden_grad = jnp.dot(query_low_grad, query_all.T, preferred_element_type=jnp.float32)
    hidden_grad = hidden_grad + jnp.dot(key_low_grad, key_all.T, preferred_element_type=jnp.float32)
    hidden_grad = hidden_grad + jnp.dot(
        value_low_grad, value_all.T, preferred_element_type=jnp.float32
    )
    input_norm_grad, attn_gain_grad = attn_pull(hidden_grad)
    input_grad = (mixed_grad + input_norm_grad)[None]
    summed_grads = (
        lax.psum_scatter(query_w_grad, ("ctx", "fsdp"), scatter_dimension=0, tiled=True),
        lax.psum_scatter(key_w_grad, ("ctx", "fsdp"), scatter_dimension=0, tiled=True),
        lax.psum_scatter(value_w_grad, ("ctx", "fsdp"), scatter_dimension=0, tiled=True),
        lax.psum_scatter(out_w_grad, ("ctx", "fsdp"), scatter_dimension=0, tiled=True),
        lax.psum_scatter(attn_gain_grad, ("ctx", "fsdp"), scatter_dimension=0, tiled=True),
        lax.psum_scatter(query_gain_grad, ("ctx", "fsdp"), scatter_dimension=0, tiled=True),
        lax.psum_scatter(key_gain_grad, ("ctx", "fsdp"), scatter_dimension=0, tiled=True),
        lax.psum_scatter(ffn_gain_grad, ("ctx", "fsdp"), scatter_dimension=0, tiled=True),
    )
    return (
        output,
        input_grad,
        summed_grads[4],
        summed_grads[5],
        summed_grads[6],
        summed_grads[7],
        summed_grads[0],
        summed_grads[1],
        summed_grads[2],
        summed_grads[3],
        expert_grads[0],
        expert_grads[1],
        expert_grads[2],
    )


HEADS = 16
LOG2E = 1.4426950408889634
VMEM_BYTES = 60 * 2**20


def dot_nn(left, right):
    return lax.dot_general(
        left, right, (((1,), (0,)), ((), ())), preferred_element_type=jnp.float32
    )


def dot_nt(left, right):
    return lax.dot_general(
        left, right, (((1,), (1,)), ((), ())), preferred_element_type=jnp.float32
    )


def dot_tn(left, right):
    return lax.dot_general(
        left, right, (((0,), (0,)), ((), ())), preferred_element_type=jnp.float32
    )


def segment_start(starts, index):
    first = starts[0]
    for c in range(1, starts.shape[0]):
        first = jnp.where(index >= starts[c], starts[c], first)
    return first


def segment_end(starts, index, total):
    last = jnp.int32(total)
    for c in range(starts.shape[0] - 1, 0, -1):
        last = jnp.where(index < starts[c], starts[c], last)
    return last


def allowed_tile(starts, key_first, query_first, size, prompt_rows):
    key_index = key_first + lax.broadcasted_iota(jnp.int32, (size, size), 0)
    query_index = query_first + lax.broadcasted_iota(jnp.int32, (1, size), 1)
    own_start = jnp.full((1, size), prompt_rows, jnp.int32)
    for c in range(1, starts.shape[0]):
        own_start = jnp.where(query_index >= starts[c], starts[c], own_start)
    return (key_index <= query_index) & ((key_index < prompt_rows) | (key_index >= own_start))


def attend_forward_kernel(
    starts,
    query_pre,
    key_pre,
    value_t,
    query_inv,
    key_inv,
    query_gain,
    key_gain,
    cosine,
    sine,
    out,
    query,
    key,
    key_t,
    log_rows,
    *,
    size,
    prompt_rows,
    score_scale,
):
    i = pl.program_id(0)
    half = HEAD // 2
    total, columns = key.shape
    spans = [slice(h * HEAD, (h + 1) * HEAD) for h in range(columns // HEAD)]
    prompt_blocks = prompt_rows // size

    @pl.when(i == 0)
    def _():
        @pl.loop(0, total // size)
        def _(b):
            at = pl.ds(pl.multiple_of(b * size, size), size)
            cos, sin = cosine[:, at], sine[:, at]
            for span in spans:
                for pre, inv, gain, is_key in (
                    (query_pre, query_inv, query_gain, False),
                    (key_pre, key_inv, key_gain, True),
                ):
                    normed = pre[span, at] * inv[:, at] * gain[span, :]
                    former, latter = normed[:half], normed[half:]
                    turned = jnp.concatenate(
                        [former * cos - latter * sin, latter * cos + former * sin], axis=0
                    )
                    if is_key:
                        key_t[span, at] = turned.astype(jnp.bfloat16)
                        key[at, span] = turned.T.astype(jnp.bfloat16)
                    else:
                        turned = turned * (score_scale * LOG2E)
                        query[at, span] = turned.T.astype(jnp.bfloat16)

    query_first = i * size
    here = pl.ds(pl.multiple_of(query_first, size), size)
    chunk = size // 2
    parts = [slice(c * chunk, (c + 1) * chunk) for c in range(2)]
    work = [(span, part) for span in spans for part in parts]
    query_all = [query[here, span] for span in spans]
    query_rows = [rows[part] for rows in query_all for part in parts]

    def fold(j, states, masked):
        at = pl.ds(pl.multiple_of(j * size, size), size)
        scores = [dot_nt(key[at, span], rows) for (span, _), rows in zip(work, query_rows)]
        if masked:
            allowed = allowed_tile(starts, j * size, query_first, size, prompt_rows)
        made = []
        for (span, part), score, (highest, denominator, weighted) in zip(work, scores, states):
            if masked:
                score = jnp.where(allowed[:, part], score, MASKED)
            new_high = jnp.maximum(highest, jnp.max(score, axis=0, keepdims=True))
            shrink = jnp.exp2(highest - new_high)
            unnormed = jnp.exp2(score - new_high)
            denominator = denominator * shrink + jnp.sum(unnormed, axis=0, keepdims=True)
            weighted = weighted * shrink + dot_nn(value_t[span, at], unnormed.astype(jnp.bfloat16))
            made.append((new_high, denominator, weighted))
        return tuple(made)

    states = tuple(
        (
            jnp.full((1, chunk), MASKED, jnp.float32),
            jnp.zeros((1, chunk), jnp.float32),
            jnp.zeros((HEAD, chunk), jnp.float32),
        )
        for _ in work
    )
    in_prompt = i < prompt_blocks
    whole = jnp.where(in_prompt, i, prompt_blocks)
    states = lax.fori_loop(0, whole, lambda j, s: fold(j, s, False), states)
    own_first = jnp.where(in_prompt, i, segment_start(starts, query_first) // size)
    states = lax.fori_loop(own_first, i + 1, lambda j, s: fold(j, s, True), states)
    for k, ((span, part), (highest, denominator, weighted)) in enumerate(zip(work, states)):
        out[part, span] = (weighted / denominator).T.astype(jnp.bfloat16)
        log_rows[k // 2 : k // 2 + 1, part] = highest + jnp.log2(denominator)


def attend_forward(starts, query_pre, key_pre, value_t, query_inv, key_inv, query_gain, key_gain, cosine, sine, size, prompt_rows, score_scale):
    columns, total = query_pre.shape
    heads = columns // HEAD
    pairs = total * total // 2

    def once(shape):
        return pl.BlockSpec(shape, lambda i, s: (0, 0), pipeline_mode=pl.Buffered(1))

    wide, tall, row = (columns, total), (total, columns), (1, total)
    gain, table = (columns, 1), (HEAD // 2, total)
    return pl.pallas_call(
        partial(attend_forward_kernel, size=size, prompt_rows=prompt_rows, score_scale=score_scale),
        grid_spec=pltpu.PrefetchScalarGridSpec(
            num_scalar_prefetch=1,
            grid=(total // size,),
            in_specs=[once(k) for k in (wide, wide, wide, row, row, gain, gain, table, table)],
            out_specs=[
                pl.BlockSpec((size, columns), lambda i, s: (i, 0)),
                pl.BlockSpec(tall, lambda i, s: (0, 0)),
                pl.BlockSpec(tall, lambda i, s: (0, 0)),
                pl.BlockSpec(wide, lambda i, s: (0, 0)),
                pl.BlockSpec((heads, size), lambda i, s: (0, i)),
            ],
        ),
        out_shape=[
            jax.ShapeDtypeStruct(tall, jnp.bfloat16),
            jax.ShapeDtypeStruct(tall, jnp.bfloat16),
            jax.ShapeDtypeStruct(tall, jnp.bfloat16),
            jax.ShapeDtypeStruct(wide, jnp.bfloat16),
            jax.ShapeDtypeStruct((heads, total), jnp.float32),
        ],
        compiler_params=pltpu.CompilerParams(vmem_limit_bytes=VMEM_BYTES),
        cost_estimate=pl.CostEstimate(
            flops=12 * pairs * columns, bytes_accessed=20 * total * columns, transcendentals=pairs * heads
        ),
        name="attend_forward",
    )(starts, query_pre, key_pre, value_t, query_inv, key_inv, query_gain, key_gain, cosine, sine)


def attend_backward_kernel(
    starts,
    query,
    key,
    key_t,
    value_t,
    out_grad,
    out,
    log_rows,
    query_pre,
    key_pre,
    query_inv,
    key_inv,
    query_gain,
    key_gain,
    cosine,
    sine,
    *refs,
    size,
    prompt_rows,
    score_scale,
):
    query_scaled, key_scaled, value_grad, query_gain_grad, key_gain_grad, dots = refs[-9:-3]
    query_sum, key_sum, row_dot = refs[-3:]
    j = pl.program_id(0)
    half = HEAD // 2
    total, columns = key.shape
    spans = [slice(h * HEAD, (h + 1) * HEAD) for h in range(columns // HEAD)]
    blocks = total // size
    prompt_blocks = prompt_rows // size

    @pl.when(j == 0)
    def _():
        query_sum[...] = jnp.zeros_like(query_sum)

        @pl.loop(0, blocks)
        def _(b):
            at = pl.ds(pl.multiple_of(b * size, size), size)
            for h, span in enumerate(spans):
                product = out_grad[at, span].astype(jnp.float32) * out[at, span].astype(jnp.float32)
                row_dot[h : h + 1, at] = jnp.sum(product.T, axis=0, keepdims=True)

    chunk = size // 2
    here = pl.ds(pl.multiple_of(j * size, size), size)
    key_rows = [key[here, span] for span in spans]
    key_cols = [key_t[span, here] for span in spans]
    value_rows = [value_t[span, here].T for span in spans]

    def fold(i, states, masked):
        if masked:
            allowed = allowed_tile(starts, j * size, i * size, size, prompt_rows)
        made = list(states)
        for c in range(2):
            at = pl.ds(pl.multiple_of(i * size + c * chunk, chunk), chunk)
            query_rows = [query[at, span] for span in spans]
            grad_rows = [out_grad[at, span] for span in spans]
            scores = [dot_nt(k, q) for k, q in zip(key_rows, query_rows)]
            prob_grads = [dot_nt(v, g) for v, g in zip(value_rows, grad_rows)]
            for h, span in enumerate(spans):
                key_part, value_part = made[h]
                prob = jnp.exp2(scores[h] - log_rows[h, :, at])
                if masked:
                    prob = jnp.where(allowed[:, c * chunk : (c + 1) * chunk], prob, 0.0)
                score_grad = (prob * (prob_grads[h] - row_dot[h : h + 1, at])).astype(jnp.bfloat16)
                value_part = value_part + dot_nn(prob.astype(jnp.bfloat16), grad_rows[h])
                key_part = key_part + dot_nn(score_grad, query_rows[h])
                query_sum[span, at] += dot_nn(key_cols[h], score_grad)
                made[h] = (key_part, value_part)
        return tuple(made)

    states = tuple(
        (jnp.zeros((size, HEAD), jnp.float32), jnp.zeros((size, HEAD), jnp.float32)) for _ in spans
    )
    in_prompt = j < prompt_blocks
    last_own = (segment_end(starts, (j + 1) * size - 1, total) - 1) // size + 1
    masked_end = jnp.where(in_prompt, j + 1, last_own)
    states = lax.fori_loop(j, masked_end, lambda i, s: fold(i, s, True), states)
    whole_end = jnp.where(in_prompt, blocks, masked_end)
    states = lax.fori_loop(masked_end, whole_end, lambda i, s: fold(i, s, False), states)
    for span, (key_part, value_part) in zip(spans, states):
        key_sum[span, here] = key_part.T
        value_grad[span, here] = value_part.T.astype(jnp.bfloat16)

    @pl.when(j == blocks - 1)
    def _():
        query_gain_grad[...] = jnp.zeros_like(query_gain_grad)
        key_gain_grad[...] = jnp.zeros_like(key_gain_grad)

        @pl.loop(0, blocks)
        def _(b):
            at = pl.ds(pl.multiple_of(b * size, size), size)
            cos, sin = cosine[:, at], sine[:, at]
            for place, (grad, factor, pre, inv, gain, scaled, gain_grad) in enumerate(
                (
                    (query_sum, score_scale, query_pre, query_inv, query_gain, query_scaled, query_gain_grad),
                    (key_sum, 1.0 / LOG2E, key_pre, key_inv, key_gain, key_scaled, key_gain_grad),
                )
            ):
                summed = None
                for span in spans:
                    turned = grad[span, at] * factor
                    former, latter = turned[:half], turned[half:]
                    back = jnp.concatenate(
                        [former * cos + latter * sin, latter * cos - former * sin], axis=0
                    )
                    before = pre[span, at]
                    gain_grad[span, :] += jnp.sum(
                        back * (before * inv[:, at]), axis=1, keepdims=True
                    )
                    back = back * gain[span, :]
                    scaled[span, at] = back
                    dot = jnp.sum(back * before, axis=0, keepdims=True)
                    summed = dot if summed is None else summed + dot
                dots[place : place + 1, at] = summed


def attend_backward(starts, head, held, query, key, key_t, value_t, out_grad, out, log_rows, query_pre, key_pre, query_inv, key_inv, query_gain, key_gain, cosine, sine, size, prompt_rows, score_scale):
    columns, total = query_pre.shape
    pairs = total * total // 2
    held = () if held is None else tuple(held)

    def once(shape, index):
        return pl.BlockSpec(shape, lambda j, s: index, pipeline_mode=pl.Buffered(1))

    wide, tall = once((HEAD, total), (head, 0)), once((total, HEAD), (0, head))
    row, table = once((1, total), (0, 0)), once((HEAD // 2, total), (0, 0))
    gain, per_head = once((HEAD, 1), (head, 0)), once((1, 1, total), (head, 0, 0))
    return pl.pallas_call(
        partial(attend_backward_kernel, size=size, prompt_rows=prompt_rows, score_scale=score_scale),
        grid_spec=pltpu.PrefetchScalarGridSpec(
            num_scalar_prefetch=1,
            grid=(total // size,),
            in_specs=[tall, tall, wide, wide, tall, tall, per_head, wide, wide, row, row, gain, gain, table, table]
            + [pl.BlockSpec(memory_space=pl.ANY)] * len(held),
            out_specs=[wide, wide, wide, gain, gain, once((2, total), (0, 0))],
            scratch_shapes=[
                pltpu.VMEM((HEAD, total), jnp.float32),
                pltpu.VMEM((HEAD, total), jnp.float32),
                pltpu.VMEM((1, total), jnp.float32),
            ],
        ),
        out_shape=[
            jax.ShapeDtypeStruct((columns, total), jnp.float32),
            jax.ShapeDtypeStruct((columns, total), jnp.float32),
            jax.ShapeDtypeStruct((columns, total), jnp.bfloat16),
            jax.ShapeDtypeStruct((columns, 1), jnp.float32),
            jax.ShapeDtypeStruct((columns, 1), jnp.float32),
            jax.ShapeDtypeStruct((2, total), jnp.float32),
        ],
        input_output_aliases={16 + k: k for k in range(len(held))},
        compiler_params=pltpu.CompilerParams(vmem_limit_bytes=VMEM_BYTES),
        cost_estimate=pl.CostEstimate(
            flops=24 * pairs * HEAD, bytes_accessed=40 * total * HEAD, transcendentals=pairs
        ),
        name="attend_backward",
    )(starts, query, key, key_t, value_t, out_grad, out, log_rows, query_pre, key_pre, query_inv, key_inv, query_gain, key_gain, cosine, sine, *held)


def project_kernel(places, *refs, count):
    blocks = refs[:count]
    w_t, gain = refs[count : count + 2]
    hidden, query_pre, key_pre, value_t, squares = refs[-5:]
    columns = query_pre.shape[0]
    for b, block in enumerate(blocks):

        @pl.when(pl.program_id(0) // 2 == b)
        def _(block=block):
            rows = block[...].astype(jnp.float32)
            inverse = lax.rsqrt(jnp.mean(rows * rows, axis=-1, keepdims=True) + EPSILON)
            hidden[...] = (rows * inverse * gain[...]).astype(jnp.bfloat16)

    for k, out in enumerate((query_pre, key_pre)):
        made = dot_nt(w_t[k * columns : (k + 1) * columns, :], hidden[...])
        out[...] = made
        squares[k : k + 1, :] = jnp.sum(made * made, axis=0, keepdims=True)
    value_t[...] = dot_nt(w_t[2 * columns :, :], hidden[...]).astype(jnp.bfloat16)


def project(places, blocks, rows, w_t, gain, held, total):
    count, width = len(blocks), blocks[0].shape[1]
    columns = w_t.shape[0] // 3
    tile = rows // 2
    held = () if held is None else tuple(held)

    def block_spec(b):
        return pl.BlockSpec((tile, width), lambda i, p: (jnp.clip(i - 2 * b, 0, 1), 0))

    def there(shape, along):
        if along == 0:
            return pl.BlockSpec(shape, lambda i, p: (2 * p[i // 2] + i % 2, 0))
        return pl.BlockSpec(shape, lambda i, p: (0, 2 * p[i // 2] + i % 2))

    return pl.pallas_call(
        partial(project_kernel, count=count),
        grid_spec=pltpu.PrefetchScalarGridSpec(
            num_scalar_prefetch=1,
            grid=(2 * count,),
            in_specs=[block_spec(b) for b in range(count)]
            + [
                pl.BlockSpec(w_t.shape, lambda i, p: (0, 0)),
                pl.BlockSpec((1, width), lambda i, p: (0, 0)),
            ]
            + [pl.BlockSpec(memory_space=pl.ANY)] * len(held),
            out_specs=[
                there((tile, width), 0),
                there((columns, tile), 1),
                there((columns, tile), 1),
                there((columns, tile), 1),
                there((2, tile), 1),
            ],
        ),
        out_shape=[
            jax.ShapeDtypeStruct((total, width), jnp.bfloat16),
            jax.ShapeDtypeStruct((columns, total), jnp.float32),
            jax.ShapeDtypeStruct((columns, total), jnp.float32),
            jax.ShapeDtypeStruct((columns, total), jnp.bfloat16),
            jax.ShapeDtypeStruct((2, total), jnp.float32),
        ],
        input_output_aliases={3 + count + k: k for k in range(len(held))},
        compiler_params=pltpu.CompilerParams(vmem_limit_bytes=VMEM_BYTES),
        cost_estimate=pl.CostEstimate(
            flops=6 * count * rows * width * columns,
            bytes_accessed=count * (4 * rows * width + 10 * rows * columns) + 6 * width * columns,
            transcendentals=count * rows,
        ),
        name="project",
    )(places, *blocks, w_t, gain, *held)


def place_rows_kernel(places, *refs):
    *pieces, out = refs
    for k, piece in enumerate(pieces):
        out[places[k]] = piece[...]


def place_rows(places, blocks, first, rows):
    width = blocks[0].shape[1]
    return pl.pallas_call(
        place_rows_kernel,
        grid_spec=pltpu.PrefetchScalarGridSpec(
            num_scalar_prefetch=1,
            grid=(1,),
            in_specs=[pl.BlockSpec((rows, width), lambda i, p: (first // rows, 0))] * len(blocks),
            out_specs=pl.BlockSpec((len(blocks), rows, width), lambda i, p: (0, 0, 0)),
        ),
        out_shape=jax.ShapeDtypeStruct((len(blocks), rows, width), blocks[0].dtype),
        compiler_params=pltpu.CompilerParams(vmem_limit_bytes=VMEM_BYTES),
        name="place_rows",
    )(places, *blocks)


def hidden_term_kernel(place, heads_grad, w_t, out_rows, *refs, start, halves):
    outs = refs[-2:] if halves else refs[-1:]
    rows = heads_grad.shape[1]
    term = dot_tn(heads_grad[...], w_t[...])
    below = out_rows[0]
    if halves:
        cut = outs[0].shape[0]
        outs[0][...] = term[:cut].astype(jnp.bfloat16)
        outs[1][: rows - cut, :] = term[cut:].astype(jnp.bfloat16)
        outs[1][rows - cut :, :] = below
        return
    (out,) = outs
    got = refs[0]
    stop = start + got.shape[0]
    upper = min(stop, rows)
    if start:
        out[:start, :] = term[:start].astype(jnp.bfloat16)
    if upper < rows:
        out[upper:rows, :] = term[upper:].astype(jnp.bfloat16)
    out[start:upper, :] = (
        term[start:upper] + got[: upper - start, :].astype(jnp.float32)
    ).astype(jnp.bfloat16)
    if stop > rows:
        below = below.astype(jnp.float32) + got[rows - start :, :].astype(jnp.float32)
    out[rows:, :] = below.astype(jnp.bfloat16)


def hidden_term(place, heads_grad, w_t, out_rows, rows, got=None, start=0):
    columns, width = w_t.shape
    whole = rows + out_rows.shape[1]
    tile = min(512, width)
    halves = got is None
    gots, outs = ([], [whole // 2] * 2) if halves else ([got], [whole])
    made = pl.pallas_call(
        partial(hidden_term_kernel, start=start, halves=halves),
        grid_spec=pltpu.PrefetchScalarGridSpec(
            num_scalar_prefetch=1,
            grid=(width // tile,),
            in_specs=[
                pl.BlockSpec((columns, rows), lambda i, p: (0, p[0])),
                pl.BlockSpec((columns, tile), lambda i, p: (0, i)),
                pl.BlockSpec((1, whole - rows, tile), lambda i, p: (p[0], 0, i)),
            ]
            + [pl.BlockSpec((g.shape[0], tile), lambda i, p: (0, i)) for g in gots],
            out_specs=[pl.BlockSpec((count, tile), lambda i, p: (0, i)) for count in outs],
        ),
        out_shape=[jax.ShapeDtypeStruct((count, width), jnp.bfloat16) for count in outs],
        compiler_params=pltpu.CompilerParams(vmem_limit_bytes=VMEM_BYTES),
        cost_estimate=pl.CostEstimate(
            flops=0, bytes_accessed=0, transcendentals=0
        ),
        name="hidden_term",
    )(place, heads_grad, w_t, out_rows, *gots)
    return made if halves else made[0]


def input_grad_kernel(place, heads_grad, w_t, before, past, tokens, gain, mixed_grad, out):
    got = before[...].astype(jnp.float32) + past[...].astype(jnp.float32)
    scaled = (dot_tn(heads_grad[...], w_t[...]) + got) * gain[...]
    inputs = tokens[...].astype(jnp.float32)
    inverse = lax.rsqrt(jnp.mean(inputs * inputs, axis=-1, keepdims=True) + EPSILON)
    normed = inputs * inverse
    along = jnp.mean(scaled * normed, axis=-1, keepdims=True)
    out[...] = mixed_grad[...] + inverse * (scaled - normed * along)


def input_grad_of(place, heads_grad, w_t, before, past, tokens, gain, mixed_grad):
    columns, width = w_t.shape
    rows = tokens.shape[0]
    tile = rows // 4
    block = pl.BlockSpec((tile, width), lambda i, p: (i, 0))
    return pl.pallas_call(
        input_grad_kernel,
        grid_spec=pltpu.PrefetchScalarGridSpec(
            num_scalar_prefetch=1,
            grid=(4,),
            in_specs=[
                pl.BlockSpec((columns, tile), lambda i, p: (0, 4 * p[0] + i)),
                pl.BlockSpec((columns, width), lambda i, p: (0, 0)),
                block,
                block,
                block,
                pl.BlockSpec((1, width), lambda i, p: (0, 0)),
                block,
            ],
            out_specs=block,
        ),
        out_shape=jax.ShapeDtypeStruct((rows, width), jnp.float32),
        compiler_params=pltpu.CompilerParams(vmem_limit_bytes=VMEM_BYTES),
        cost_estimate=pl.CostEstimate(
            flops=2 * rows * width * columns,
            bytes_accessed=2 * columns * (rows + width) + 14 * rows * width,
            transcendentals=rows,
        ),
        name="input_grad",
    )(place, heads_grad, w_t, before, past, tokens, gain, mixed_grad)


def out_grad_kernel(branch, w_out, out):
    made = dot_nt(branch[...], w_out[...]).astype(jnp.bfloat16)
    columns = out.shape[2]
    for k in range(out.shape[0]):
        out[k] = made[:, k * columns : (k + 1) * columns]


def out_grad_of(branch, w_out, contexts):
    rows, width = branch.shape
    columns = w_out.shape[0] // contexts
    return pl.pallas_call(
        out_grad_kernel,
        grid=(contexts // 2,),
        in_specs=[
            pl.BlockSpec((rows, width), lambda i: (0, 0)),
            pl.BlockSpec((2 * columns, width), lambda i: (i, 0)),
        ],
        out_specs=pl.BlockSpec((2, rows, columns), lambda i: (i, 0, 0)),
        out_shape=jax.ShapeDtypeStruct((contexts, rows, columns), jnp.bfloat16),
        compiler_params=pltpu.CompilerParams(vmem_limit_bytes=VMEM_BYTES),
        cost_estimate=pl.CostEstimate(
            flops=2 * rows * width * width, bytes_accessed=2 * width * width, transcendentals=0
        ),
        name="out_grad",
    )(branch, w_out)


def heads_grad_kernel(query_scaled, key_scaled, value_grad, query_pre, key_pre, inverse, dots, out):
    columns = query_scaled.shape[0]
    for k, (scaled, pre) in enumerate(((query_scaled, query_pre), (key_scaled, key_pre))):
        inv = inverse[k : k + 1, :]
        factor = inv * inv * dots[k : k + 1, :]
        out[k * columns : (k + 1) * columns, :] = (inv * (scaled[...] - pre[...] * factor)).astype(
            jnp.bfloat16
        )
    out[2 * columns :, :] = value_grad[...]


def heads_grad_of(query_scaled, key_scaled, value_grad, query_pre, key_pre, inverse, dots):
    columns, total = query_scaled.shape
    tile = total // 4
    wide = pl.BlockSpec((columns, tile), lambda i: (0, i))
    row = pl.BlockSpec((2, tile), lambda i: (0, i))
    return pl.pallas_call(
        heads_grad_kernel,
        grid=(4,),
        in_specs=[wide] * 5 + [row] * 2,
        out_specs=pl.BlockSpec((3 * columns, tile), lambda i: (0, i)),
        out_shape=jax.ShapeDtypeStruct((3 * columns, total), jnp.bfloat16),
        compiler_params=pltpu.CompilerParams(vmem_limit_bytes=VMEM_BYTES),
        cost_estimate=pl.CostEstimate(
            flops=8 * columns * total, bytes_accessed=24 * columns * total, transcendentals=0
        ),
        name="heads_grad",
    )(query_scaled, key_scaled, value_grad, query_pre, key_pre, inverse, dots)


def heads_product_kernel(heads_grad, hidden, others, out):
    columns = heads_grad.shape[0]
    out[0, :, :columns] = dot_nn(heads_grad[...], hidden[...]).T.astype(jnp.bfloat16)
    out[0, :, columns:] = others[...].astype(jnp.bfloat16)


def heads_product_of(heads_grad, hidden_all, others, contexts):
    columns, total = heads_grad.shape
    width = hidden_all.shape[1]
    tile, extra = width // contexts, others.shape[1]
    return pl.pallas_call(
        heads_product_kernel,
        grid=(contexts,),
        in_specs=[
            pl.BlockSpec((columns, total), lambda i: (0, 0), pipeline_mode=pl.Buffered(1)),
            pl.BlockSpec((total, tile), lambda i: (0, i)),
            pl.BlockSpec((tile, extra), lambda i: (i, 0)),
        ],
        out_specs=pl.BlockSpec((1, tile, columns + extra), lambda i: (i, 0, 0)),
        out_shape=jax.ShapeDtypeStruct((contexts, tile, columns + extra), jnp.bfloat16),
        compiler_params=pltpu.CompilerParams(vmem_limit_bytes=VMEM_BYTES),
        cost_estimate=pl.CostEstimate(
            flops=2 * columns * total * width,
            bytes_accessed=2 * total * (columns + width),
            transcendentals=0,
        ),
        name="heads_product",
    )(heads_grad, hidden_all, others)


def gather_pieces_kernel(me, *refs):
    *pieces, out = refs
    for step, piece in enumerate(pieces):
        out[lax.rem(me[0] + step, len(pieces))] = piece[...]


def gather_pieces(me, pieces):
    return pl.pallas_call(
        gather_pieces_kernel,
        grid_spec=pltpu.PrefetchScalarGridSpec(
            num_scalar_prefetch=1,
            grid=(1,),
            in_specs=[pl.BlockSpec(piece.shape, lambda i, m: (0, 0)) for piece in pieces],
            out_specs=pl.BlockSpec((len(pieces),) + pieces[0].shape, lambda i, m: (0, 0, 0)),
        ),
        out_shape=jax.ShapeDtypeStruct((len(pieces),) + pieces[0].shape, pieces[0].dtype),
        compiler_params=pltpu.CompilerParams(vmem_limit_bytes=VMEM_BYTES),
        name="gather_pieces",
    )(me[None], *pieces)


def slot_match(rank_row, slots):
    return lax.broadcasted_iota(jnp.int32, (slots, rank_row.shape[1]), 0) == rank_row


def slot_gates(match, gate_row):
    return jnp.sum(jnp.where(match, gate_row, 0.0), axis=1, keepdims=True)


def experts_forward_kernel(*refs, count, slots, aliased, tiles):
    ranks, gates = refs[:2]
    blocks = refs[2 : 2 + count]
    w_gate, w_up, w_down = refs[2 + count : 5 + count]
    refs = refs[5 + count + aliased :]
    taken, active, gate_slope, up_slope = refs[:4]
    outs = refs[4 : 4 + count]
    made, weights = refs[4 + count :]
    e, f = pl.program_id(0), pl.program_id(1)
    tile, wide_tile = w_gate.shape[2], w_down.shape[2]

    @pl.when(f == 0)
    def _():
        for b in range(count):
            here = slice(b * slots, (b + 1) * slots)
            match = slot_match(ranks[b, e], slots)
            weights[here, :] = slot_gates(match, gates[b, e])
            taken[0, here, :] = dot_nn(match.astype(jnp.bfloat16), blocks[b][...]).astype(
                jnp.bfloat16
            )

    @pl.when(f < tiles)
    def _():
        at = pl.ds(pl.multiple_of(f * tile, tile), tile)
        rows = taken[0]
        gate_pre = dot_nn(rows, w_gate[0])
        up_pre = dot_nn(rows, w_up[0])
        sigmoid_gate = 1.0 / (1.0 + jnp.exp(-gate_pre))
        silu = gate_pre * sigmoid_gate
        active[0, :, at] = (silu * up_pre).astype(jnp.bfloat16)
        up_slope[0, :, at] = silu.astype(jnp.bfloat16)
        gate_slope[0, :, at] = (up_pre * (sigmoid_gate + silu * (1.0 - sigmoid_gate))).astype(
            jnp.bfloat16
        )

    @pl.when(f >= tiles)
    def _():
        at = pl.ds(pl.multiple_of((f - tiles) * wide_tile, wide_tile), wide_tile)
        made[e, :, at] = (dot_nn(active[0], w_down[0]) * weights[...]).astype(jnp.bfloat16)

    @pl.when((f == pl.num_programs(1) - 1) & (e == pl.num_programs(0) - 1))
    def _():
        combine(ranks, made, outs, count, slots)


def combine(ranks, made, outs, count, slots):
    for b in range(count):
        summed = None
        for k in range(made.shape[0]):
            match = slot_match(ranks[b, k], slots).astype(jnp.float32).astype(jnp.bfloat16)
            term = dot_tn(match, made[k, b * slots : (b + 1) * slots, :])
            summed = term if summed is None else summed + term
        outs[b][...] = summed.astype(jnp.bfloat16)


def experts_backward_kernel(*refs, count, slots, aliased, tiles):
    ranks, gates = refs[:2]
    blocks = refs[2 : 2 + count]
    w_gate, w_up, w_down, gate_slope, up_slope = refs[2 + count : 7 + count]
    refs = refs[7 + count + aliased :]
    taken, gate_grad, up_grad = refs[:3]
    outs = refs[3 : 3 + count]
    (made,) = refs[3 + count :]
    e, f = pl.program_id(0), pl.program_id(1)
    tile, wide_tile = w_down.shape[1], w_gate.shape[1]

    @pl.when(f == 0)
    def _():
        for b in range(count):
            match = slot_match(ranks[b, e], slots)
            weight = slot_gates(match, gates[b, e])
            taken[0, b * slots : (b + 1) * slots, :] = (
                dot_nn(match.astype(jnp.bfloat16), blocks[b][...]) * weight
            ).astype(jnp.bfloat16)

    @pl.when(f < tiles)
    def _():
        at = pl.ds(pl.multiple_of(f * tile, tile), tile)
        active_grad = dot_nt(taken[0], w_down[0])
        gate_grad[0, :, at] = (active_grad * gate_slope[0].astype(jnp.float32)).astype(jnp.bfloat16)
        up_grad[0, :, at] = (active_grad * up_slope[0].astype(jnp.float32)).astype(jnp.bfloat16)

    @pl.when(f >= tiles)
    def _():
        at = pl.ds(pl.multiple_of((f - tiles) * wide_tile, wide_tile), wide_tile)
        made[e, :, at] = (dot_nt(gate_grad[0], w_gate[0]) + dot_nt(up_grad[0], w_up[0])).astype(
            jnp.bfloat16
        )

    @pl.when((f == pl.num_programs(1) - 1) & (e == pl.num_programs(0) - 1))
    def _():
        combine(ranks, made, outs, count, slots)


def experts_stage(
    forward, ranks, gates, blocks, weights, slopes, held, place, slots, all_slots, light=False
):
    count = len(blocks)
    rows, width = blocks[0].shape
    experts, _, hidden_units = weights[0].shape
    tile, wide_tile = min(512, hidden_units), min(1024, width)
    tiles, wide_tiles = hidden_units // tile, width // wide_tile
    part = count * slots

    def first(f):
        return jnp.minimum(f, tiles - 1)

    def later(f):
        return jnp.maximum(f - tiles, 0)

    info = pl.BlockSpec((count, experts, 1, rows), lambda e, f: (0, 0, 0, 0))
    block = pl.BlockSpec((rows, width), lambda e, f: (0, 0))
    wide = pl.BlockSpec((1, part, width), lambda e, f: (e, place, 0))
    narrow = pl.BlockSpec((1, part, hidden_units), lambda e, f: (e, place, 0))
    slope = pl.BlockSpec((1, part, tile), lambda e, f: (e, 0, first(f)))
    own = pl.BlockSpec((1, part, hidden_units), lambda e, f: (e, 0, 0))
    if forward:
        kernel, name = experts_forward_kernel, "experts_forward"
        into = pl.BlockSpec((1, width, tile), lambda e, f: (e, 0, first(f)))
        back = pl.BlockSpec((1, hidden_units, wide_tile), lambda e, f: (e, 0, later(f)))
        narrow_outs, own_outs, scratch = 1, 2, [pltpu.VMEM((part, 1), jnp.float32)]
    else:
        kernel, name = experts_backward_kernel, "experts_backward"
        into = pl.BlockSpec((1, wide_tile, hidden_units), lambda e, f: (e, later(f), 0))
        back = pl.BlockSpec((1, tile, width), lambda e, f: (e, first(f), 0))
        narrow_outs, own_outs, scratch = 2, 0, []
    held = () if held is None else tuple(held)
    before = 2 + count + 3 + len(slopes)
    scale = 0 if light else 1
    flops = 2 * experts * part * width * (3 * hidden_units + 2 * rows)
    return pl.pallas_call(
        partial(kernel, count=count, slots=slots, aliased=len(held), tiles=tiles),
        grid=(experts, tiles + wide_tiles),
        in_specs=[info, info]
        + [block] * count
        + [into, into, back]
        + [slope] * len(slopes)
        + [pl.BlockSpec(memory_space=pl.ANY)] * len(held),
        out_specs=[wide] + [narrow] * narrow_outs + [own] * own_outs + [block] * count,
        out_shape=[jax.ShapeDtypeStruct((experts, all_slots, width), jnp.bfloat16)]
        + [jax.ShapeDtypeStruct((experts, all_slots, hidden_units), jnp.bfloat16)] * narrow_outs
        + [jax.ShapeDtypeStruct((experts, part, hidden_units), jnp.bfloat16)] * own_outs
        + [jax.ShapeDtypeStruct((rows, width), jnp.bfloat16)] * count,
        scratch_shapes=[pltpu.VMEM((experts, part, width), jnp.bfloat16)] + scratch,
        input_output_aliases={before + k: k for k in range(len(held))},
        compiler_params=pltpu.CompilerParams(vmem_limit_bytes=VMEM_BYTES),
        cost_estimate=pl.CostEstimate(
            flops=scale * flops,
            bytes_accessed=scale
            * 2
            * (3 * experts * width * hidden_units + 4 * count * rows * width),
            transcendentals=scale * experts * part * hidden_units,
        ),
        name=name,
    )(ranks, gates, *blocks, *weights, *slopes, *held)


def ring_of(contexts):
    order = list(range(0, contexts, 2)) + list(range(contexts - 1, 0, -2))
    place_of = [order.index(c) for c in range(contexts)]
    up = [(order[p], order[(p + 1) % contexts]) for p in range(contexts)]
    down = [(b, a) for a, b in up]
    return order, place_of, up, down


class RingGather:
    def __init__(self, own, ring):
        _, _, self.up, self.down = ring
        self.half = len(self.up) // 2
        self.step = 0
        self.blocks = {0: own}
        self.from_before = self.from_after = own

    def advance(self, *earlier):
        self.step += 1
        before, past = self.from_before, self.from_after
        if earlier:
            before, past = lax.optimization_barrier((before, past) + earlier)[:2]
        if self.step < self.half:
            self.from_before = lax.ppermute(before, "ctx", self.up)
            self.from_after = lax.ppermute(past, "ctx", self.down)
            self.blocks[-self.step] = self.from_before
            self.blocks[self.step] = self.from_after
            return (-self.step, self.step)
        cut = before.shape[0] // 2
        first = lax.ppermute(before[:cut], "ctx", self.up)
        second = lax.ppermute(past[cut:], "ctx", self.down)
        self.blocks[self.half] = jnp.concatenate([first, second], axis=0)
        return (self.half,)


def add_low(left, right):
    return (left.astype(jnp.float32) + right.astype(jnp.float32)).astype(jnp.bfloat16)


class RingScatter:
    def __init__(self, ring):
        _, _, self.up, self.down = ring
        self.half = len(self.up) // 2
        self.step = self.half

    def prepare(self, terms, *earlier):
        if self.step == self.half:
            far = after(terms[self.half], *earlier)
            cut = far.shape[0] // 2
            before, past = far[:cut], far[cut:]
        else:
            before, past = terms[-self.step], terms[self.step]
            got_before, got_past = self.to_before, self.to_after
            if earlier:
                before, past = lax.optimization_barrier((before, past) + earlier)[:2]
            cut = got_before.shape[0]
            if cut < before.shape[0]:
                before = jnp.concatenate([add_low(got_before, before[:cut]), before[cut:]], axis=0)
                past = jnp.concatenate([past[:cut], add_low(got_past, past[cut:])], axis=0)
            else:
                before, past = add_low(got_before, before), add_low(got_past, past)
        self.payload = (before, past)
        return self.payload

    def send(self, *earlier):
        before, past = self.payload
        if earlier:
            before, past = lax.optimization_barrier((before, past) + earlier)[:2]
        self.to_before = lax.ppermute(before, "ctx", self.down)
        self.to_after = lax.ppermute(past, "ctx", self.up)
        self.step -= 1
        return self.payload

    def advance(self, terms, *earlier):
        self.prepare(terms, *earlier)
        return self.send()

    def finish(self, own):
        return (
            own.astype(jnp.float32)
            + self.to_before.astype(jnp.float32)
            + self.to_after.astype(jnp.float32)
        )


def sum_over_ctx(values, contexts):
    bit = 1
    while bit < contexts:
        values = values + lax.ppermute(values, "ctx", [(c, c ^ bit) for c in range(contexts)])
        bit *= 2
    return values


def after(value, *earlier):
    return lax.optimization_barrier((value,) + earlier)[0]


def shards_by_heads(
    tokens,
    cotangent,
    cont_lengths,
    routes,
    gates,
    attn_gain,
    query_gain,
    key_gain,
    ffn_gain,
    w_query,
    w_key,
    w_value,
    w_out,
    w_gate,
    w_up,
    w_down,
):
    both = ("ctx", "fsdp")
    contexts, splits = lax.axis_size("ctx"), lax.axis_size("fsdp")
    rows, width = tokens.shape[1:]
    route_count = routes.shape[2]
    total = rows * contexts
    prompt_rows = total // 2
    columns = width // contexts
    size = min(512, prompt_rows)
    local_experts = w_gate.shape[0]
    expert_total = local_experts * contexts
    slots = max(2, rows * route_count * 5 // (4 * expert_total))
    all_slots = contexts * slots
    score_scale = HEAD ** (-0.5)
    me = lax.axis_index("ctx")
    ring = ring_of(contexts)
    half = contexts // 2
    place = jnp.where(me % 2 == 0, me // 2, contexts - 1 - me // 2)

    def owner(offset):
        at = (place + offset) % contexts
        return jnp.where(at < half, 2 * at, 2 * (contexts - 1 - at) + 1)

    others = [k for step in range(1, half) for k in (-step, step)] + [half]

    own_rows = w_out.shape[0]
    token_ring = RingGather(jnp.concatenate([tokens[0], w_out], axis=0), ring)

    chosen = routes[0].T[None] == jnp.arange(expert_total, dtype=jnp.int32)[:, None, None]
    member = jnp.any(chosen, axis=1)
    gate_rows = jnp.sum(jnp.where(chosen, gates[0].T[None], 0.0), axis=1)
    earlier = jnp.tril(jnp.ones((rows, rows), jnp.bfloat16), -1)
    rank = jnp.einsum(
        "et,ut->eu", member.astype(jnp.bfloat16), earlier, preferred_element_type=jnp.float32
    )
    rank = jnp.where(member, rank, -1.0)
    rank_high = jnp.floor(rank / 16.0)
    gate_high = gate_rows.astype(jnp.bfloat16).astype(jnp.float32)
    routing = jnp.stack([rank_high, rank - 16.0 * rank_high, gate_high, gate_rows - gate_high])
    routing = routing.astype(jnp.bfloat16).reshape(4, contexts, local_experts * rows)
    routing = jnp.transpose(routing, (1, 0, 2)).reshape(contexts, own_rows, -1)
    routing_columns = routing.shape[2]

    cut = jnp.stack([w_query, w_key, w_value]).reshape(3, own_rows, contexts, columns)
    cut = jnp.transpose(cut, (2, 1, 0, 3)).reshape(contexts, own_rows, 3 * columns)
    own_gains = jnp.stack([attn_gain, query_gain, key_gain, ffn_gain], axis=1)
    cut = jnp.concatenate(
        [cut, jnp.broadcast_to(own_gains, (contexts,) + own_gains.shape), routing], axis=2
    )
    spare = -cut.shape[2] % 128
    cut = jnp.pad(cut, ((0, 0), (0, 0), (0, spare)))
    pieces = []
    for step in range(contexts):
        piece = lax.dynamic_index_in_dim(cut, (me - step) % contexts, 0, keepdims=False)
        if step:
            pairs = [(c, (c - step) % contexts) for c in range(contexts)]
            piece = lax.ppermute(piece, "ctx", pairs)
        pieces.append(piece)
    first_piece = pieces[1]
    pieces = gather_pieces(me, pieces)
    token_ring.advance(first_piece)
    gate_all = lax.all_gather(after(w_gate, pieces), "fsdp", axis=1, tiled=True)
    w_all = lax.all_gather(pieces, "fsdp", axis=1, tiled=True).reshape(width, -1)
    up_all = lax.all_gather(w_up, "fsdp", axis=1, tiled=True)
    for _ in range(2, half):
        token_ring.advance()
    w_t = w_all[:, : 3 * columns].T
    all_gains = w_all[:, 3 * columns : 3 * columns + 4].astype(jnp.float32).T
    gain_attn, gain_ffn = all_gains[0], all_gains[3]
    gain_query = lax.dynamic_slice_in_dim(all_gains[1], me * columns, columns)[:, None]
    gain_key = lax.dynamic_slice_in_dim(all_gains[2], me * columns, columns)[:, None]

    owners = owner(jnp.arange(contexts, dtype=jnp.int32))
    routing = pieces[:, :, 3 * columns + 4 : 3 * columns + 4 + routing_columns]
    routing = routing.reshape(contexts, 4, local_experts, 1, rows)[owners].astype(jnp.float32)
    all_ranks = (16.0 * routing[:, 0] + routing[:, 1]).astype(jnp.int32)
    all_gates = routing[:, 2] + routing[:, 3]

    lengths_in = cont_lengths[0]
    token_index = jnp.arange(total, dtype=jnp.int32)
    _, position = places(token_index, lengths_in, prompt_rows)
    starts = prompt_rows + jnp.cumsum(lengths_in) - lengths_in
    frequency = ROPE_BASE ** (-jnp.arange(HEAD // 2).astype(jnp.float32) / (HEAD // 2))
    angles = frequency[:, None] * position.astype(jnp.float32)[None, :]
    cosine, sine = jnp.cos(angles), jnp.sin(angles)

    def project_all(offsets, made):
        blocks = [token_ring.blocks[offset] for offset in offsets]
        places_of = owner(jnp.asarray(offsets, jnp.int32))
        return project(places_of, blocks, rows, w_t, gain_attn[None], made, total)

    made = project_all([0] + others[: 2 * (half - 2)], None)
    token_ring.advance(made[-1], up_all, gate_all)
    made = project_all(others[2 * (half - 2) : -1], made)
    token_ring.blocks[half] = after(token_ring.blocks[half], made[-1])
    made = project_all(others[-1:], made)
    hidden_all, query_pre, key_pre, value_t, squares = made
    w_out_rows = place_rows(
        after(owners, made[-1]), [token_ring.blocks[k if k <= half else k - contexts] for k in range(contexts)], rows, own_rows
    )
    out_all = lax.all_gather(w_out_rows, "fsdp", axis=1, tiled=True).reshape(width, width)
    down_all = lax.all_gather(w_down, "fsdp", axis=1, tiled=True)

    squares = sum_over_ctx(squares, contexts)
    inverse = lax.rsqrt(squares / width + EPSILON)
    query_inv, key_inv = inverse[0:1], inverse[1:2]
    grad_ring = RingGather(cotangent[0], ring)
    grad_ring.advance(squares)

    attended, query, key, key_t, log_rows = attend_forward(
        starts, query_pre, key_pre, value_t, query_inv, key_inv, gain_query, gain_key, cosine, sine, size, prompt_rows, score_scale
    )
    sent = after(attended, grad_ring.from_before, grad_ring.from_after)
    back = lax.all_to_all(
        sent.reshape(contexts, rows, columns), "ctx", split_axis=0, concat_axis=0, tiled=True
    )
    grad_ring.advance(attended)
    own_attended = jnp.transpose(back, (1, 0, 2)).reshape(rows, width)
    inputs = tokens[0].astype(jnp.float32)
    mixed = inputs + jnp.dot(own_attended, out_all, preferred_element_type=jnp.float32)
    mixed_inv = lax.rsqrt(jnp.mean(mixed * mixed, axis=-1, keepdims=True) + EPSILON)
    second = (mixed * mixed_inv * gain_ffn).astype(jnp.bfloat16)

    second_ring = RingGather(second, ring)
    weights = (gate_all, up_all, down_all)

    def stage_info(offsets):
        ranks = jnp.stack([all_ranks[k] for k in offsets])
        stage_gates = jnp.stack([all_gates[k] for k in offsets])
        if len(offsets) == 2:
            return ranks, stage_gates, offsets[1] - 1
        return ranks, stage_gates, contexts - (2 if offsets[0] == 0 else 1)

    stages = [(0,)] + [(-step, step) for step in range(1, half)] + [(half,)]
    infos = [stage_info(stage) for stage in stages]
    result_terms, second_terms, slopes = {}, {}, {}
    kept = kept_grads = None

    def forward(step, *earlier):
        nonlocal kept
        ranks, stage_gates, at = infos[step]
        ranks = after(ranks, *earlier) if earlier else ranks
        blocks = [second_ring.blocks[k] for k in stages[step]]
        made = experts_stage(
            True, ranks, stage_gates, blocks, weights, (), kept, at, slots, all_slots
        )
        kept, slopes[step], terms = made[:2], made[2:4], made[4:]
        result_terms.update(zip(stages[step], terms))
        return terms[0]

    def backward(step, *earlier, light=False):
        nonlocal kept_grads
        ranks, stage_gates, at = infos[step]
        ranks = after(ranks, *earlier) if earlier else ranks
        blocks = [grad_ring.blocks[k] for k in stages[step]]
        made = experts_stage(
            False,
            ranks,
            stage_gates,
            blocks,
            weights,
            slopes[step],
            kept_grads,
            at,
            slots,
            all_slots,
            light,
        )
        kept_grads, terms = made[:3], made[3:]
        second_terms.update(zip(stages[step], terms))
        return terms[0]

    def weight_grad(left, right):
        return jnp.einsum("emd,emf->edf", left, right, preferred_element_type=jnp.float32).astype(
            jnp.bfloat16
        )

    second_ring.advance()
    grad_second = (grad_ring.from_before, grad_ring.from_after)
    done = forward(0)
    done = backward(0, done, *grad_second, light=True)
    for step in range(1, half):
        near = [second_ring.blocks[k] for k in stages[step]]
        second_ring.advance(done)
        waits = (done,)
        if step > 1:
            waits += (grad_ring.from_before, grad_ring.from_after)
        if step in (1, half - 1):
            grad_ring.advance(done, *near)
        done = forward(step, *waits)
        if step < half - 2:
            done = backward(step, done, light=True)
    done = forward(half, done)

    second_sum, result_sum = RingScatter(ring), RingScatter(ring)
    result_sum.advance(result_terms)
    backward(half, done)
    sent = second_sum.advance(second_terms, result_sum.to_before, result_sum.to_after)
    backward(half - 1, *sent)
    sent = second_sum.advance(second_terms)
    backward(half - 2, *sent)
    sent = second_sum.advance(second_terms)
    rows_taken, active = kept
    route_grad, gate_grad, up_grad = kept_grads
    gate_product = weight_grad(after(rows_taken, *sent), gate_grad)
    sent = second_sum.advance(second_terms, gate_product)
    result_sum.prepare(result_terms, *sent)
    up_product = weight_grad(after(rows_taken, *result_sum.payload), up_grad)
    second_grad = second_sum.finish(after(second_terms[0], up_product))

    def fsdp_sum_low(product):
        return lax.psum_scatter(product, "fsdp", scatter_dimension=1, tiled=True)


    upstream = cotangent[0].astype(jnp.float32)
    mixed_normed = mixed * mixed_inv
    ffn_gain_grad = jnp.sum(second_grad * mixed_normed, axis=0)
    scaled = second_grad * gain_ffn
    mixed_grad = upstream + mixed_inv * (
        scaled - mixed_normed * jnp.mean(scaled * mixed_normed, axis=-1, keepdims=True)
    )
    branch = mixed_grad.astype(jnp.bfloat16)
    out_grad = out_grad_of(branch, out_all, contexts)
    w_out_grad = lax.dot_general(
        own_attended, after(branch, out_grad), (((0,), (0,)), ((), ())), preferred_element_type=jnp.float32
    ).astype(jnp.bfloat16)
    out_grad = lax.all_to_all(out_grad, "ctx", split_axis=0, concat_axis=0, tiled=True)
    out_grad = out_grad.reshape(total, columns)
    w_out_grad = fsdp_sum_low(
        after(w_out_grad, out_grad).reshape(contexts, splits * own_rows, width)
    )
    gate_w_grad = fsdp_sum_low(after(gate_product, out_grad))
    up_w_grad = fsdp_sum_low(after(up_product, out_grad))

    log_rows = log_rows.reshape(columns // HEAD, 1, total)
    held, dots, waits = None, 0.0, (out_grad,)
    for head in range(columns // HEAD):
        if head == 1:
            result_sum.prepare(result_terms, dots)
            waits = result_sum.payload
        if head < 2:
            result_sum.send(out_grad)
        *held, part = attend_backward(
            after(starts, *waits), head, held, query, key, key_t, value_t, out_grad, attended, log_rows, query_pre, key_pre, query_inv, key_inv, gain_query, gain_key, cosine, sine, size, prompt_rows, score_scale
        )
        dots = dots + part
    query_scaled, key_scaled, value_grad, query_gain_grad, key_gain_grad = held
    dots = after(dots, result_sum.to_before, result_sum.to_after)
    result_sum.prepare(result_terms, dots)
    dots = sum_over_ctx(dots, contexts) / width
    dots = after(dots, *result_sum.payload)
    heads_grad = heads_grad_of(
        query_scaled, key_scaled, value_grad, query_pre, key_pre, inverse, dots
    )

    def own_columns(grad):
        return lax.dynamic_update_slice_in_dim(
            jnp.zeros((width, 1), jnp.float32), grad, me * columns, 0
        )

    other_grads = jnp.concatenate(
        [
            ffn_gain_grad[:, None],
            own_columns(query_gain_grad),
            own_columns(key_gain_grad),
            jnp.zeros((width, 125), jnp.float32),
        ],
        axis=1,
    )
    def term(offset, *earlier, **got):
        at = after(owner(offset)[None], *earlier)
        return hidden_term(at, heads_grad, w_t, w_out_grad, rows, **got)

    result_sum.send(dots)
    hidden_sum = RingScatter(ring)
    hidden_sum.payload = far = term(half)
    hidden_sum.send()
    heads_product = heads_product_of(
        heads_grad, hidden_all, after(other_grads, *far), contexts
    )
    heads_w_grad = fsdp_sum_low(after(heads_product, hidden_sum.to_before, hidden_sum.to_after))
    done = (result_sum.to_before, result_sum.to_after)
    for step in range(half - 1, 0, -1):
        start = far[0].shape[0] if step == half - 1 else 0
        if step == half - 2:
            done = (heads_product, down_product, gate_w_grad)
        if step == 1:
            done = (up_w_grad,)
        hidden_sum.payload = sent = (
            term(-step, *done, got=hidden_sum.to_before),
            term(step, *done, got=hidden_sum.to_after, start=start),
        )
        hidden_sum.send()
        if step == half - 1:
            down_product = weight_grad(after(active, *sent), route_grad)
            down_w_grad = fsdp_sum_low(
                after(down_product, hidden_sum.to_before, hidden_sum.to_after)
            )
            heads_w_grad = lax.all_to_all(
                heads_w_grad, "ctx", split_axis=0, concat_axis=0, tiled=True
            )
        done = ()
    input_grad = input_grad_of(
        after(owner(0)[None], heads_w_grad),
        heads_grad,
        w_t,
        hidden_sum.to_before,
        hidden_sum.to_after,
        tokens[0],
        gain_attn[None],
        mixed_grad,
    )
    w_out_grad = (
        lax.dynamic_index_in_dim(w_out_grad, me, 0, keepdims=False).astype(jnp.float32)
        + hidden_sum.to_before[rows:].astype(jnp.float32)
        + hidden_sum.to_after[rows:].astype(jnp.float32)
    )
    routed = result_sum.finish(result_terms[0])
    output = (mixed + routed)[None]

    heads_w_grad = heads_w_grad.astype(jnp.float32)
    other_grads = jnp.sum(heads_w_grad[:, :, 3 * columns : 3 * columns + 3], axis=0)
    heads_w_grad = jnp.transpose(
        heads_w_grad[:, :, : 3 * columns].reshape(contexts, own_rows, 3, columns), (2, 1, 0, 3)
    ).reshape(3, own_rows, width)

    attn_gain_grad = jnp.sum(
        w_query.astype(jnp.float32) * heads_w_grad[0]
        + w_key.astype(jnp.float32) * heads_w_grad[1]
        + w_value.astype(jnp.float32) * heads_w_grad[2],
        axis=1,
    ) / attn_gain.astype(jnp.float32)

    return (
        output,
        input_grad[None],
        attn_gain_grad,
        other_grads[:, 1],
        other_grads[:, 2],
        other_grads[:, 0],
        heads_w_grad[0],
        heads_w_grad[1],
        heads_w_grad[2],
        w_out_grad,
        gate_w_grad.astype(jnp.float32),
        up_w_grad.astype(jnp.float32),
        down_w_grad.astype(jnp.float32),
    )


def solution(mesh):
    contexts = mesh.shape["ctx"]
    fits = contexts == 8
    placed = (
        P("fsdp", "ctx", None),
        P("fsdp", "ctx", None),
        P("fsdp", None),
        P("fsdp", "ctx", None),
        P("fsdp", "ctx", None),
        P(("ctx", "fsdp")),
        P(("ctx", "fsdp")),
        P(("ctx", "fsdp")),
        P(("ctx", "fsdp")),
        P(("ctx", "fsdp"), None),
        P(("ctx", "fsdp"), None),
        P(("ctx", "fsdp"), None),
        P(("ctx", "fsdp"), None),
        P("ctx", "fsdp", None),
        P("ctx", "fsdp", None),
        P("ctx", "fsdp", None),
    )
    return jax.shard_map(
        shards_by_heads if fits else shards_wide,
        mesh=mesh,
        in_specs=placed,
        out_specs=(
            P("fsdp", "ctx", None),
            P("fsdp", "ctx", None),
            P(("ctx", "fsdp")),
            P(("ctx", "fsdp")),
            P(("ctx", "fsdp")),
            P(("ctx", "fsdp")),
            P(("ctx", "fsdp"), None),
            P(("ctx", "fsdp"), None),
            P(("ctx", "fsdp"), None),
            P(("ctx", "fsdp"), None),
            P("ctx", "fsdp", None),
            P("ctx", "fsdp", None),
            P("ctx", "fsdp", None),
        ),
        check_vma=False,
    )
```

```python
from functools import partial

import jax
import jax.numpy as jnp
from jax import lax
from jax.experimental import pallas as pl
from jax.experimental.pallas import tpu as pltpu
from jax.sharding import PartitionSpec as P

HEAD = 128


EPSILON = 1e-05
ROPE_BASE = 10000.0
MASKED = -1e30


def norm_rows(values_in, gain_in):
    return (
        values_in
        * lax.rsqrt(jnp.mean(values_in * values_in, axis=-1, keepdims=True) + EPSILON)
        * gain_in
    )


def places(token_index, lengths_in, prompt_rows):
    ends = prompt_rows + jnp.cumsum(lengths_in)
    passed = (token_index[:, None] >= ends[None, :]).astype(jnp.int32)
    before = jnp.sum(passed * lengths_in[None, :], axis=1)
    inside = token_index >= prompt_rows
    segment = jnp.where(inside, 1 + jnp.sum(passed, axis=1), 0)
    position = jnp.where(inside, token_index - before, token_index)
    return (segment, position)


def rotate(values_in, positions):
    full_shape = values_in.shape
    per_head = values_in.reshape(full_shape[:-1] + (full_shape[-1] // HEAD, HEAD))
    half_dim = HEAD // 2
    frequency = ROPE_BASE ** (-jnp.arange(half_dim).astype(values_in.dtype) / half_dim)
    angles = positions.astype(values_in.dtype)[..., None] * frequency
    cosine = jnp.cos(angles)[..., None, :]
    sine = jnp.sin(angles)[..., None, :]
    former = per_head[..., :half_dim]
    latter = per_head[..., half_dim:]
    turned = jnp.concatenate(
        [former * cosine - latter * sine, latter * cosine + former * sine], axis=-1
    )
    return turned.reshape(full_shape)


def allowed_pairs(query_index, query_seg, key_index, key_seg):
    return (key_index[None, :] <= query_index[:, None]) & (
        (key_seg[None, :] == 0) | (key_seg[None, :] == query_seg[:, None])
    )


def attend_fold(
    state_in,
    shard_piece,
    first_row,
    query_heads,
    own_index,
    own_seg,
    lengths_in,
    prompt_rows,
    score_scale,
):
    highest, denominator, weighted = state_in
    key_rows, value_rows = shard_piece
    piece_count = key_rows.shape[0]
    key_index = jnp.arange(piece_count, dtype=jnp.int32)
    key_seg, _ = places(key_index, lengths_in, prompt_rows)
    key_heads = key_rows.reshape(piece_count, -1, HEAD)
    value_heads = value_rows.reshape(piece_count, -1, HEAD)
    scores = (
        jnp.einsum("qhd,khd->hqk", query_heads, key_heads, preferred_element_type=jnp.float32)
        * score_scale
    )
    allowed = allowed_pairs(own_index, own_seg, key_index, key_seg)
    masked = jnp.where(allowed[None], scores, MASKED)
    new_high = jnp.maximum(highest, jnp.max(masked, axis=-1))
    shrink = jnp.exp(highest - new_high)
    unnormed = jnp.where(allowed[None], jnp.exp(masked - new_high[..., None]), 0.0)
    denominator = jnp.sum(unnormed, axis=-1)
    weighted = jnp.einsum(
        "hqk,khd->hqd",
        unnormed.astype(jnp.bfloat16),
        value_heads,
        preferred_element_type=jnp.float32,
    )
    return (new_high, denominator, weighted)


def pair_terms(
    query_heads,
    grad_heads,
    log_rows,
    dot_rows,
    query_index,
    query_seg,
    key_heads,
    value_heads,
    key_index,
    key_seg,
    score_scale,
):
    scores = (
        jnp.einsum("qhd,khd->hqk", query_heads, key_heads, preferred_element_type=jnp.float32)
        * score_scale
    )
    allowed = allowed_pairs(query_index, query_seg, key_index, key_seg)
    prob = jnp.where(
        allowed[None], jnp.exp(jnp.where(allowed[None], scores, MASKED) - log_rows[..., None]), 0.0
    )
    prob_grad = jnp.einsum(
        "qhd,khd->hqk", grad_heads, value_heads, preferred_element_type=jnp.float32
    )
    score_grad = (prob * (prob_grad - dot_rows[..., None])).astype(jnp.bfloat16)
    return (prob, score_grad)


def slot_targets(route_list, expert_total, capacity):
    onehot = (route_list[:, None] == jnp.arange(expert_total, dtype=jnp.int32)[None, :]).astype(
        jnp.int32
    )
    slot_rank = jnp.sum((jnp.cumsum(onehot, axis=0) - 1) * onehot, axis=1)
    return route_list * capacity + slot_rank


def shards_wide(
    tokens,
    cotangent,
    cont_lengths,
    routes,
    gates,
    attn_gain,
    query_gain,
    key_gain,
    ffn_gain,
    w_query,
    w_key,
    w_value,
    w_out,
    w_gate,
    w_up,
    w_down,
):
    row_count = tokens.shape[1]
    model_width = tokens.shape[2]
    route_count = routes.shape[2]
    context_size = lax.axis_size("ctx")
    all_rows = row_count * context_size
    prompt_rows = all_rows // 2
    local_experts = w_gate.shape[0]
    expert_total = local_experts * context_size
    capacity = max(2, row_count * route_count * 5 // (4 * expert_total))
    head_count = model_width // HEAD
    score_scale = HEAD ** (-0.5)
    lengths_in = cont_lengths[0]
    own_index = lax.axis_index("ctx") * row_count + jnp.arange(row_count, dtype=jnp.int32)
    own_seg, own_pos = places(own_index, lengths_in, prompt_rows)
    attention_set = (
        lax.all_gather(w_query, ("ctx", "fsdp"), axis=0, tiled=True),
        lax.all_gather(w_key, ("ctx", "fsdp"), axis=0, tiled=True),
        lax.all_gather(w_value, ("ctx", "fsdp"), axis=0, tiled=True),
        lax.all_gather(w_out, ("ctx", "fsdp"), axis=0, tiled=True),
        lax.all_gather(attn_gain, ("ctx", "fsdp"), axis=0, tiled=True),
        lax.all_gather(query_gain, ("ctx", "fsdp"), axis=0, tiled=True),
        lax.all_gather(key_gain, ("ctx", "fsdp"), axis=0, tiled=True),
        lax.all_gather(ffn_gain, ("ctx", "fsdp"), axis=0, tiled=True),
    )
    query_all, key_all, value_all, out_all = (
        attention_set[0],
        attention_set[1],
        attention_set[2],
        attention_set[3],
    )
    gain_attn = attention_set[4].astype(jnp.float32)
    gain_query = attention_set[5].astype(jnp.float32)
    gain_key = attention_set[6].astype(jnp.float32)
    gain_ffn = attention_set[7].astype(jnp.float32)
    expert_set = (
        lax.all_gather(w_gate, "fsdp", axis=1, tiled=True),
        lax.all_gather(w_up, "fsdp", axis=1, tiled=True),
        lax.all_gather(w_down, "fsdp", axis=1, tiled=True),
    )
    gate_all, up_all, down_all = expert_set
    inputs = tokens[0].astype(jnp.float32)
    normed, attn_pull = jax.vjp(norm_rows, inputs, gain_attn)
    hidden = normed.astype(jnp.bfloat16)
    query_pre = jnp.dot(hidden, query_all, preferred_element_type=jnp.float32)
    key_pre = jnp.dot(hidden, key_all, preferred_element_type=jnp.float32)
    values = jnp.dot(hidden, value_all, preferred_element_type=jnp.float32).astype(jnp.bfloat16)
    query_rot, query_pull = jax.vjp(
        lambda pre_in, gain_in: rotate(norm_rows(pre_in, gain_in), own_pos), query_pre, gain_query
    )
    key_rot, key_pull = jax.vjp(
        lambda pre_in, gain_in: rotate(norm_rows(pre_in, gain_in), own_pos), key_pre, gain_key
    )
    query_low = query_rot.astype(jnp.bfloat16)
    key_low = key_rot.astype(jnp.bfloat16)
    query_heads = query_low.reshape(row_count, head_count, HEAD)
    folder = partial(
        attend_fold,
        query_heads=query_heads,
        own_index=own_index,
        own_seg=own_seg,
        lengths_in=lengths_in,
        prompt_rows=prompt_rows,
        score_scale=score_scale,
    )
    start_state = (
        jnp.full((head_count, row_count), MASKED, jnp.float32),
        jnp.zeros((head_count, row_count), jnp.float32),
        jnp.zeros((head_count, row_count, HEAD), jnp.float32),
    )
    final_state = folder(
        start_state,
        (
            lax.all_gather(key_low, "ctx", axis=0, tiled=True),
            lax.all_gather(values, "ctx", axis=0, tiled=True),
        ),
        jnp.int32(0),
    )
    highest, denominator, weighted = final_state
    log_total = highest + jnp.log(denominator)
    attn_heads = jnp.transpose(weighted / denominator[..., None], (1, 0, 2))
    attended = attn_heads.reshape(row_count, model_width).astype(jnp.bfloat16)
    mixed = inputs + jnp.dot(attended, out_all, preferred_element_type=jnp.float32)
    normed_second, ffn_pull = jax.vjp(norm_rows, mixed, gain_ffn)
    second = normed_second.astype(jnp.bfloat16)
    route_list = routes[0].reshape(-1)
    targets = slot_targets(route_list, expert_total, capacity)

    def dispatch_rows(route_rows):
        buffer = (
            jnp.zeros((expert_total * capacity, model_width), jnp.bfloat16)
            .at[targets]
            .set(route_rows)
        )
        return buffer.reshape(context_size, local_experts * capacity, model_width)

    sent_rows = dispatch_rows(jnp.repeat(second, route_count, axis=0))
    arrived = lax.all_to_all(sent_rows, "ctx", split_axis=0, concat_axis=0, tiled=True).reshape(
        context_size, local_experts, capacity, model_width
    )
    gate_pre = jnp.einsum("sekd,edf->sekf", arrived, gate_all, preferred_element_type=jnp.float32)
    up_pre = jnp.einsum("sekd,edf->sekf", arrived, up_all, preferred_element_type=jnp.float32)
    active = (jax.nn.silu(gate_pre) * up_pre).astype(jnp.bfloat16)
    expert_out = jnp.einsum(
        "sekf,efd->sekd", active, down_all, preferred_element_type=jnp.float32
    ).astype(jnp.bfloat16)
    returned = lax.all_to_all(
        expert_out.reshape(context_size, local_experts * capacity, model_width),
        "ctx",
        split_axis=0,
        concat_axis=0,
        tiled=True,
    )
    per_route = (
        returned.reshape(expert_total * capacity, model_width)[targets]
        .astype(jnp.float32)
        .reshape(row_count, route_count, model_width)
    )
    gate_values = gates[0]
    result = mixed + jnp.sum(gate_values[..., None] * per_route, axis=1)
    output = result[None]
    upstream = cotangent[0].astype(jnp.float32)
    route_grad = (
        (gate_values[..., None] * upstream[:, None, :])
        .astype(jnp.bfloat16)
        .reshape(row_count * route_count, model_width)
    )
    grad_arrived = lax.all_to_all(
        dispatch_rows(route_grad), "ctx", split_axis=0, concat_axis=0, tiled=True
    ).reshape(context_size, local_experts, capacity, model_width)
    active_grad = jnp.einsum(
        "sekd,efd->sekf", grad_arrived, down_all, preferred_element_type=jnp.float32
    )
    down_w_grad = jnp.einsum(
        "sekf,sekd->efd", active, grad_arrived, preferred_element_type=jnp.float32
    )
    sigmoid_gate = jax.nn.sigmoid(gate_pre)
    gate_grad = (
        active_grad * up_pre * sigmoid_gate * (1.0 + gate_pre * (1.0 - sigmoid_gate))
    ).astype(jnp.bfloat16)
    up_grad = (active_grad * gate_pre * sigmoid_gate).astype(jnp.bfloat16)
    gate_w_grad = jnp.einsum(
        "sekd,sekf->edf", arrived, gate_grad, preferred_element_type=jnp.float32
    )
    up_w_grad = jnp.einsum("sekd,sekf->edf", arrived, up_grad, preferred_element_type=jnp.float32)
    arrived_grad = jnp.einsum(
        "sekf,edf->sekd", gate_grad, gate_all, preferred_element_type=jnp.float32
    )
    arrived_grad = (
        arrived_grad
        + jnp.einsum("sekf,edf->sekd", up_grad, up_all, preferred_element_type=jnp.float32)
    ).astype(jnp.bfloat16)
    grad_back = lax.all_to_all(
        arrived_grad.reshape(context_size, local_experts * capacity, model_width),
        "ctx",
        split_axis=0,
        concat_axis=0,
        tiled=True,
    )
    second_grad = jnp.sum(
        grad_back.reshape(expert_total * capacity, model_width)[targets]
        .astype(jnp.float32)
        .reshape(row_count, route_count, model_width),
        axis=1,
    )
    expert_grads = (
        lax.psum_scatter(
            gate_w_grad.astype(jnp.bfloat16), "fsdp", scatter_dimension=1, tiled=True
        ).astype(jnp.float32),
        lax.psum_scatter(
            up_w_grad.astype(jnp.bfloat16), "fsdp", scatter_dimension=1, tiled=True
        ).astype(jnp.float32),
        lax.psum_scatter(
            down_w_grad.astype(jnp.bfloat16), "fsdp", scatter_dimension=1, tiled=True
        ).astype(jnp.float32),
    )
    mixed_norm_grad, ffn_gain_grad = ffn_pull(second_grad)
    mixed_grad = upstream + mixed_norm_grad
    branch_grad = mixed_grad.astype(jnp.bfloat16)
    out_w_grad = jnp.dot(attended.T, branch_grad, preferred_element_type=jnp.float32)
    attended_grad = jnp.dot(branch_grad, out_all.T, preferred_element_type=jnp.float32).astype(
        jnp.bfloat16
    )
    grad_heads = attended_grad.reshape(row_count, head_count, HEAD)
    row_dot = jnp.transpose(jnp.sum(grad_heads.astype(jnp.float32) * attn_heads, axis=-1))
    keys_whole, values_whole = (
        lax.all_gather(key_low, "ctx", axis=0, tiled=True),
        lax.all_gather(values, "ctx", axis=0, tiled=True),
    )
    block_rows = min(1024, all_rows)
    block_count = all_rows // block_rows
    block_index = jnp.arange(all_rows, dtype=jnp.int32).reshape(block_count, block_rows)
    key_blocks = keys_whole.reshape(block_count, block_rows, model_width)
    value_blocks = values_whole.reshape(block_count, block_rows, model_width)

    def query_side(key_rows, value_rows, key_index):
        key_seg, _ = places(key_index, lengths_in, prompt_rows)
        key_heads = key_rows.reshape(block_rows, head_count, HEAD)
        value_heads = value_rows.reshape(block_rows, head_count, HEAD)
        prob, score_grad = pair_terms(
            query_heads,
            grad_heads,
            log_total,
            row_dot,
            own_index,
            own_seg,
            key_heads,
            value_heads,
            key_index,
            key_seg,
            score_scale,
        )
        query_term = (
            jnp.einsum("hqk,khd->qhd", score_grad, key_heads, preferred_element_type=jnp.float32)
            * score_scale
        )
        return (prob, score_grad, query_term)

    def back_block(query_grad, block_args):
        key_rows, value_rows, key_index = block_args
        prob, score_grad, query_term = query_side(key_rows, value_rows, key_index)
        key_term = (
            jnp.einsum("hqk,qhd->khd", score_grad, query_heads, preferred_element_type=jnp.float32)
            * score_scale
        )
        value_term = jnp.einsum(
            "hqk,qhd->khd",
            prob.astype(jnp.bfloat16),
            grad_heads,
            preferred_element_type=jnp.float32,
        )
        return (
            query_grad + query_term,
            (
                key_term.reshape(block_rows, model_width),
                value_term.reshape(block_rows, model_width),
            ),
        )

    query_grad, (key_terms, value_terms) = lax.scan(
        back_block,
        jnp.zeros((row_count, head_count, HEAD), jnp.float32),
        (key_blocks, value_blocks, block_index),
    )
    key_grad, value_grad = (
        lax.psum_scatter(
            key_terms.reshape(all_rows, model_width).astype(jnp.bfloat16),
            "ctx",
            scatter_dimension=0,
            tiled=True,
        ).astype(jnp.float32),
        lax.psum_scatter(
            value_terms.reshape(all_rows, model_width).astype(jnp.bfloat16),
            "ctx",
            scatter_dimension=0,
            tiled=True,
        ).astype(jnp.float32),
    )
    query_pre_grad, query_gain_grad = query_pull(query_grad.reshape(row_count, model_width))
    key_pre_grad, key_gain_grad = key_pull(key_grad)
    query_low_grad = query_pre_grad.astype(jnp.bfloat16)
    key_low_grad = key_pre_grad.astype(jnp.bfloat16)
    value_low_grad = value_grad.astype(jnp.bfloat16)
    query_w_grad = jnp.dot(hidden.T, query_low_grad, preferred_element_type=jnp.float32)
    key_w_grad = jnp.dot(hidden.T, key_low_grad, preferred_element_type=jnp.float32)
    value_w_grad = jnp.dot(hidden.T, value_low_grad, preferred_element_type=jnp.float32)
    hidden_grad = jnp.dot(query_low_grad, query_all.T, preferred_element_type=jnp.float32)
    hidden_grad = hidden_grad + jnp.dot(key_low_grad, key_all.T, preferred_element_type=jnp.float32)
    hidden_grad = hidden_grad + jnp.dot(
        value_low_grad, value_all.T, preferred_element_type=jnp.float32
    )
    input_norm_grad, attn_gain_grad = attn_pull(hidden_grad)
    input_grad = (mixed_grad + input_norm_grad)[None]
    summed_grads = (
        lax.psum_scatter(query_w_grad, ("ctx", "fsdp"), scatter_dimension=0, tiled=True),
        lax.psum_scatter(key_w_grad, ("ctx", "fsdp"), scatter_dimension=0, tiled=True),
        lax.psum_scatter(value_w_grad, ("ctx", "fsdp"), scatter_dimension=0, tiled=True),
        lax.psum_scatter(out_w_grad, ("ctx", "fsdp"), scatter_dimension=0, tiled=True),
        lax.psum_scatter(attn_gain_grad, ("ctx", "fsdp"), scatter_dimension=0, tiled=True),
        lax.psum_scatter(query_gain_grad, ("ctx", "fsdp"), scatter_dimension=0, tiled=True),
        lax.psum_scatter(key_gain_grad, ("ctx", "fsdp"), scatter_dimension=0, tiled=True),
        lax.psum_scatter(ffn_gain_grad, ("ctx", "fsdp"), scatter_dimension=0, tiled=True),
    )
    return (
        output,
        input_grad,
        summed_grads[4],
        summed_grads[5],
        summed_grads[6],
        summed_grads[7],
        summed_grads[0],
        summed_grads[1],
        summed_grads[2],
        summed_grads[3],
        expert_grads[0],
        expert_grads[1],
        expert_grads[2],
    )


HEADS = 16
LOG2E = 1.4426950408889634
VMEM_BYTES = 60 * 2**20


def dot_nn(left, right):
    return lax.dot_general(
        left, right, (((1,), (0,)), ((), ())), preferred_element_type=jnp.float32
    )


def dot_nt(left, right):
    return lax.dot_general(
        left, right, (((1,), (1,)), ((), ())), preferred_element_type=jnp.float32
    )


def dot_tn(left, right):
    return lax.dot_general(
        left, right, (((0,), (0,)), ((), ())), preferred_element_type=jnp.float32
    )


def segment_start(starts, index):
    first = starts[0]
    for c in range(1, starts.shape[0]):
        first = jnp.where(index >= starts[c], starts[c], first)
    return first


def segment_end(starts, index, total):
    last = jnp.int32(total)
    for c in range(starts.shape[0] - 1, 0, -1):
        last = jnp.where(index < starts[c], starts[c], last)
    return last


def allowed_tile(starts, key_first, query_first, size, prompt_rows):
    key_index = key_first + lax.broadcasted_iota(jnp.int32, (size, size), 0)
    query_index = query_first + lax.broadcasted_iota(jnp.int32, (1, size), 1)
    own_start = jnp.full((1, size), prompt_rows, jnp.int32)
    for c in range(1, starts.shape[0]):
        own_start = jnp.where(query_index >= starts[c], starts[c], own_start)
    return (key_index <= query_index) & ((key_index < prompt_rows) | (key_index >= own_start))


def attend_forward_kernel(
    starts,
    query_pre,
    key_pre,
    value_t,
    query_inv,
    key_inv,
    query_gain,
    key_gain,
    cosine,
    sine,
    out,
    query,
    key,
    key_t,
    log_rows,
    *,
    size,
    prompt_rows,
    score_scale,
):
    i = pl.program_id(0)
    half = HEAD // 2
    total, columns = key.shape
    spans = [slice(h * HEAD, (h + 1) * HEAD) for h in range(columns // HEAD)]
    prompt_blocks = prompt_rows // size

    @pl.when(i == 0)
    def _():
        @pl.loop(0, total // size)
        def _(b):
            at = pl.ds(pl.multiple_of(b * size, size), size)
            cos, sin = cosine[:, at], sine[:, at]
            for span in spans:
                for pre, inv, gain, is_key in (
                    (query_pre, query_inv, query_gain, False),
                    (key_pre, key_inv, key_gain, True),
                ):
                    normed = pre[span, at] * inv[:, at] * gain[span, :]
                    former, latter = normed[:half], normed[half:]
                    turned = jnp.concatenate(
                        [former * cos - latter * sin, latter * cos + former * sin], axis=0
                    )
                    if is_key:
                        key_t[span, at] = turned.astype(jnp.bfloat16)
                        key[at, span] = turned.T.astype(jnp.bfloat16)
                    else:
                        turned = turned * (score_scale * LOG2E)
                        query[at, span] = turned.T.astype(jnp.bfloat16)

    query_first = i * size
    here = pl.ds(pl.multiple_of(query_first, size), size)
    chunk = size // 2
    parts = [slice(c * chunk, (c + 1) * chunk) for c in range(2)]
    work = [(span, part) for span in spans for part in parts]
    query_all = [query[here, span] for span in spans]
    query_rows = [rows[part] for rows in query_all for part in parts]

    def fold(j, states, masked):
        at = pl.ds(pl.multiple_of(j * size, size), size)
        scores = [dot_nt(key[at, span], rows) for (span, _), rows in zip(work, query_rows)]
        if masked:
            allowed = allowed_tile(starts, j * size, query_first, size, prompt_rows)
        made = []
        for (span, part), score, (highest, denominator, weighted) in zip(work, scores, states):
            if masked:
                score = jnp.where(allowed[:, part], score, MASKED)
            new_high = jnp.maximum(highest, jnp.max(score, axis=0, keepdims=True))
            shrink = jnp.exp2(highest - new_high)
            unnormed = jnp.exp2(score - new_high)
            denominator = denominator * shrink + jnp.sum(unnormed, axis=0, keepdims=True)
            weighted = weighted * shrink + dot_nn(value_t[span, at], unnormed.astype(jnp.bfloat16))
            made.append((new_high, denominator, weighted))
        return tuple(made)

    states = tuple(
        (
            jnp.full((1, chunk), MASKED, jnp.float32),
            jnp.zeros((1, chunk), jnp.float32),
            jnp.zeros((HEAD, chunk), jnp.float32),
        )
        for _ in work
    )
    in_prompt = i < prompt_blocks
    whole = jnp.where(in_prompt, i, prompt_blocks)
    states = lax.fori_loop(0, whole, lambda j, s: fold(j, s, False), states)
    own_first = jnp.where(in_prompt, i, segment_start(starts, query_first) // size)
    states = lax.fori_loop(own_first, i + 1, lambda j, s: fold(j, s, True), states)
    for k, ((span, part), (highest, denominator, weighted)) in enumerate(zip(work, states)):
        out[part, span] = (weighted / denominator).T.astype(jnp.bfloat16)
        log_rows[k // 2 : k // 2 + 1, part] = highest + jnp.log2(denominator)


def attend_forward(starts, query_pre, key_pre, value_t, query_inv, key_inv, query_gain, key_gain, cosine, sine, size, prompt_rows, score_scale):
    columns, total = query_pre.shape
    heads = columns // HEAD
    pairs = total * total // 2

    def once(shape):
        return pl.BlockSpec(shape, lambda i, s: (0, 0), pipeline_mode=pl.Buffered(1))

    wide, tall, row = (columns, total), (total, columns), (1, total)
    gain, table = (columns, 1), (HEAD // 2, total)
    return pl.pallas_call(
        partial(attend_forward_kernel, size=size, prompt_rows=prompt_rows, score_scale=score_scale),
        grid_spec=pltpu.PrefetchScalarGridSpec(
            num_scalar_prefetch=1,
            grid=(total // size,),
            in_specs=[once(k) for k in (wide, wide, wide, row, row, gain, gain, table, table)],
            out_specs=[
                pl.BlockSpec((size, columns), lambda i, s: (i, 0)),
                pl.BlockSpec(tall, lambda i, s: (0, 0)),
                pl.BlockSpec(tall, lambda i, s: (0, 0)),
                pl.BlockSpec(wide, lambda i, s: (0, 0)),
                pl.BlockSpec((heads, size), lambda i, s: (0, i)),
            ],
        ),
        out_shape=[
            jax.ShapeDtypeStruct(tall, jnp.bfloat16),
            jax.ShapeDtypeStruct(tall, jnp.bfloat16),
            jax.ShapeDtypeStruct(tall, jnp.bfloat16),
            jax.ShapeDtypeStruct(wide, jnp.bfloat16),
            jax.ShapeDtypeStruct((heads, total), jnp.float32),
        ],
        compiler_params=pltpu.CompilerParams(vmem_limit_bytes=VMEM_BYTES),
        cost_estimate=pl.CostEstimate(
            flops=12 * pairs * columns, bytes_accessed=20 * total * columns, transcendentals=pairs * heads
        ),
        name="attend_forward",
    )(starts, query_pre, key_pre, value_t, query_inv, key_inv, query_gain, key_gain, cosine, sine)


def attend_backward_kernel(
    starts,
    query,
    key,
    key_t,
    value_t,
    out_grad,
    out,
    log_rows,
    query_pre,
    key_pre,
    query_inv,
    key_inv,
    query_gain,
    key_gain,
    cosine,
    sine,
    *refs,
    size,
    prompt_rows,
    score_scale,
):
    query_scaled, key_scaled, value_grad, query_gain_grad, key_gain_grad, dots = refs[-9:-3]
    query_sum, key_sum, row_dot = refs[-3:]
    j = pl.program_id(0)
    half = HEAD // 2
    total, columns = key.shape
    spans = [slice(h * HEAD, (h + 1) * HEAD) for h in range(columns // HEAD)]
    blocks = total // size
    prompt_blocks = prompt_rows // size

    @pl.when(j == 0)
    def _():
        query_sum[...] = jnp.zeros_like(query_sum)

        @pl.loop(0, blocks)
        def _(b):
            at = pl.ds(pl.multiple_of(b * size, size), size)
            for h, span in enumerate(spans):
                product = out_grad[at, span].astype(jnp.float32) * out[at, span].astype(jnp.float32)
                row_dot[h : h + 1, at] = jnp.sum(product.T, axis=0, keepdims=True)

    chunk = size // 2
    here = pl.ds(pl.multiple_of(j * size, size), size)
    key_rows = [key[here, span] for span in spans]
    key_cols = [key_t[span, here] for span in spans]
    value_rows = [value_t[span, here].T for span in spans]

    def fold(i, states, masked):
        if masked:
            allowed = allowed_tile(starts, j * size, i * size, size, prompt_rows)
        made = list(states)
        for c in range(2):
            at = pl.ds(pl.multiple_of(i * size + c * chunk, chunk), chunk)
            query_rows = [query[at, span] for span in spans]
            grad_rows = [out_grad[at, span] for span in spans]
            scores = [dot_nt(k, q) for k, q in zip(key_rows, query_rows)]
            prob_grads = [dot_nt(v, g) for v, g in zip(value_rows, grad_rows)]
            for h, span in enumerate(spans):
                key_part, value_part = made[h]
                prob = jnp.exp2(scores[h] - log_rows[h, :, at])
                if masked:
                    prob = jnp.where(allowed[:, c * chunk : (c + 1) * chunk], prob, 0.0)
                score_grad = (prob * (prob_grads[h] - row_dot[h : h + 1, at])).astype(jnp.bfloat16)
                value_part = value_part + dot_nn(prob.astype(jnp.bfloat16), grad_rows[h])
                key_part = key_part + dot_nn(score_grad, query_rows[h])
                query_sum[span, at] += dot_nn(key_cols[h], score_grad)
                made[h] = (key_part, value_part)
        return tuple(made)

    states = tuple(
        (jnp.zeros((size, HEAD), jnp.float32), jnp.zeros((size, HEAD), jnp.float32)) for _ in spans
    )
    in_prompt = j < prompt_blocks
    last_own = (segment_end(starts, (j + 1) * size - 1, total) - 1) // size + 1
    masked_end = jnp.where(in_prompt, j + 1, last_own)
    states = lax.fori_loop(j, masked_end, lambda i, s: fold(i, s, True), states)
    whole_end = jnp.where(in_prompt, blocks, masked_end)
    states = lax.fori_loop(masked_end, whole_end, lambda i, s: fold(i, s, False), states)
    for span, (key_part, value_part) in zip(spans, states):
        key_sum[span, here] = key_part.T
        value_grad[span, here] = value_part.T.astype(jnp.bfloat16)

    @pl.when(j == blocks - 1)
    def _():
        query_gain_grad[...] = jnp.zeros_like(query_gain_grad)
        key_gain_grad[...] = jnp.zeros_like(key_gain_grad)

        @pl.loop(0, blocks)
        def _(b):
            at = pl.ds(pl.multiple_of(b * size, size), size)
            cos, sin = cosine[:, at], sine[:, at]
            for place, (grad, factor, pre, inv, gain, scaled, gain_grad) in enumerate(
                (
                    (query_sum, score_scale, query_pre, query_inv, query_gain, query_scaled, query_gain_grad),
                    (key_sum, 1.0 / LOG2E, key_pre, key_inv, key_gain, key_scaled, key_gain_grad),
                )
            ):
                summed = None
                for span in spans:
                    turned = grad[span, at] * factor
                    former, latter = turned[:half], turned[half:]
                    back = jnp.concatenate(
                        [former * cos + latter * sin, latter * cos - former * sin], axis=0
                    )
                    before = pre[span, at]
                    gain_grad[span, :] += jnp.sum(
                        back * (before * inv[:, at]), axis=1, keepdims=True
                    )
                    back = back * gain[span, :]
                    scaled[span, at] = back
                    dot = jnp.sum(back * before, axis=0, keepdims=True)
                    summed = dot if summed is None else summed + dot
                dots[place : place + 1, at] = summed


def attend_backward(starts, head, held, query, key, key_t, value_t, out_grad, out, log_rows, query_pre, key_pre, query_inv, key_inv, query_gain, key_gain, cosine, sine, size, prompt_rows, score_scale):
    columns, total = query_pre.shape
    pairs = total * total // 2
    held = () if held is None else tuple(held)

    def once(shape, index):
        return pl.BlockSpec(shape, lambda j, s: index, pipeline_mode=pl.Buffered(1))

    wide, tall = once((HEAD, total), (head, 0)), once((total, HEAD), (0, head))
    row, table = once((1, total), (0, 0)), once((HEAD // 2, total), (0, 0))
    gain, per_head = once((HEAD, 1), (head, 0)), once((1, 1, total), (head, 0, 0))
    return pl.pallas_call(
        partial(attend_backward_kernel, size=size, prompt_rows=prompt_rows, score_scale=score_scale),
        grid_spec=pltpu.PrefetchScalarGridSpec(
            num_scalar_prefetch=1,
            grid=(total // size,),
            in_specs=[tall, tall, wide, wide, tall, tall, per_head, wide, wide, row, row, gain, gain, table, table]
            + [pl.BlockSpec(memory_space=pl.ANY)] * len(held),
            out_specs=[wide, wide, wide, gain, gain, once((2, total), (0, 0))],
            scratch_shapes=[
                pltpu.VMEM((HEAD, total), jnp.float32),
                pltpu.VMEM((HEAD, total), jnp.float32),
                pltpu.VMEM((1, total), jnp.float32),
            ],
        ),
        out_shape=[
            jax.ShapeDtypeStruct((columns, total), jnp.float32),
            jax.ShapeDtypeStruct((columns, total), jnp.float32),
            jax.ShapeDtypeStruct((columns, total), jnp.bfloat16),
            jax.ShapeDtypeStruct((columns, 1), jnp.float32),
            jax.ShapeDtypeStruct((columns, 1), jnp.float32),
            jax.ShapeDtypeStruct((2, total), jnp.float32),
        ],
        input_output_aliases={16 + k: k for k in range(len(held))},
        compiler_params=pltpu.CompilerParams(vmem_limit_bytes=VMEM_BYTES),
        cost_estimate=pl.CostEstimate(
            flops=24 * pairs * HEAD, bytes_accessed=40 * total * HEAD, transcendentals=pairs
        ),
        name="attend_backward",
    )(starts, query, key, key_t, value_t, out_grad, out, log_rows, query_pre, key_pre, query_inv, key_inv, query_gain, key_gain, cosine, sine, *held)


def project_kernel(places, *refs, count):
    blocks = refs[:count]
    w_t, gain = refs[count : count + 2]
    hidden, query_pre, key_pre, value_t, squares = refs[-5:]
    columns = query_pre.shape[0]
    for b, block in enumerate(blocks):

        @pl.when(pl.program_id(0) // 2 == b)
        def _(block=block):
            rows = block[...].astype(jnp.float32)
            inverse = lax.rsqrt(jnp.mean(rows * rows, axis=-1, keepdims=True) + EPSILON)
            hidden[...] = (rows * inverse * gain[...]).astype(jnp.bfloat16)

    for k, out in enumerate((query_pre, key_pre)):
        made = dot_nt(w_t[k * columns : (k + 1) * columns, :], hidden[...])
        out[...] = made
        squares[k : k + 1, :] = jnp.sum(made * made, axis=0, keepdims=True)
    value_t[...] = dot_nt(w_t[2 * columns :, :], hidden[...]).astype(jnp.bfloat16)


def project(places, blocks, rows, w_t, gain, held, total):
    count, width = len(blocks), blocks[0].shape[1]
    columns = w_t.shape[0] // 3
    tile = rows // 2
    held = () if held is None else tuple(held)

    def block_spec(b):
        return pl.BlockSpec((tile, width), lambda i, p: (jnp.clip(i - 2 * b, 0, 1), 0))

    def there(shape, along):
        if along == 0:
            return pl.BlockSpec(shape, lambda i, p: (2 * p[i // 2] + i % 2, 0))
        return pl.BlockSpec(shape, lambda i, p: (0, 2 * p[i // 2] + i % 2))

    return pl.pallas_call(
        partial(project_kernel, count=count),
        grid_spec=pltpu.PrefetchScalarGridSpec(
            num_scalar_prefetch=1,
            grid=(2 * count,),
            in_specs=[block_spec(b) for b in range(count)]
            + [
                pl.BlockSpec(w_t.shape, lambda i, p: (0, 0)),
                pl.BlockSpec((1, width), lambda i, p: (0, 0)),
            ]
            + [pl.BlockSpec(memory_space=pl.ANY)] * len(held),
            out_specs=[
                there((tile, width), 0),
                there((columns, tile), 1),
                there((columns, tile), 1),
                there((columns, tile), 1),
                there((2, tile), 1),
            ],
        ),
        out_shape=[
            jax.ShapeDtypeStruct((total, width), jnp.bfloat16),
            jax.ShapeDtypeStruct((columns, total), jnp.float32),
            jax.ShapeDtypeStruct((columns, total), jnp.float32),
            jax.ShapeDtypeStruct((columns, total), jnp.bfloat16),
            jax.ShapeDtypeStruct((2, total), jnp.float32),
        ],
        input_output_aliases={3 + count + k: k for k in range(len(held))},
        compiler_params=pltpu.CompilerParams(vmem_limit_bytes=VMEM_BYTES),
        cost_estimate=pl.CostEstimate(
            flops=6 * count * rows * width * columns,
            bytes_accessed=count * (4 * rows * width + 10 * rows * columns) + 6 * width * columns,
            transcendentals=count * rows,
        ),
        name="project",
    )(places, *blocks, w_t, gain, *held)


def place_rows_kernel(places, *refs):
    *pieces, out = refs
    for k, piece in enumerate(pieces):
        out[places[k]] = piece[...]


def place_rows(places, blocks, first, rows):
    width = blocks[0].shape[1]
    return pl.pallas_call(
        place_rows_kernel,
        grid_spec=pltpu.PrefetchScalarGridSpec(
            num_scalar_prefetch=1,
            grid=(1,),
            in_specs=[pl.BlockSpec((rows, width), lambda i, p: (first // rows, 0))] * len(blocks),
            out_specs=pl.BlockSpec((len(blocks), rows, width), lambda i, p: (0, 0, 0)),
        ),
        out_shape=jax.ShapeDtypeStruct((len(blocks), rows, width), blocks[0].dtype),
        compiler_params=pltpu.CompilerParams(vmem_limit_bytes=VMEM_BYTES),
        name="place_rows",
    )(places, *blocks)


def hidden_term_kernel(place, heads_grad, w_t, out_rows, *refs, start, halves):
    outs = refs[-2:] if halves else refs[-1:]
    rows = heads_grad.shape[1]
    term = dot_tn(heads_grad[...], w_t[...])
    below = out_rows[0]
    if halves:
        cut = outs[0].shape[0]
        outs[0][...] = term[:cut].astype(jnp.bfloat16)
        outs[1][: rows - cut, :] = term[cut:].astype(jnp.bfloat16)
        outs[1][rows - cut :, :] = below
        return
    (out,) = outs
    got = refs[0]
    stop = start + got.shape[0]
    upper = min(stop, rows)
    if start:
        out[:start, :] = term[:start].astype(jnp.bfloat16)
    if upper < rows:
        out[upper:rows, :] = term[upper:].astype(jnp.bfloat16)
    out[start:upper, :] = (
        term[start:upper] + got[: upper - start, :].astype(jnp.float32)
    ).astype(jnp.bfloat16)
    if stop > rows:
        below = below.astype(jnp.float32) + got[rows - start :, :].astype(jnp.float32)
    out[rows:, :] = below.astype(jnp.bfloat16)


def hidden_term(place, heads_grad, w_t, out_rows, rows, got=None, start=0):
    columns, width = w_t.shape
    whole = rows + out_rows.shape[1]
    tile = min(512, width)
    halves = got is None
    gots, outs = ([], [whole // 2] * 2) if halves else ([got], [whole])
    made = pl.pallas_call(
        partial(hidden_term_kernel, start=start, halves=halves),
        grid_spec=pltpu.PrefetchScalarGridSpec(
            num_scalar_prefetch=1,
            grid=(width // tile,),
            in_specs=[
                pl.BlockSpec((columns, rows), lambda i, p: (0, p[0])),
                pl.BlockSpec((columns, tile), lambda i, p: (0, i)),
                pl.BlockSpec((1, whole - rows, tile), lambda i, p: (p[0], 0, i)),
            ]
            + [pl.BlockSpec((g.shape[0], tile), lambda i, p: (0, i)) for g in gots],
            out_specs=[pl.BlockSpec((count, tile), lambda i, p: (0, i)) for count in outs],
        ),
        out_shape=[jax.ShapeDtypeStruct((count, width), jnp.bfloat16) for count in outs],
        compiler_params=pltpu.CompilerParams(vmem_limit_bytes=VMEM_BYTES),
        cost_estimate=pl.CostEstimate(
            flops=0, bytes_accessed=0, transcendentals=0
        ),
        name="hidden_term",
    )(place, heads_grad, w_t, out_rows, *gots)
    return made if halves else made[0]


def input_grad_kernel(place, heads_grad, w_t, before, past, tokens, gain, mixed_grad, out):
    got = before[...].astype(jnp.float32) + past[...].astype(jnp.float32)
    scaled = (dot_tn(heads_grad[...], w_t[...]) + got) * gain[...]
    inputs = tokens[...].astype(jnp.float32)
    inverse = lax.rsqrt(jnp.mean(inputs * inputs, axis=-1, keepdims=True) + EPSILON)
    normed = inputs * inverse
    along = jnp.mean(scaled * normed, axis=-1, keepdims=True)
    out[...] = mixed_grad[...] + inverse * (scaled - normed * along)


def input_grad_of(place, heads_grad, w_t, before, past, tokens, gain, mixed_grad):
    columns, width = w_t.shape
    rows = tokens.shape[0]
    tile = rows // 4
    block = pl.BlockSpec((tile, width), lambda i, p: (i, 0))
    return pl.pallas_call(
        input_grad_kernel,
        grid_spec=pltpu.PrefetchScalarGridSpec(
            num_scalar_prefetch=1,
            grid=(4,),
            in_specs=[
                pl.BlockSpec((columns, tile), lambda i, p: (0, 4 * p[0] + i)),
                pl.BlockSpec((columns, width), lambda i, p: (0, 0)),
                block,
                block,
                block,
                pl.BlockSpec((1, width), lambda i, p: (0, 0)),
                block,
            ],
            out_specs=block,
        ),
        out_shape=jax.ShapeDtypeStruct((rows, width), jnp.float32),
        compiler_params=pltpu.CompilerParams(vmem_limit_bytes=VMEM_BYTES),
        cost_estimate=pl.CostEstimate(
            flops=2 * rows * width * columns,
            bytes_accessed=2 * columns * (rows + width) + 14 * rows * width,
            transcendentals=rows,
        ),
        name="input_grad",
    )(place, heads_grad, w_t, before, past, tokens, gain, mixed_grad)


def mixed_grad_kernel(own, before, past, mixed, cotangent, gain, mixed_grad, branch, gain_grad):
    second_grad = (
        own[...].astype(jnp.float32)
        + before[...].astype(jnp.float32)
        + past[...].astype(jnp.float32)
    )
    values = mixed[...]
    inverse = lax.rsqrt(jnp.mean(values * values, axis=-1, keepdims=True) + EPSILON)
    normed = values * inverse
    scaled = second_grad * gain[...]
    along = jnp.mean(scaled * normed, axis=-1, keepdims=True)
    made = cotangent[...].astype(jnp.float32) + inverse * (scaled - normed * along)
    mixed_grad[...] = made
    branch[...] = made.astype(jnp.bfloat16)
    part = jnp.sum(second_grad * normed, axis=0, keepdims=True)

    @pl.when(pl.program_id(0) == 0)
    def _():
        gain_grad[...] = part

    @pl.when(pl.program_id(0) > 0)
    def _():
        gain_grad[...] += part


def mixed_grad_of(own, before, past, mixed, cotangent, gain):
    rows, width = mixed.shape
    block = pl.BlockSpec((rows // 4, width), lambda i: (i, 0))
    line = pl.BlockSpec((1, width), lambda i: (0, 0))
    return pl.pallas_call(
        mixed_grad_kernel,
        grid=(4,),
        in_specs=[block] * 5 + [line],
        out_specs=[block, block, line],
        out_shape=[
            jax.ShapeDtypeStruct((rows, width), jnp.float32),
            jax.ShapeDtypeStruct((rows, width), jnp.bfloat16),
            jax.ShapeDtypeStruct((1, width), jnp.float32),
        ],
        compiler_params=pltpu.CompilerParams(vmem_limit_bytes=VMEM_BYTES),
        cost_estimate=pl.CostEstimate(
            flops=16 * rows * width, bytes_accessed=18 * rows * width, transcendentals=rows
        ),
        name="mixed_grad",
    )(own, before, past, mixed, cotangent, gain)


def out_grad_kernel(branch, w_out, out):
    made = dot_nt(branch[...], w_out[...]).astype(jnp.bfloat16)
    columns = out.shape[2]
    for k in range(out.shape[0]):
        out[k] = made[:, k * columns : (k + 1) * columns]


def out_grad_of(branch, w_out, contexts):
    rows, width = branch.shape
    columns = w_out.shape[0] // contexts
    return pl.pallas_call(
        out_grad_kernel,
        grid=(contexts // 2,),
        in_specs=[
            pl.BlockSpec((rows, width), lambda i: (0, 0)),
            pl.BlockSpec((2 * columns, width), lambda i: (i, 0)),
        ],
        out_specs=pl.BlockSpec((2, rows, columns), lambda i: (i, 0, 0)),
        out_shape=jax.ShapeDtypeStruct((contexts, rows, columns), jnp.bfloat16),
        compiler_params=pltpu.CompilerParams(vmem_limit_bytes=VMEM_BYTES),
        cost_estimate=pl.CostEstimate(
            flops=2 * rows * width * width, bytes_accessed=2 * width * width, transcendentals=0
        ),
        name="out_grad",
    )(branch, w_out)


def heads_grad_kernel(query_scaled, key_scaled, value_grad, query_pre, key_pre, inverse, dots, out):
    columns = query_scaled.shape[0]
    for k, (scaled, pre) in enumerate(((query_scaled, query_pre), (key_scaled, key_pre))):
        inv = inverse[k : k + 1, :]
        factor = inv * inv * dots[k : k + 1, :]
        out[k * columns : (k + 1) * columns, :] = (inv * (scaled[...] - pre[...] * factor)).astype(
            jnp.bfloat16
        )
    out[2 * columns :, :] = value_grad[...]


def heads_grad_of(query_scaled, key_scaled, value_grad, query_pre, key_pre, inverse, dots):
    columns, total = query_scaled.shape
    tile = total // 4
    wide = pl.BlockSpec((columns, tile), lambda i: (0, i))
    row = pl.BlockSpec((2, tile), lambda i: (0, i))
    return pl.pallas_call(
        heads_grad_kernel,
        grid=(4,),
        in_specs=[wide] * 5 + [row] * 2,
        out_specs=pl.BlockSpec((3 * columns, tile), lambda i: (0, i)),
        out_shape=jax.ShapeDtypeStruct((3 * columns, total), jnp.bfloat16),
        compiler_params=pltpu.CompilerParams(vmem_limit_bytes=VMEM_BYTES),
        cost_estimate=pl.CostEstimate(
            flops=8 * columns * total, bytes_accessed=24 * columns * total, transcendentals=0
        ),
        name="heads_grad",
    )(query_scaled, key_scaled, value_grad, query_pre, key_pre, inverse, dots)


def heads_product_kernel(heads_grad, hidden, others, out):
    columns = heads_grad.shape[0]
    out[0, :, :columns] = dot_nn(heads_grad[...], hidden[...]).T.astype(jnp.bfloat16)
    out[0, :, columns:] = others[...].astype(jnp.bfloat16)


def heads_product_of(heads_grad, hidden_all, others, contexts):
    columns, total = heads_grad.shape
    width = hidden_all.shape[1]
    tile, extra = width // contexts, others.shape[1]
    return pl.pallas_call(
        heads_product_kernel,
        grid=(contexts,),
        in_specs=[
            pl.BlockSpec((columns, total), lambda i: (0, 0), pipeline_mode=pl.Buffered(1)),
            pl.BlockSpec((total, tile), lambda i: (0, i)),
            pl.BlockSpec((tile, extra), lambda i: (i, 0)),
        ],
        out_specs=pl.BlockSpec((1, tile, columns + extra), lambda i: (i, 0, 0)),
        out_shape=jax.ShapeDtypeStruct((contexts, tile, columns + extra), jnp.bfloat16),
        compiler_params=pltpu.CompilerParams(vmem_limit_bytes=VMEM_BYTES),
        cost_estimate=pl.CostEstimate(
            flops=2 * columns * total * width,
            bytes_accessed=2 * total * (columns + width),
            transcendentals=0,
        ),
        name="heads_product",
    )(heads_grad, hidden_all, others)


def gather_pieces_kernel(me, *refs):
    *pieces, out = refs
    for step, piece in enumerate(pieces):
        out[lax.rem(me[0] + step, len(pieces))] = piece[...]


def gather_pieces(me, pieces):
    return pl.pallas_call(
        gather_pieces_kernel,
        grid_spec=pltpu.PrefetchScalarGridSpec(
            num_scalar_prefetch=1,
            grid=(1,),
            in_specs=[pl.BlockSpec(piece.shape, lambda i, m: (0, 0)) for piece in pieces],
            out_specs=pl.BlockSpec((len(pieces),) + pieces[0].shape, lambda i, m: (0, 0, 0)),
        ),
        out_shape=jax.ShapeDtypeStruct((len(pieces),) + pieces[0].shape, pieces[0].dtype),
        compiler_params=pltpu.CompilerParams(vmem_limit_bytes=VMEM_BYTES),
        name="gather_pieces",
    )(me[None], *pieces)


def slot_match(rank_row, slots):
    return lax.broadcasted_iota(jnp.int32, (slots, rank_row.shape[1]), 0) == rank_row


def slot_gates(match, gate_row):
    return jnp.sum(jnp.where(match, gate_row, 0.0), axis=1, keepdims=True)


def take_rows(match, pieces):
    first, made = 0, 0.0
    for piece in pieces:
        last = first + piece.shape[0]
        made = made + dot_nn(match[:, first:last], piece[...])
        first = last
    return made


def pieces_of(refs, count):
    size = len(refs) // count
    return [refs[b * size : (b + 1) * size] for b in range(count)]


def experts_forward_kernel(*refs, count, pieces, slots, aliased, tiles):
    ranks, gates = refs[:2]
    blocks = pieces_of(refs[2 : 2 + pieces], count)
    w_gate, w_up, w_down = refs[2 + pieces : 5 + pieces]
    refs = refs[5 + pieces + aliased :]
    taken, active, gate_slope, up_slope = refs[:4]
    outs = pieces_of(refs[4 : 4 + pieces], count)
    made, weights = refs[4 + pieces :]
    e, f = pl.program_id(0), pl.program_id(1)
    tile, wide_tile = w_gate.shape[2], w_down.shape[2]

    @pl.when(f == 0)
    def _():
        for b in range(count):
            here = slice(b * slots, (b + 1) * slots)
            match = slot_match(ranks[b, e], slots)
            weights[here, :] = slot_gates(match, gates[b, e])
            taken[0, here, :] = take_rows(match.astype(jnp.bfloat16), blocks[b]).astype(
                jnp.bfloat16
            )

    @pl.when(f < tiles)
    def _():
        at = pl.ds(pl.multiple_of(f * tile, tile), tile)
        rows = taken[0]
        gate_pre = dot_nn(rows, w_gate[0])
        up_pre = dot_nn(rows, w_up[0])
        sigmoid_gate = 1.0 / (1.0 + jnp.exp(-gate_pre))
        silu = gate_pre * sigmoid_gate
        active[0, :, at] = (silu * up_pre).astype(jnp.bfloat16)
        up_slope[0, :, at] = silu.astype(jnp.bfloat16)
        gate_slope[0, :, at] = (up_pre * (sigmoid_gate + silu * (1.0 - sigmoid_gate))).astype(
            jnp.bfloat16
        )

    @pl.when(f >= tiles)
    def _():
        at = pl.ds(pl.multiple_of((f - tiles) * wide_tile, wide_tile), wide_tile)
        made[e, :, at] = (dot_nn(active[0], w_down[0]) * weights[...]).astype(jnp.bfloat16)

    @pl.when((f == pl.num_programs(1) - 1) & (e == pl.num_programs(0) - 1))
    def _():
        combine(ranks, made, outs, count, slots)


def combine(ranks, made, outs, count, slots):
    for b in range(count):
        summed = None
        for k in range(made.shape[0]):
            match = slot_match(ranks[b, k], slots).astype(jnp.float32).astype(jnp.bfloat16)
            term = dot_tn(match, made[k, b * slots : (b + 1) * slots, :])
            summed = term if summed is None else summed + term
        first = 0
        for out in outs[b]:
            last = first + out.shape[0]
            out[...] = summed[first:last].astype(jnp.bfloat16)
            first = last


def experts_backward_kernel(*refs, count, pieces, slots, aliased, tiles):
    ranks, gates = refs[:2]
    blocks = pieces_of(refs[2 : 2 + pieces], count)
    w_gate, w_up, w_down, gate_slope, up_slope = refs[2 + pieces : 7 + pieces]
    refs = refs[7 + pieces + aliased :]
    taken, gate_grad, up_grad = refs[:3]
    outs = pieces_of(refs[3 : 3 + pieces], count)
    (made,) = refs[3 + pieces :]
    e, f = pl.program_id(0), pl.program_id(1)
    tile, wide_tile = w_down.shape[1], w_gate.shape[1]

    @pl.when(f == 0)
    def _():
        for b in range(count):
            match = slot_match(ranks[b, e], slots)
            weight = slot_gates(match, gates[b, e])
            taken[0, b * slots : (b + 1) * slots, :] = (
                take_rows(match.astype(jnp.bfloat16), blocks[b]) * weight
            ).astype(jnp.bfloat16)

    @pl.when(f < tiles)
    def _():
        at = pl.ds(pl.multiple_of(f * tile, tile), tile)
        active_grad = dot_nt(taken[0], w_down[0])
        gate_grad[0, :, at] = (active_grad * gate_slope[0].astype(jnp.float32)).astype(jnp.bfloat16)
        up_grad[0, :, at] = (active_grad * up_slope[0].astype(jnp.float32)).astype(jnp.bfloat16)

    @pl.when(f >= tiles)
    def _():
        at = pl.ds(pl.multiple_of((f - tiles) * wide_tile, wide_tile), wide_tile)
        made[e, :, at] = (dot_nt(gate_grad[0], w_gate[0]) + dot_nt(up_grad[0], w_up[0])).astype(
            jnp.bfloat16
        )

    @pl.when((f == pl.num_programs(1) - 1) & (e == pl.num_programs(0) - 1))
    def _():
        combine(ranks, made, outs, count, slots)


def experts_stage(
    forward, ranks, gates, blocks, weights, slopes, held, place, slots, all_slots, light=False
):
    count, pieces = ranks.shape[0], len(blocks)
    rows, width = ranks.shape[3], blocks[0].shape[1]
    experts, _, hidden_units = weights[0].shape
    tile, wide_tile = min(512, hidden_units), min(1024, width)
    tiles, wide_tiles = hidden_units // tile, width // wide_tile
    part = count * slots

    def first(f):
        return jnp.minimum(f, tiles - 1)

    def later(f):
        return jnp.maximum(f - tiles, 0)

    info = pl.BlockSpec((count, experts, 1, rows), lambda e, f: (0, 0, 0, 0))
    block = pl.BlockSpec(blocks[0].shape, lambda e, f: (0, 0))
    wide = pl.BlockSpec((1, part, width), lambda e, f: (e, place, 0))
    narrow = pl.BlockSpec((1, part, hidden_units), lambda e, f: (e, place, 0))
    slope = pl.BlockSpec((1, part, tile), lambda e, f: (e, 0, first(f)))
    own = pl.BlockSpec((1, part, hidden_units), lambda e, f: (e, 0, 0))
    if forward:
        kernel, name = experts_forward_kernel, "experts_forward"
        into = pl.BlockSpec((1, width, tile), lambda e, f: (e, 0, first(f)))
        back = pl.BlockSpec((1, hidden_units, wide_tile), lambda e, f: (e, 0, later(f)))
        narrow_outs, own_outs, scratch = 1, 2, [pltpu.VMEM((part, 1), jnp.float32)]
    else:
        kernel, name = experts_backward_kernel, "experts_backward"
        into = pl.BlockSpec((1, wide_tile, hidden_units), lambda e, f: (e, later(f), 0))
        back = pl.BlockSpec((1, tile, width), lambda e, f: (e, first(f), 0))
        narrow_outs, own_outs, scratch = 2, 0, []
    held = () if held is None else tuple(held)
    before = 2 + pieces + 3 + len(slopes)
    scale = 0 if light else 1
    flops = 2 * experts * part * width * (3 * hidden_units + 2 * rows)
    return pl.pallas_call(
        partial(
            kernel, count=count, pieces=pieces, slots=slots, aliased=len(held), tiles=tiles
        ),
        grid=(experts, tiles + wide_tiles),
        in_specs=[info, info]
        + [block] * pieces
        + [into, into, back]
        + [slope] * len(slopes)
        + [pl.BlockSpec(memory_space=pl.ANY)] * len(held),
        out_specs=[wide] + [narrow] * narrow_outs + [own] * own_outs + [block] * pieces,
        out_shape=[jax.ShapeDtypeStruct((experts, all_slots, width), jnp.bfloat16)]
        + [jax.ShapeDtypeStruct((experts, all_slots, hidden_units), jnp.bfloat16)] * narrow_outs
        + [jax.ShapeDtypeStruct((experts, part, hidden_units), jnp.bfloat16)] * own_outs
        + [jax.ShapeDtypeStruct(blocks[0].shape, jnp.bfloat16)] * pieces,
        scratch_shapes=[pltpu.VMEM((experts, part, width), jnp.bfloat16)] + scratch,
        input_output_aliases={before + k: k for k in range(len(held))},
        compiler_params=pltpu.CompilerParams(vmem_limit_bytes=VMEM_BYTES),
        cost_estimate=pl.CostEstimate(
            flops=scale * flops,
            bytes_accessed=scale
            * 2
            * (3 * experts * width * hidden_units + 4 * count * rows * width),
            transcendentals=scale * experts * part * hidden_units,
        ),
        name=name,
    )(ranks, gates, *blocks, *weights, *slopes, *held)


def ring_of(contexts):
    order = list(range(0, contexts, 2)) + list(range(contexts - 1, 0, -2))
    place_of = [order.index(c) for c in range(contexts)]
    up = [(order[p], order[(p + 1) % contexts]) for p in range(contexts)]
    down = [(b, a) for a, b in up]
    return order, place_of, up, down


class RingGather:
    def __init__(self, own, ring):
        _, _, self.up, self.down = ring
        self.half = len(self.up) // 2
        self.step = 0
        self.blocks = {0: own}
        self.from_before = self.from_after = own

    def advance(self, *earlier):
        self.step += 1
        before, past = self.from_before, self.from_after
        if earlier:
            before, past = lax.optimization_barrier((before, past) + earlier)[:2]
        if self.step < self.half:
            self.from_before = lax.ppermute(before, "ctx", self.up)
            self.from_after = lax.ppermute(past, "ctx", self.down)
            self.blocks[-self.step] = self.from_before
            self.blocks[self.step] = self.from_after
            return (-self.step, self.step)
        cut = before.shape[0] // 2
        first = lax.ppermute(before[:cut], "ctx", self.up)
        second = lax.ppermute(past[cut:], "ctx", self.down)
        self.blocks[self.half] = (first, second)
        return (self.half,)


def add_low(left, right):
    return (left.astype(jnp.float32) + right.astype(jnp.float32)).astype(jnp.bfloat16)


class RingScatter:
    def __init__(self, ring):
        _, _, self.up, self.down = ring
        self.half = len(self.up) // 2
        self.step = self.half

    def prepare(self, terms, *earlier):
        if self.step == self.half:
            before, past = terms[self.half]
            if earlier:
                before, past = lax.optimization_barrier((before, past) + earlier)[:2]
        else:
            before, past = terms[-self.step], terms[self.step]
            got_before, got_past = self.to_before, self.to_after
            if earlier:
                before, past = lax.optimization_barrier((before, past) + earlier)[:2]
            cut = got_before.shape[0]
            if cut < before.shape[0]:
                before = jnp.concatenate([add_low(got_before, before[:cut]), before[cut:]], axis=0)
                past = jnp.concatenate([past[:cut], add_low(got_past, past[cut:])], axis=0)
            else:
                before, past = add_low(got_before, before), add_low(got_past, past)
        self.payload = (before, past)
        return self.payload

    def send(self, *earlier):
        before, past = self.payload
        if earlier:
            before, past = lax.optimization_barrier((before, past) + earlier)[:2]
        self.to_before = lax.ppermute(before, "ctx", self.down)
        self.to_after = lax.ppermute(past, "ctx", self.up)
        self.step -= 1
        return self.payload

    def advance(self, terms, *earlier):
        self.prepare(terms, *earlier)
        return self.send()

    def finish(self, own):
        return (
            own.astype(jnp.float32)
            + self.to_before.astype(jnp.float32)
            + self.to_after.astype(jnp.float32)
        )


def sum_over_ctx(values, contexts):
    bit = 1
    while bit < contexts:
        values = values + lax.ppermute(values, "ctx", [(c, c ^ bit) for c in range(contexts)])
        bit *= 2
    return values


def after(value, *earlier):
    return lax.optimization_barrier((value,) + earlier)[0]


def shards_by_heads(
    tokens,
    cotangent,
    cont_lengths,
    routes,
    gates,
    attn_gain,
    query_gain,
    key_gain,
    ffn_gain,
    w_query,
    w_key,
    w_value,
    w_out,
    w_gate,
    w_up,
    w_down,
):
    both = ("ctx", "fsdp")
    contexts, splits = lax.axis_size("ctx"), lax.axis_size("fsdp")
    rows, width = tokens.shape[1:]
    route_count = routes.shape[2]
    total = rows * contexts
    prompt_rows = total // 2
    columns = width // contexts
    size = min(512, prompt_rows)
    local_experts = w_gate.shape[0]
    expert_total = local_experts * contexts
    slots = max(2, rows * route_count * 5 // (4 * expert_total))
    all_slots = contexts * slots
    score_scale = HEAD ** (-0.5)
    me = lax.axis_index("ctx")
    ring = ring_of(contexts)
    half = contexts // 2
    place = jnp.where(me % 2 == 0, me // 2, contexts - 1 - me // 2)

    def owner(offset):
        at = (place + offset) % contexts
        return jnp.where(at < half, 2 * at, 2 * (contexts - 1 - at) + 1)

    others = [k for step in range(1, half) for k in (-step, step)] + [half]

    own_rows = w_out.shape[0]
    token_ring = RingGather(jnp.concatenate([tokens[0], w_out], axis=0), ring)

    chosen = routes[0].T[None] == jnp.arange(expert_total, dtype=jnp.int32)[:, None, None]
    member = jnp.any(chosen, axis=1)
    gate_rows = jnp.sum(jnp.where(chosen, gates[0].T[None], 0.0), axis=1)
    earlier = jnp.tril(jnp.ones((rows, rows), jnp.bfloat16), -1)
    rank = jnp.einsum(
        "et,ut->eu", member.astype(jnp.bfloat16), earlier, preferred_element_type=jnp.float32
    )
    rank = jnp.where(member, rank, -1.0)
    rank_high = jnp.floor(rank / 16.0)
    gate_high = gate_rows.astype(jnp.bfloat16).astype(jnp.float32)
    routing = jnp.stack([rank_high, rank - 16.0 * rank_high, gate_high, gate_rows - gate_high])
    routing = routing.astype(jnp.bfloat16).reshape(4, contexts, local_experts * rows)
    routing = jnp.transpose(routing, (1, 0, 2)).reshape(contexts, own_rows, -1)
    routing_columns = routing.shape[2]

    cut = jnp.stack([w_query, w_key, w_value]).reshape(3, own_rows, contexts, columns)
    cut = jnp.transpose(cut, (2, 1, 0, 3)).reshape(contexts, own_rows, 3 * columns)
    own_gains = jnp.stack([attn_gain, query_gain, key_gain, ffn_gain], axis=1)
    cut = jnp.concatenate(
        [cut, jnp.broadcast_to(own_gains, (contexts,) + own_gains.shape), routing], axis=2
    )
    spare = -cut.shape[2] % 128
    cut = jnp.pad(cut, ((0, 0), (0, 0), (0, spare)))
    pieces = []
    for step in range(contexts):
        piece = lax.dynamic_index_in_dim(cut, (me - step) % contexts, 0, keepdims=False)
        if step:
            pairs = [(c, (c - step) % contexts) for c in range(contexts)]
            piece = lax.ppermute(piece, "ctx", pairs)
        pieces.append(piece)
    first_piece = pieces[1]
    pieces = gather_pieces(me, pieces)
    token_ring.advance(first_piece)
    gate_all = lax.all_gather(after(w_gate, pieces), "fsdp", axis=1, tiled=True)
    w_all = lax.all_gather(pieces, "fsdp", axis=1, tiled=True).reshape(width, -1)
    up_all = lax.all_gather(w_up, "fsdp", axis=1, tiled=True)
    for _ in range(2, half):
        token_ring.advance()
    w_t = w_all[:, : 3 * columns].T
    all_gains = w_all[:, 3 * columns : 3 * columns + 4].astype(jnp.float32).T
    gain_attn, gain_ffn = all_gains[0], all_gains[3]
    gain_query = lax.dynamic_slice_in_dim(all_gains[1], me * columns, columns)[:, None]
    gain_key = lax.dynamic_slice_in_dim(all_gains[2], me * columns, columns)[:, None]

    owners = owner(jnp.arange(contexts, dtype=jnp.int32))
    routing = pieces[:, :, 3 * columns + 4 : 3 * columns + 4 + routing_columns]
    routing = routing.reshape(contexts, 4, local_experts, 1, rows)[owners].astype(jnp.float32)
    all_ranks = (16.0 * routing[:, 0] + routing[:, 1]).astype(jnp.int32)
    all_gates = routing[:, 2] + routing[:, 3]

    lengths_in = cont_lengths[0]
    token_index = jnp.arange(total, dtype=jnp.int32)
    _, position = places(token_index, lengths_in, prompt_rows)
    starts = prompt_rows + jnp.cumsum(lengths_in) - lengths_in
    frequency = ROPE_BASE ** (-jnp.arange(HEAD // 2).astype(jnp.float32) / (HEAD // 2))
    angles = frequency[:, None] * position.astype(jnp.float32)[None, :]
    cosine, sine = jnp.cos(angles), jnp.sin(angles)

    def project_all(offsets, made):
        blocks = [token_ring.blocks[offset] for offset in offsets]
        places_of = owner(jnp.asarray(offsets, jnp.int32))
        return project(places_of, blocks, rows, w_t, gain_attn[None], made, total)

    made = project_all([0] + others[: 2 * (half - 2)], None)
    token_ring.advance(made[-1], up_all, gate_all)
    made = project_all(others[2 * (half - 2) : -1], made)
    far_tokens = jnp.concatenate(token_ring.blocks[half], axis=0)
    token_ring.blocks[half] = after(far_tokens, made[-1])
    made = project_all(others[-1:], made)
    hidden_all, query_pre, key_pre, value_t, squares = made
    w_out_rows = place_rows(
        after(owners, made[-1]), [token_ring.blocks[k if k <= half else k - contexts] for k in range(contexts)], rows, own_rows
    )
    out_all = lax.all_gather(w_out_rows, "fsdp", axis=1, tiled=True).reshape(width, width)
    down_all = lax.all_gather(w_down, "fsdp", axis=1, tiled=True)

    squares = sum_over_ctx(squares, contexts)
    inverse = lax.rsqrt(squares / width + EPSILON)
    query_inv, key_inv = inverse[0:1], inverse[1:2]
    grad_ring = RingGather(cotangent[0], ring)
    grad_ring.advance(squares)

    attended, query, key, key_t, log_rows = attend_forward(
        starts, query_pre, key_pre, value_t, query_inv, key_inv, gain_query, gain_key, cosine, sine, size, prompt_rows, score_scale
    )
    sent = after(attended, grad_ring.from_before, grad_ring.from_after)
    back = lax.all_to_all(
        sent.reshape(contexts, rows, columns), "ctx", split_axis=0, concat_axis=0, tiled=True
    )
    grad_ring.advance(attended)
    own_attended = jnp.transpose(back, (1, 0, 2)).reshape(rows, width)
    inputs = tokens[0].astype(jnp.float32)
    mixed = inputs + jnp.dot(own_attended, out_all, preferred_element_type=jnp.float32)
    mixed_inv = lax.rsqrt(jnp.mean(mixed * mixed, axis=-1, keepdims=True) + EPSILON)
    second = (mixed * mixed_inv * gain_ffn).astype(jnp.bfloat16)

    second_ring = RingGather(second, ring)
    weights = (gate_all, up_all, down_all)

    def stage_info(offsets):
        ranks = jnp.stack([all_ranks[k] for k in offsets])
        stage_gates = jnp.stack([all_gates[k] for k in offsets])
        if len(offsets) == 2:
            return ranks, stage_gates, offsets[1] - 1
        return ranks, stage_gates, contexts - (2 if offsets[0] == 0 else 1)

    stages = [(0,)] + [(-step, step) for step in range(1, half)] + [(half,)]
    infos = [stage_info(stage) for stage in stages]
    result_terms, second_terms, slopes = {}, {}, {}
    kept = kept_grads = None

    def blocks_of(ring_of_blocks, step):
        if step == half:
            return list(ring_of_blocks.blocks[half])
        return [ring_of_blocks.blocks[k] for k in stages[step]]

    def terms_of(step, terms):
        return {half: tuple(terms)} if step == half else dict(zip(stages[step], terms))

    def forward(step, *earlier):
        nonlocal kept
        ranks, stage_gates, at = infos[step]
        ranks = after(ranks, *earlier) if earlier else ranks
        blocks = blocks_of(second_ring, step)
        made = experts_stage(
            True, ranks, stage_gates, blocks, weights, (), kept, at, slots, all_slots
        )
        kept, slopes[step], terms = made[:2], made[2:4], made[4:]
        result_terms.update(terms_of(step, terms))
        return terms[0]

    def backward(step, *earlier, light=False):
        nonlocal kept_grads
        ranks, stage_gates, at = infos[step]
        ranks = after(ranks, *earlier) if earlier else ranks
        blocks = blocks_of(grad_ring, step)
        made = experts_stage(
            False,
            ranks,
            stage_gates,
            blocks,
            weights,
            slopes[step],
            kept_grads,
            at,
            slots,
            all_slots,
            light,
        )
        kept_grads, terms = made[:3], made[3:]
        second_terms.update(terms_of(step, terms))
        return terms[0]

    def weight_grad(left, right):
        return jnp.einsum("emd,emf->edf", left, right, preferred_element_type=jnp.float32).astype(
            jnp.bfloat16
        )

    second_ring.advance()
    grad_second = (grad_ring.from_before, grad_ring.from_after)
    done = forward(0)
    done = backward(0, done, *grad_second, light=True)
    for step in range(1, half):
        near = [second_ring.blocks[k] for k in stages[step]]
        second_ring.advance(done)
        waits = (done,)
        if step > 1:
            waits += (grad_ring.from_before, grad_ring.from_after)
        if step in (1, half - 1):
            grad_ring.advance(done, *near)
        done = forward(step, *waits)
        if step < half - 2:
            done = backward(step, done, light=True)
    done = forward(half, done)

    second_sum, result_sum = RingScatter(ring), RingScatter(ring)
    result_sum.advance(result_terms)
    backward(half, done)
    sent = second_sum.advance(second_terms, result_sum.to_before, result_sum.to_after)
    backward(half - 1, *sent)
    sent = second_sum.advance(second_terms)
    backward(half - 2, *sent)
    sent = second_sum.advance(second_terms)
    rows_taken, active = kept
    route_grad, gate_grad, up_grad = kept_grads
    gate_product = weight_grad(after(rows_taken, *sent), gate_grad)
    sent = second_sum.advance(second_terms, gate_product)
    result_sum.prepare(result_terms, *sent)
    up_product = weight_grad(after(rows_taken, *result_sum.payload), up_grad)
    mixed_grad, branch, ffn_gain_grad = mixed_grad_of(
        second_terms[0],
        second_sum.to_before,
        second_sum.to_after,
        mixed,
        cotangent[0],
        after(gain_ffn[None], up_product),
    )
    ffn_gain_grad = ffn_gain_grad[0]

    def fsdp_sum_low(product):
        return lax.psum_scatter(product, "fsdp", scatter_dimension=1, tiled=True)


    out_grad = out_grad_of(branch, out_all, contexts)
    w_out_grad = lax.dot_general(
        own_attended, after(branch, out_grad), (((0,), (0,)), ((), ())), preferred_element_type=jnp.float32
    ).astype(jnp.bfloat16)
    out_grad = lax.all_to_all(out_grad, "ctx", split_axis=0, concat_axis=0, tiled=True)
    out_grad = out_grad.reshape(total, columns)
    w_out_grad = fsdp_sum_low(
        after(w_out_grad, out_grad).reshape(contexts, splits * own_rows, width)
    )
    gate_w_grad = fsdp_sum_low(after(gate_product, out_grad))
    up_w_grad = fsdp_sum_low(after(up_product, out_grad))

    log_rows = log_rows.reshape(columns // HEAD, 1, total)
    held, dots, waits = None, 0.0, (out_grad,)
    for head in range(columns // HEAD):
        if head == 1:
            result_sum.prepare(result_terms, dots)
            waits = result_sum.payload
        if head < 2:
            result_sum.send(out_grad)
        *held, part = attend_backward(
            after(starts, *waits), head, held, query, key, key_t, value_t, out_grad, attended, log_rows, query_pre, key_pre, query_inv, key_inv, gain_query, gain_key, cosine, sine, size, prompt_rows, score_scale
        )
        dots = dots + part
    query_scaled, key_scaled, value_grad, query_gain_grad, key_gain_grad = held
    dots = after(dots, result_sum.to_before, result_sum.to_after)
    result_sum.prepare(result_terms, dots)
    dots = sum_over_ctx(dots, contexts) / width
    dots = after(dots, *result_sum.payload)
    heads_grad = heads_grad_of(
        query_scaled, key_scaled, value_grad, query_pre, key_pre, inverse, dots
    )

    def own_columns(grad):
        return lax.dynamic_update_slice_in_dim(
            jnp.zeros((width, 1), jnp.float32), grad, me * columns, 0
        )

    other_grads = jnp.concatenate(
        [
            ffn_gain_grad[:, None],
            own_columns(query_gain_grad),
            own_columns(key_gain_grad),
            jnp.zeros((width, 125), jnp.float32),
        ],
        axis=1,
    )
    def term(offset, *earlier, **got):
        at = after(owner(offset)[None], *earlier)
        return hidden_term(at, heads_grad, w_t, w_out_grad, rows, **got)

    result_sum.send(dots)
    hidden_sum = RingScatter(ring)
    hidden_sum.payload = far = term(half)
    hidden_sum.send()
    heads_product = heads_product_of(
        heads_grad, hidden_all, after(other_grads, *far), contexts
    )
    heads_w_grad = fsdp_sum_low(after(heads_product, hidden_sum.to_before, hidden_sum.to_after))
    done = (result_sum.to_before, result_sum.to_after)
    for step in range(half - 1, 0, -1):
        start = far[0].shape[0] if step == half - 1 else 0
        if step == half - 2:
            done = (heads_product, down_product, gate_w_grad)
        if step == 1:
            done = (up_w_grad,)
        hidden_sum.payload = sent = (
            term(-step, *done, got=hidden_sum.to_before),
            term(step, *done, got=hidden_sum.to_after, start=start),
        )
        hidden_sum.send()
        if step == half - 1:
            down_product = weight_grad(after(active, *sent), route_grad)
            down_w_grad = fsdp_sum_low(
                after(down_product, hidden_sum.to_before, hidden_sum.to_after)
            )
            heads_w_grad = lax.all_to_all(
                heads_w_grad, "ctx", split_axis=0, concat_axis=0, tiled=True
            )
        done = ()
    input_grad = input_grad_of(
        after(owner(0)[None], heads_w_grad),
        heads_grad,
        w_t,
        hidden_sum.to_before,
        hidden_sum.to_after,
        tokens[0],
        gain_attn[None],
        mixed_grad,
    )
    w_out_grad = (
        lax.dynamic_index_in_dim(w_out_grad, me, 0, keepdims=False).astype(jnp.float32)
        + hidden_sum.to_before[rows:].astype(jnp.float32)
        + hidden_sum.to_after[rows:].astype(jnp.float32)
    )
    routed = result_sum.finish(result_terms[0])
    output = (mixed + routed)[None]

    heads_w_grad = heads_w_grad.astype(jnp.float32)
    other_grads = jnp.sum(heads_w_grad[:, :, 3 * columns : 3 * columns + 3], axis=0)
    heads_w_grad = jnp.transpose(
        heads_w_grad[:, :, : 3 * columns].reshape(contexts, own_rows, 3, columns), (2, 1, 0, 3)
    ).reshape(3, own_rows, width)

    attn_gain_grad = jnp.sum(
        w_query.astype(jnp.float32) * heads_w_grad[0]
        + w_key.astype(jnp.float32) * heads_w_grad[1]
        + w_value.astype(jnp.float32) * heads_w_grad[2],
        axis=1,
    ) / attn_gain.astype(jnp.float32)

    return (
        output,
        input_grad[None],
        attn_gain_grad,
        other_grads[:, 1],
        other_grads[:, 2],
        other_grads[:, 0],
        heads_w_grad[0],
        heads_w_grad[1],
        heads_w_grad[2],
        w_out_grad,
        gate_w_grad.astype(jnp.float32),
        up_w_grad.astype(jnp.float32),
        down_w_grad.astype(jnp.float32),
    )


def solution(mesh):
    contexts = mesh.shape["ctx"]
    fits = contexts == 8
    placed = (
        P("fsdp", "ctx", None),
        P("fsdp", "ctx", None),
        P("fsdp", None),
        P("fsdp", "ctx", None),
        P("fsdp", "ctx", None),
        P(("ctx", "fsdp")),
        P(("ctx", "fsdp")),
        P(("ctx", "fsdp")),
        P(("ctx", "fsdp")),
        P(("ctx", "fsdp"), None),
        P(("ctx", "fsdp"), None),
        P(("ctx", "fsdp"), None),
        P(("ctx", "fsdp"), None),
        P("ctx", "fsdp", None),
        P("ctx", "fsdp", None),
        P("ctx", "fsdp", None),
    )
    return jax.shard_map(
        shards_by_heads if fits else shards_wide,
        mesh=mesh,
        in_specs=placed,
        out_specs=(
            P("fsdp", "ctx", None),
            P("fsdp", "ctx", None),
            P(("ctx", "fsdp")),
            P(("ctx", "fsdp")),
            P(("ctx", "fsdp")),
            P(("ctx", "fsdp")),
            P(("ctx", "fsdp"), None),
            P(("ctx", "fsdp"), None),
            P(("ctx", "fsdp"), None),
            P(("ctx", "fsdp"), None),
            P("ctx", "fsdp", None),
            P("ctx", "fsdp", None),
            P("ctx", "fsdp", None),
        ),
        check_vma=False,
    )
```
